128 devices in a mesh: seq: 16 (over x, y), exp: 8 (over z, core).
Axes of the slice: x: 4, y: 4, z: 4, core: 2. Of those that a mesh axis runs over, the one named last changes fastest.
Arguments:
- x_in: bfloat16 [4096, 8192], P('seq', 'exp'), may hold values from -6 to 6
- z_in: bfloat16 [4096, 8192], P('seq', 'exp'), may hold values from -6 to 6
- conv_weight: float32 [4, 8192], P(None, 'exp'), may hold values from -3 to 3
- conv_bias: float32 [8192], P('exp'), may hold values from -0.5 to 0.5
- x_proj: bfloat16 [8192, 288], P('exp'), may hold values from -0.0625 to 0.0625
- dt_proj: bfloat16 [256, 8192], P(None, 'exp'), may hold values from -0.375 to 0.375
- dt_bias: float32 [8192], P('exp'), may hold values from -3 to -1.5
- a_log: float32 [8192, 16], P('exp'), may hold values from -8.5 to -1.2
- d_skip: float32 [8192], P('exp'), may hold values from 0.5 to 1.5
- out_proj: bfloat16 [8192, 4096], P('exp', 'seq'), may hold values from -0.0625 to 0.0625
- residual: bfloat16 [4096, 4096], P(('seq', 'exp')), may hold values from -3 to 3
- expert_ids: int32 [4096, 2], P(('seq', 'exp')), may hold values from 0 to 15, all different within a row; in each aligned block of 32 rows (0 to 31, 32 to 63, ...) at most 8 rows name the same one
- gate_weights: float32 [4096, 2], P(('seq', 'exp')), may hold values from 0.1 to 1
- w_gate: bfloat16 [8, 4096, 12288], P('exp', None, 'seq'), may hold values from -0.09375 to 0.09375
- w_up: bfloat16 [8, 4096, 12288], P('exp', None, 'seq'), may hold values from -0.09375 to 0.09375
- w_down: bfloat16 [8, 12288, 4096], P('exp', 'seq'), may hold values from -0.0546875 to 0.0546875
Outputs:
- layer_out: float32 [4096, 4096], P(('seq', 'exp'))
The draws below stay inside these ranges and needn't reach their ends.
Inputs may be any that keep to these rules, and one draw needn't show every extreme that they name: `expert_ids`: each token names 2 different experts; among the 32 tokens of one device no expert is named by more than 8 tokens.
All inputs are finite; a program needn't handle non-finite values.
Results may differ from the reference program's by a relative error of at most 0.0043.
Values may be sent and summed in bfloat16 or wider, within the bound.
No kernel may reach another device: no remote copies, remote signals or barrier semaphores. Data moves between devices by JAX's collectives and lax.ppermute only.
A program may use at most 128 MiB of HBM per device.

```python
import math
import jax
import jax.numpy as jnp
import numpy as np
from jax import lax

D = 4096
INNER = 8192
RANK = 256
STATE = 16
CONV = 4
FF = 12288
EXPERTS = 16
TOP = 2
TOKENS = 4096
TOK_DEV = 32
CAP = 8
WIN_EXP = 8
ROWS_ALL = 1024
N_SEQ = 16


def shard_levels(key, extent, cuts, least, top_value):
    def one(dim, shards_of):
        draws = jax.random.uniform(jax.random.fold_in(jax.random.fold_in(key, 6), dim), (shards_of,), jnp.float32, least / len(cuts), top_value / len(cuts))
        return jnp.repeat(jnp.exp(draws), extent[dim] // shards_of).reshape((-1,) + (1,) * (len(extent) - dim - 1))

    factor_of = one(*cuts[0])
    for cut in cuts[1:]:
        factor_of = factor_of * one(*cut)
    return factor_of


def assign_block(key, own, number, rows, number_of, top, limit, slope):
    order = jax.random.permutation(key, number_of)
    packed, ordinary = load_shares(number_of, rows * top, limit, slope, True), load_shares(number_of, rows * top, limit, slope, False)
    places = jnp.arange(number_of)

    def named(sizes, rotation):
        used = int((sizes > 0).sum())
        fixed = max(1, used // 4)
        moved = fixed + (places - fixed + rotation * (used - fixed)) % max(1, number_of - fixed)
        return jnp.zeros((number_of,), jnp.int32).at[order[jnp.where(places < fixed, places, moved)]].set(jnp.asarray(sizes, jnp.int32))

    sizes = jnp.where(number % 4 == 0, named(packed, number // 4), named(ordinary, number - number // 4 - 1))
    mixed = jax.random.permutation(jax.random.fold_in(own, 3), number_of)
    giver, taker = mixed[0:number_of // 2 * 2:2], mixed[1:number_of // 2 * 2:2]
    room = jnp.minimum(sizes[giver] - 1, limit - sizes[taker]) // 2
    room = jnp.where((giver == order[0]) | (taker == order[0]) | (sizes[taker] == 0), 0, jnp.maximum(room, 0))
    moved = jax.random.randint(jax.random.fold_in(own, 4), (number_of // 2,), 0, 1 << 20) % (room + 1)
    sizes = sizes.at[giver].add(-moved).at[taker].add(moved)
    members = jnp.searchsorted(jnp.cumsum(sizes), jnp.arange(rows * top), side="right").astype(jnp.int32)
    listing = members.reshape(top, rows).T
    listing = listing[jax.random.permutation(jax.random.fold_in(own, 1), rows)]
    rotation = jax.random.randint(jax.random.fold_in(own, 2), (rows, 1), 0, top)
    return jnp.take_along_axis(listing, (jnp.arange(top)[None, :] + rotation) % top, axis=1)


def load_shares(number_of, total, bound, lean, full):
    portions = [(1 << 20) // math.isqrt(standing ** lean) + 1 for standing in range(1, number_of + 1)]
    largest = bound if full else min(bound, max(-(-total // number_of), total * portions[0] // sum(portions)))
    least = 1 if total - largest >= number_of - 1 else 0
    holding, rest = [largest] + [least] * (number_of - 1), total - largest - least * (number_of - 1)
    while rest > 0:
        candidates = [i for i in range(1, number_of) if holding[i] < largest] or [i for i in range(1, number_of) if holding[i] < bound]
        mass, left = sum([portions[i] for i in candidates]), rest
        for i in candidates:
            more = min(bound - holding[i], max(1, left * portions[i] // mass), rest)
            holding[i] = holding[i] + more
            rest = rest - more
    return np.array(holding)


def centred(own_key, shape, deviation, reach, pieces=(), kind=jnp.bfloat16):
    values = jax.random.normal(own_key, shape, jnp.float32) * deviation
    if len(pieces) > 0:
        values = shard_levels(own_key, shape, pieces, -0.22, 0.18) * values
    return jnp.clip(values, min=-reach, max=reach).astype(kind)


def setup_inputs(seed: int = 0) -> dict:
    streams_of = jax.random.split(jax.random.key(seed), 17)
    x_in = centred(streams_of[0], (TOKENS, INNER), 1.0, 6.0, ((0, 16), (1, 8)))
    z_in = centred(streams_of[1], (TOKENS, INNER), 1.0, 6.0, ((0, 16), (1, 8)))
    conv_weight = centred(streams_of[2], (CONV, INNER), CONV ** -0.5, 3.0, ((1, 8),), jnp.float32)
    conv_bias = jnp.clip(jax.random.uniform(streams_of[3], (INNER,), jnp.float32, -0.5, 0.5) * shard_levels(streams_of[3], (INNER,), ((0, 8),), -0.4, 0.0), -0.5, 0.5)
    x_proj = centred(streams_of[4], (INNER, RANK + 2 * STATE), INNER ** -0.5, 0.0625, ((0, 8),))
    dt_proj = centred(streams_of[5], (RANK, INNER), RANK ** -0.5, 0.375, ((1, 8),))
    dt_bias = jnp.clip(-3.0 + 1.5 * jax.random.uniform(streams_of[6], (INNER,), jnp.float32) ** shard_levels(streams_of[6], (INNER,), ((0, 8),), -0.2, 0.2), -3.0, -1.5)
    a_log = jnp.clip(-8.5 + 7.3 * jax.random.uniform(streams_of[7], (INNER, STATE), jnp.float32) ** shard_levels(streams_of[7], (INNER, STATE), ((0, 8),), -0.2, 0.2), -8.5, -1.2)
    d_skip = jnp.clip(0.5 + 1.0 * jax.random.uniform(streams_of[8], (INNER,), jnp.float32) ** shard_levels(streams_of[8], (INNER,), ((0, 8),), -0.2, 0.2), 0.5, 1.5)
    out_proj = centred(streams_of[9], (INNER, D), INNER ** -0.5, 0.0625, ((0, 8), (1, 16)))
    residual = centred(streams_of[10], (TOKENS, D), 0.5, 3.0, ((0, 128),))
    expert_ids_keys = jax.random.split(jax.random.fold_in(streams_of[11], 1), TOKENS // TOK_DEV)
    expert_ids_turns = jax.random.permutation(jax.random.fold_in(streams_of[11], 3), TOKENS // TOK_DEV)
    expert_ids = jax.vmap(lambda own, number: assign_block(jax.random.fold_in(streams_of[11], 2), own, number, TOK_DEV, EXPERTS, TOP, CAP, 2))(expert_ids_keys, expert_ids_turns).reshape((TOKENS, TOP))
    gate_weights = jnp.clip(0.1 + 0.9 * jax.random.uniform(streams_of[12], (TOKENS, TOP), jnp.float32) ** shard_levels(streams_of[12], (TOKENS, TOP), ((0, 128),), -0.2, 0.2), 0.1, 1.0)
    w_gate = centred(streams_of[13], (WIN_EXP, D, FF), D ** -0.5, 0.09375, ((0, 8), (2, 16)))
    w_up = centred(streams_of[14], (WIN_EXP, D, FF), D ** -0.5, 0.09375, ((0, 8), (2, 16)))
    w_down = centred(streams_of[15], (WIN_EXP, FF, D), FF ** -0.5, 0.0546875, ((0, 8), (1, 16)))
    return {"x_in": x_in, "z_in": z_in, "conv_weight": conv_weight, "conv_bias": conv_bias, "x_proj": x_proj, "dt_proj": dt_proj, "dt_bias": dt_bias, "a_log": a_log, "d_skip": d_skip, "out_proj": out_proj, "residual": residual, "expert_ids": expert_ids, "gate_weights": gate_weights, "w_gate": w_gate, "w_up": w_up, "w_down": w_down}


def rms_scale(hidden):
    return hidden * lax.rsqrt(lax.optimization_barrier(jnp.mean(hidden * hidden, axis=-1, keepdims=True)) + 1e-06)

def reference(x_in, z_in, conv_weight, conv_bias, x_proj, dt_proj, dt_bias, a_log, d_skip, out_proj, residual, expert_ids, gate_weights, w_gate, w_up, w_down):
    inputs = x_in.astype(jnp.float32)
    padded = jnp.concatenate([jnp.zeros((CONV - 1, INNER), jnp.float32), inputs], axis=0)
    conv = jnp.zeros((TOKENS, INNER), jnp.float32) + conv_bias[None, :]
    for offset in range(CONV):
        conv = conv + conv_weight[offset][None, :] * padded[offset:offset + TOKENS]
    mixed_in = jax.nn.silu(conv).astype(jnp.bfloat16)
    projected = jnp.dot(mixed_in, x_proj, preferred_element_type=jnp.float32)
    low_rank = projected[:, :RANK].astype(jnp.bfloat16)
    b_coef = projected[:, RANK:RANK + STATE]
    c_coef = projected[:, RANK + STATE:]
    delta = jax.nn.softplus(jnp.dot(low_rank, dt_proj, preferred_element_type=jnp.float32) + dt_bias[None, :])
    rates = -jnp.exp(a_log)
    signal = mixed_in.astype(jnp.float32)

    def advance(state, item):
        step_delta, step_x, step_b, step_c = item
        state = jnp.exp(step_delta[:, None] * rates) * state + (step_delta * step_x)[:, None] * step_b[None, :]
        return (state, lax.optimization_barrier(jnp.sum(state * step_c[None, :], axis=1)))
    start_state = jnp.zeros((INNER, STATE), jnp.float32)
    _, scanned = lax.scan(advance, start_state, (delta, signal, b_coef, c_coef))
    output = scanned + d_skip[None, :] * signal
    gated = (output * jax.nn.silu(z_in.astype(jnp.float32))).astype(jnp.bfloat16)
    hidden = residual.astype(jnp.float32) + jnp.dot(gated, out_proj, preferred_element_type=jnp.float32)
    normed = rms_scale(hidden).astype(jnp.bfloat16)
    combined = jnp.zeros((TOKENS, D), jnp.float32)
    positions = jnp.arange(TOKENS, dtype=jnp.int32)
    group_width = FF // N_SEQ
    for expert in range(WIN_EXP):
        chosen = expert_ids == expert
        routed = jnp.any(chosen, axis=1)
        weight = lax.optimization_barrier(jnp.sum(jnp.where(chosen, gate_weights, jnp.zeros_like(gate_weights)), axis=1))
        sort_key = jnp.where(routed, 0, 1).astype(jnp.int32) * TOKENS + positions
        order = jnp.argsort(sort_key)[:ROWS_ALL].astype(jnp.int32)
        rows = normed[order]
        gate = jnp.dot(rows, w_gate[expert], preferred_element_type=jnp.float32)
        upper = jnp.dot(rows, w_up[expert], preferred_element_type=jnp.float32)
        inner = (jax.nn.silu(gate) * upper).astype(jnp.bfloat16)
        total = jnp.zeros((ROWS_ALL, D), jnp.float32)
        for group in range(N_SEQ):
            low = group * group_width
            piece = jnp.dot(inner[:, low:low + group_width], w_down[expert, low:low + group_width], preferred_element_type=jnp.float32)
            total = total + lax.optimization_barrier(piece.astype(jnp.bfloat16)).astype(jnp.float32)
        result = lax.optimization_barrier(total.astype(jnp.bfloat16)).astype(jnp.float32)
        combined = combined.at[order].add(weight[order][:, None] * result)
    return hidden + combined
```

```python
import functools
import math

import jax
import jax.numpy as jnp
from jax import lax
from jax.experimental import pallas as pl
from jax.experimental.pallas import tpu as pltpu
from jax.sharding import PartitionSpec as P

RANK = 256
STATE = 16
CONV = 4
SEG = 8
LANES = 128
LOG2E = math.log2(math.e)
F32 = jnp.float32
BF16 = jnp.bfloat16
MIB = 1024 * 1024


def whole():
    return pl.BlockSpec(memory_space=pltpu.VMEM)


def far():
    return pl.BlockSpec(memory_space=pltpu.HBM)


def params(mib):
    return pltpu.CompilerParams(vmem_limit_bytes=mib * MIB)


def lines(stage):
    side = math.isqrt(lax.axis_size("seq"))
    owners = lax.axis_size("exp")
    groups = []
    for owner in range(owners):
        along_x = (owner % 2 == 0) == (stage == 0)
        for fixed in range(side):
            members = [(m * side + fixed if along_x else fixed * side + m) for m in range(side)]
            groups.append([m * owners + owner for m in members])
    return groups


def along(block, stage, distance):
    route = []
    for members in lines(stage):
        count = len(members)
        route += [(members[i], members[(i + distance) % count]) for i in range(count)]
    return lax.ppermute(block, ("seq", "exp"), route)


def passed_along(block, axis, distance):
    devices = range(lax.axis_size(axis))
    route = [(i - distance, i) for i in devices if i - distance in devices]
    return lax.ppermute(block, axis, route)


def conv_kernel(
    x_hbm,
    weight_hbm,
    bias_hbm,
    proj_hbm,
    rim_ref,
    mixed_ref,
    part_ref,
    x_ref,
    weight_ref,
    bias_ref,
    proj_ref,
    padded,
    sems,
):
    sources = (x_hbm, weight_hbm, bias_hbm, proj_hbm)
    targets = (x_ref, weight_ref, bias_ref, proj_ref)
    copies = [pltpu.make_async_copy(*pair, sems.at[k]) for k, pair in enumerate(zip(sources, targets))]
    for copy in copies:
        copy.start()
    length, channels = x_ref.shape
    steps = length // SEG
    head = 8
    for copy in copies[:3]:
        copy.wait()
    for lane in range(0, channels, LANES):
        block = padded.at[lane // LANES]
        block[head - (CONV - 1) : head, :] = rim_ref[:, lane : lane + LANES].astype(F32)
        block[head:, :] = x_ref[:, lane : lane + LANES].astype(F32)

    def step(i, carry):
        rows = pl.ds(pl.multiple_of(i * SEG, SEG), SEG)
        for lane in range(0, channels, LANES):
            lanes = pl.ds(lane, LANES)
            acc = jnp.broadcast_to(bias_ref[:, lanes], (SEG, LANES))
            for tap in range(CONV):
                taken = padded[
                    lane // LANES, pl.ds(i + head - (CONV - 1) + tap, SEG, stride=steps), :
                ]
                acc = acc + weight_ref[tap : tap + 1, lanes] * taken
            mixed_ref[rows, lanes] = (acc * jax.nn.sigmoid(acc)).astype(BF16).astype(F32)
        return carry

    lax.fori_loop(0, steps, step, 0)
    copies[3].wait()
    part_ref[...] = jnp.dot(
        mixed_ref[...].astype(BF16), proj_ref[...], preferred_element_type=F32
    )


def spread(target, packed_ref, first):
    packed = packed_ref[...].astype(F32)
    coef = packed[:, RANK : RANK + 2 * STATE] + packed[:, RANK + 2 * STATE :]
    for n in range(STATE):
        target[n] = jnp.broadcast_to(coef[:, first + n : first + n + 1], (coef.shape[0], LANES))


def scan_kernel(
    packed_ref,
    mixed_ref,
    rates_ref,
    proj_hbm,
    bias_hbm,
    y_ref,
    delta_ref,
    before_hbm,
    enter_hbm,
    msg_hbm,
    b_wide,
    c_wide,
    proj_ref,
    bias_ref,
    before_ref,
    enter_ref,
    msg_ref,
    in_sems,
    out_sems,
):
    length, channels = mixed_ref.shape
    steps = length // SEG
    copies = [
        pltpu.make_async_copy(proj_hbm, proj_ref, in_sems.at[0]),
        pltpu.make_async_copy(bias_hbm, bias_ref, in_sems.at[1]),
    ]
    for copy in copies:
        copy.start()
    spread(b_wide, packed_ref, 0)
    spread(c_wide, packed_ref, STATE)
    for copy in copies:
        copy.wait()
    copies = []
    raw = jnp.dot(packed_ref[:, :RANK], proj_ref[...], preferred_element_type=F32) + bias_ref[...]
    delta_ref[...] = jnp.maximum(raw, 0.0) + jnp.log1p(jnp.exp(-jnp.abs(raw)))
    row = lax.broadcasted_iota(jnp.int32, (SEG, LANES), 0)

    def shifted(value, by, fill):
        return jnp.where(row < by, fill, pltpu.roll(value, by, axis=0))

    for lane in range(0, channels, LANES):
        lanes = pl.ds(lane, LANES)
        rates = [
            jnp.broadcast_to(rates_ref[n : n + 1, lanes], (SEG, LANES)) for n in range(STATE)
        ]

        def step(i, carry):
            elapsed, states = carry
            rows = pl.ds(pl.multiple_of(i * SEG, SEG), SEG)
            delta = delta_ref[rows, lanes]
            drive = delta * mixed_ref[rows, lanes]
            fresh, terms = [], []
            for n in range(STATE):
                state = jnp.exp2(delta * rates[n]) * states[n] + drive * b_wide[n, rows, :]
                fresh.append(state)
                terms.append(state * c_wide[n, rows, :])
            while len(terms) > 1:
                terms = [a + b for a, b in zip(terms[::2], terms[1::2])]
            y_ref[rows, lanes] = terms[0]
            return elapsed + delta, tuple(fresh)

        zero = jnp.zeros((SEG, LANES), F32)
        elapsed, states = lax.fori_loop(0, steps, step, (zero, (zero,) * STATE), unroll=2)
        total = elapsed
        for by in (1, 2, 4):
            total = total + shifted(total, by, 0.0)
        before_ref[:, lanes] = shifted(total, 1, 0.0)
        last = total[SEG - 1 : SEG, :]
        for n in range(STATE):
            decay = jnp.exp2(elapsed * rates[n])
            state = states[n]
            for by in (1, 2, 4):
                state = decay * shifted(state, by, 0.0) + state
                decay = decay * shifted(decay, by, 1.0)
            enter_ref[n, :, lanes] = shifted(state, 1, 0.0)
            msg_ref[n, 0:1, lanes] = state[SEG - 1 : SEG, :]
            msg_ref[n, 1:2, lanes] = last
        block = lane // LANES
        fresh = [
            pltpu.make_async_copy(
                before_ref.at[:, lanes], before_hbm.at[:, lanes], out_sems.at[0, block]
            ),
            pltpu.make_async_copy(
                enter_ref.at[:, :, lanes], enter_hbm.at[:, :, lanes], out_sems.at[1, block]
            ),
            pltpu.make_async_copy(
                msg_ref.at[:, :, lanes], msg_hbm.at[:, :, lanes], out_sems.at[2, block]
            ),
        ]
        for copy in fresh:
            copy.start()
        copies += fresh
    for copy in copies:
        copy.wait()


def relay_kernel(place_ref, ends_ref, rates_ref, out_ref):
    rate = rates_ref[pl.ds(place_ref[0], 1), :]
    state = jnp.zeros_like(rate)
    for device in range(ends_ref.shape[0]):
        out_ref[device] = state
        state = jnp.exp2(ends_ref[device, 1:2, :] * rate) * state + ends_ref[device, 0:1, :]


def finish_kernel(
    order_ref,
    entering_ref,
    rates_ref,
    delta_ref,
    packed_ref,
    y_ref,
    mixed_ref,
    before_hbm,
    enter_hbm,
    skip_hbm,
    z_hbm,
    gated_ref,
    before_ref,
    enter_ref,
    skip_ref,
    z_ref,
    c_wide,
    z_wide,
    gated,
    sems,
):
    length, channels = mixed_ref.shape
    steps = length // SEG
    sources = (before_hbm, enter_hbm, skip_hbm, z_hbm)
    targets = (before_ref, enter_ref, skip_ref, z_ref)
    copies = [pltpu.make_async_copy(*pair, sems.at[k]) for k, pair in enumerate(zip(sources, targets))]
    for copy in copies:
        copy.start()
    spread(c_wide, packed_ref, STATE)
    for copy in copies:
        copy.wait()
    for lane in range(0, channels, LANES):
        z_wide[lane // LANES] = z_ref[:, lane : lane + LANES].astype(F32)

    for lane in range(0, channels, LANES):
        lanes = pl.ds(lane, LANES)
        rates = [
            jnp.broadcast_to(rates_ref[n : n + 1, lanes], (SEG, LANES)) for n in range(STATE)
        ]
        before = before_ref[:, lanes]
        held = [
            jnp.exp2(before * rates[n]) * entering_ref[n : n + 1, lanes] + enter_ref[n, :, lanes]
            for n in range(STATE)
        ]
        skip = skip_ref[:, lanes]

        def step(i, elapsed):
            rows = pl.ds(pl.multiple_of(i * SEG, SEG), SEG)
            apart = pl.ds(i, SEG, stride=steps)
            elapsed = elapsed + delta_ref[rows, lanes]
            terms = [
                jnp.exp2(elapsed * rates[n]) * held[n] * c_wide[n, rows, :] for n in range(STATE)
            ]
            while len(terms) > 1:
                terms = [a + b for a, b in zip(terms[::2], terms[1::2])]
            output = y_ref[rows, lanes] + terms[0] + skip * mixed_ref[rows, lanes]
            z = z_wide[lane // LANES, apart, :]
            gated[lane // LANES, apart, :] = output * (z * jax.nn.sigmoid(z))
            return elapsed

        lax.fori_loop(0, steps, step, jnp.zeros((SEG, LANES), F32), unroll=2)
    for place in range(SEG):
        rows = pl.ds(pl.multiple_of(order_ref[place] * steps, steps), steps)
        for lane in range(0, channels, LANES):
            gated_ref[place * steps : (place + 1) * steps, lane : lane + LANES] = gated[
                lane // LANES, rows, :
            ].astype(BF16)


def outward_kernel(gated_ref, proj_hbm, send_ref, keep_ref, proj, arrived):
    parts, _, width = proj_hbm.shape
    middle = send_ref.shape[0]
    for part in range(parts):
        pltpu.make_async_copy(proj_hbm.at[part], proj.at[part], arrived.at[part]).start()

    def product(part, carry):
        pltpu.make_async_copy(proj_hbm.at[part], proj.at[part], arrived.at[part]).wait()
        columns = pl.ds(pl.multiple_of(part * width, width), width)
        terms = jnp.dot(gated_ref[...], proj[part], preferred_element_type=F32)
        send_ref[:, columns] = terms[:middle].astype(BF16)
        keep_ref[:, columns] = terms[middle:]
        return carry

    lax.fori_loop(0, parts, product, 0)


def expert_kernel(rows_ref, gate_ref, up_ref, down_ref, out_ref, inner):
    tile = 256

    def widen(part, carry):
        columns = pl.ds(pl.multiple_of(part * tile, tile), tile)
        gate = jnp.dot(rows_ref[...], gate_ref[:, columns], preferred_element_type=F32)
        upper = jnp.dot(rows_ref[...], up_ref[:, columns], preferred_element_type=F32)
        inner[:, columns] = (gate * jax.nn.sigmoid(gate) * upper).astype(BF16)
        return carry

    lax.fori_loop(0, inner.shape[1] // tile, widen, 0)

    def narrow(part, carry):
        columns = pl.ds(pl.multiple_of(part * tile, tile), tile)
        piece = jnp.dot(inner[...], down_ref[:, columns], preferred_element_type=F32)
        out_ref[:, columns] = piece.astype(BF16)
        return carry

    lax.fori_loop(0, out_ref.shape[1] // tile, narrow, 0)


def expert(rows, gate, up, down):
    count, features = rows.shape
    hidden = gate.shape[1]
    return pl.pallas_call(
        expert_kernel,
        out_shape=jax.ShapeDtypeStruct((count, features), BF16),
        in_specs=[whole()] * 4,
        out_specs=whole(),
        scratch_shapes=[pltpu.VMEM((count, hidden), BF16)],
        compiler_params=params(12),
        cost_estimate=pl.CostEstimate(
            flops=6 * count * features * hidden,
            bytes_accessed=4 * count * features,
            transcendentals=count * hidden,
        ),
        name="expert",
    )(rows, gate, up, down)


def halves(block):
    middle = block.shape[0] // 2
    return block[:middle], block[middle:]


def added(*blocks):
    total = blocks[0].astype(F32)
    for block in blocks[1:]:
        total = total + block.astype(F32)
    return total.astype(BF16)


def experts_on_grid(rows, gate, up, down):
    run = functools.partial(expert, gate=gate, up=up, down=down)
    behind = along(rows, 0, 1)
    ahead = along(rows, 0, -1)
    across = along(rows, 0, 2)
    own = jnp.concatenate([rows, behind, ahead, across], axis=0)
    behind = along(own, 1, 1)
    ahead = along(own, 1, -1)
    own_out = run(own)
    behind, ahead, own_out = lax.optimization_barrier((behind, ahead, own_out))
    far_first = along(halves(behind)[0], 1, 1)
    far_second = along(halves(ahead)[1], 1, -1)
    behind_out = run(behind)
    far_first, far_second, behind_out = lax.optimization_barrier((far_first, far_second, behind_out))
    far_out = run(jnp.concatenate([far_first, far_second], axis=0))
    first, second = halves(far_out)
    from_behind = along(first, 1, 1)
    from_ahead = along(second, 1, -1)
    ahead_out = run(ahead)
    from_behind, from_ahead, ahead_out = lax.optimization_barrier(
        (from_behind, from_ahead, ahead_out)
    )
    ahead_first, ahead_second = halves(ahead_out)
    behind_first, behind_second = halves(behind_out)
    ahead_sum = jnp.concatenate([added(ahead_first, from_behind), ahead_second], axis=0)
    behind_sum = jnp.concatenate([behind_first, added(behind_second, from_ahead)], axis=0)
    ahead_sum, behind_sum = lax.optimization_barrier((ahead_sum, behind_sum))
    from_behind = along(ahead_sum, 1, 1)
    from_ahead = along(behind_sum, 1, -1)
    total = added(own_out, from_behind, from_ahead)
    kept, behind, ahead, across = jnp.split(total, 4, axis=0)
    return added(kept, along(behind, 0, -1), along(ahead, 0, 1), along(across, 0, 2))


def mixer(x_in, z_in, conv_weight, conv_bias, x_proj, dt_proj, dt_bias, a_log, d_skip, out_proj):
    length, channels = x_in.shape
    steps = length // SEG
    owners = lax.axis_size("exp")
    seqs = lax.axis_size("seq")
    columns = lax.all_gather(out_proj, "seq", axis=0)
    rates = (-jnp.exp(a_log) * LOG2E).T
    rim = passed_along(x_in[length - (CONV - 1) :], "seq", 1)
    mixed, partial = pl.pallas_call(
        conv_kernel,
        out_shape=(
            jax.ShapeDtypeStruct((length, channels), F32),
            jax.ShapeDtypeStruct((length, RANK + 2 * STATE), F32),
        ),
        in_specs=[far()] * 4 + [whole()],
        out_specs=[whole()] * 2,
        scratch_shapes=[
            pltpu.VMEM(x_in.shape, BF16),
            pltpu.VMEM(conv_weight.shape, F32),
            pltpu.VMEM((1, channels), F32),
            pltpu.VMEM(x_proj.shape, BF16),
            pltpu.VMEM((channels // LANES, length + 8, LANES), F32),
            pltpu.SemaphoreType.DMA((4,)),
        ],
        compiler_params=params(12),
        name="conv",
    )(x_in, conv_weight, conv_bias[None, :], x_proj, rim)
    share = lax.all_to_all(
        partial.reshape(owners, length // owners, -1), "exp", split_axis=0, concat_axis=0, tiled=True
    )
    summed = jnp.sum(share, axis=0)
    low = summed[:, :RANK].astype(BF16)
    coef = summed[:, RANK:]
    coef_high = coef.astype(BF16)
    coef_low = (coef - coef_high.astype(F32)).astype(BF16)
    packed = jnp.concatenate([low, coef_high, coef_low], axis=1)
    packed = lax.all_to_all(
        jnp.broadcast_to(packed[None], (owners,) + packed.shape),
        "exp",
        split_axis=0,
        concat_axis=0,
        tiled=True,
    ).reshape(length, -1)
    y_local, delta, before, enter, message = pl.pallas_call(
        scan_kernel,
        out_shape=(
            jax.ShapeDtypeStruct((length, channels), F32),
            jax.ShapeDtypeStruct((length, channels), F32),
            jax.ShapeDtypeStruct((SEG, channels), F32),
            jax.ShapeDtypeStruct((STATE, SEG, channels), F32),
            jax.ShapeDtypeStruct((STATE, 2, channels), F32),
        ),
        in_specs=[whole()] * 3 + [far()] * 2,
        out_specs=[whole()] * 2 + [far()] * 3,
        scratch_shapes=[
            pltpu.VMEM((STATE, length, LANES), F32),
            pltpu.VMEM((STATE, length, LANES), F32),
            pltpu.VMEM(dt_proj.shape, BF16),
            pltpu.VMEM((1, channels), F32),
            pltpu.VMEM((SEG, channels), F32),
            pltpu.VMEM((STATE, SEG, channels), F32),
            pltpu.VMEM((STATE, 2, channels), F32),
            pltpu.SemaphoreType.DMA((2,)),
            pltpu.SemaphoreType.DMA((3, channels // LANES)),
        ],
        compiler_params=params(14),
        name="scan",
    )(packed, mixed, rates, dt_proj, dt_bias[None, :])
    ends = lax.all_to_all(message, "seq", split_axis=0, concat_axis=0, tiled=True)
    place = lax.axis_index("seq").astype(jnp.int32).reshape(1)
    entering = pl.pallas_call(
        relay_kernel,
        out_shape=jax.ShapeDtypeStruct((seqs, 1, channels), F32),
        in_specs=[pl.BlockSpec(memory_space=pltpu.SMEM), whole(), whole()],
        out_specs=whole(),
        compiler_params=params(4),
        name="relay",
    )(place, ends, rates)
    entering = lax.all_to_all(entering, "seq", split_axis=0, concat_axis=0, tiled=True)
    side = owners // 2
    owner = lax.axis_index("exp").astype(jnp.int32)
    chips = (owner // 2 + jnp.arange(side, dtype=jnp.int32)) % side
    order = jnp.concatenate([chips * 2 + 1 - owner % 2, chips * 2 + owner % 2])
    gated = pl.pallas_call(
        finish_kernel,
        out_shape=jax.ShapeDtypeStruct((length, channels), BF16),
        in_specs=[pl.BlockSpec(memory_space=pltpu.SMEM)] + [whole()] * 6 + [far()] * 4,
        out_specs=whole(),
        scratch_shapes=[
            pltpu.VMEM((SEG, channels), F32),
            pltpu.VMEM((STATE, SEG, channels), F32),
            pltpu.VMEM((1, channels), F32),
            pltpu.VMEM((length, channels), BF16),
            pltpu.VMEM((STATE, length, LANES), F32),
            pltpu.VMEM((channels // LANES, length, LANES), F32),
            pltpu.VMEM((channels // LANES, length, LANES), F32),
            pltpu.SemaphoreType.DMA((4,)),
        ],
        compiler_params=params(14),
        name="finish",
    )(
        order,
        entering.reshape(STATE, channels),
        rates,
        delta,
        packed,
        y_local,
        mixed,
        before,
        enter,
        d_skip[None, :],
        z_in,
    )
    width = out_proj.shape[1]
    features = seqs * width
    send, keep = pl.pallas_call(
        outward_kernel,
        out_shape=(
            jax.ShapeDtypeStruct((length // 2, features), BF16),
            jax.ShapeDtypeStruct((length // 2, features), F32),
        ),
        in_specs=[whole(), far()],
        out_specs=[whole()] * 2,
        scratch_shapes=[
            pltpu.VMEM((seqs, channels, width), BF16),
            pltpu.SemaphoreType.DMA((seqs,)),
        ],
        compiler_params=params(14),
        name="outward",
    )(gated, columns)
    swap = [(e, e + 1 - 2 * (e % 2)) for e in range(owners)]
    sums = keep + lax.ppermute(send, "exp", swap).astype(F32)
    sums = sums.reshape(side, length // owners, features)
    total = sums[0]
    for hop in range(1, side):
        route = [(e, (e + 2 * hop) % owners) for e in range(owners)]
        total = total + lax.ppermute(sums[hop].astype(BF16), "exp", route).astype(F32)
    return total


def shards(
    x_in,
    z_in,
    conv_weight,
    conv_bias,
    x_proj,
    dt_proj,
    dt_bias,
    a_log,
    d_skip,
    out_proj,
    residual,
    expert_ids,
    gate_weights,
    w_gate,
    w_up,
    w_down,
):
    owners = lax.axis_size("exp")
    tok_rows = residual.shape[0]
    mixed = mixer(
        x_in, z_in, conv_weight, conv_bias, x_proj, dt_proj, dt_bias, a_log, d_skip, out_proj
    )
    hidden = residual.astype(jnp.float32) + mixed
    normed = (hidden * lax.rsqrt(jnp.mean(hidden * hidden, axis=-1, keepdims=True) + 1e-06)).astype(
        jnp.bfloat16
    )
    capacity = max(2, tok_rows // 4)
    slots = owners * capacity
    chosen_count = expert_ids.shape[1]
    flat_ids = expert_ids.reshape(-1)
    hits = (flat_ids[:, None] == jnp.arange(owners, dtype=jnp.int32)[None, :]).astype(jnp.int32)
    before = jnp.cumsum(hits, axis=0) - hits
    ranked = jnp.sum(before * hits, axis=1)
    valid = jnp.sum(hits, axis=1)
    target = flat_ids * capacity + ranked
    placed = (
        (target[:, None] == jnp.arange(slots, dtype=jnp.int32)[None, :]) & (valid[:, None] > 0)
    ).astype(jnp.float32)
    dispatch_table = jnp.sum(placed.reshape(tok_rows, chosen_count, slots), axis=1)
    combine_table = jnp.sum(
        (placed * gate_weights.reshape(-1)[:, None]).reshape(tok_rows, chosen_count, slots), axis=1
    )
    outgoing = jnp.einsum(
        "ts,td->sd", dispatch_table.astype(jnp.bfloat16), normed, preferred_element_type=jnp.float32
    )
    outgoing = outgoing.astype(jnp.bfloat16).reshape(owners, capacity, -1)
    arrived = lax.all_to_all(outgoing, "exp", split_axis=0, concat_axis=0, tiled=True)
    summed = experts_on_grid(arrived.reshape(slots, -1), w_gate[0], w_up[0], w_down[0])
    expert_out = summed.reshape(owners, capacity, -1)
    returned_rows = lax.all_to_all(
        expert_out, "exp", split_axis=0, concat_axis=0, tiled=True
    ).reshape(slots, -1)
    combined = jnp.dot(
        combine_table, returned_rows.astype(jnp.float32), precision=lax.Precision.HIGHEST
    )
    return hidden + combined


def solution(mesh):
    placed = (
        P("seq", "exp"),
        P("seq", "exp"),
        P(None, "exp"),
        P("exp"),
        P("exp", None),
        P(None, "exp"),
        P("exp"),
        P("exp", None),
        P("exp"),
        P("exp", "seq"),
        P(("seq", "exp"), None),
        P(("seq", "exp"), None),
        P(("seq", "exp"), None),
        P("exp", None, "seq"),
        P("exp", None, "seq"),
        P("exp", "seq", None),
    )
    return jax.shard_map(
        shards, mesh=mesh, in_specs=placed, out_specs=P(("seq", "exp"), None), check_vma=False
    )
```

```python
import functools
import math

import jax
import jax.numpy as jnp
from jax import lax
from jax.experimental import pallas as pl
from jax.experimental.pallas import tpu as pltpu
from jax.sharding import PartitionSpec as P

RANK = 256
STATE = 16
CONV = 4
SEG = 8
LANES = 128
LOG2E = math.log2(math.e)
F32 = jnp.float32
BF16 = jnp.bfloat16
MIB = 1024 * 1024


def whole():
    return pl.BlockSpec(memory_space=pltpu.VMEM)


def far():
    return pl.BlockSpec(memory_space=pltpu.HBM)


def params(mib):
    return pltpu.CompilerParams(vmem_limit_bytes=mib * MIB)


def lines(stage):
    side = math.isqrt(lax.axis_size("seq"))
    owners = lax.axis_size("exp")
    groups = []
    for owner in range(owners):
        along_x = (owner % 2 == 0) == (stage == 0)
        for fixed in range(side):
            members = [(m * side + fixed if along_x else fixed * side + m) for m in range(side)]
            groups.append([m * owners + owner for m in members])
    return groups


def along(block, stage, distance):
    route = []
    for members in lines(stage):
        count = len(members)
        route += [(members[i], members[(i + distance) % count]) for i in range(count)]
    return lax.ppermute(block, ("seq", "exp"), route)


def passed_along(block, axis, distance):
    devices = range(lax.axis_size(axis))
    route = [(i - distance, i) for i in devices if i - distance in devices]
    return lax.ppermute(block, axis, route)


def conv_kernel(
    x_hbm,
    weight_hbm,
    bias_hbm,
    proj_hbm,
    rim_ref,
    mixed_ref,
    part_ref,
    x_ref,
    weight_ref,
    bias_ref,
    proj_ref,
    padded,
    sems,
):
    sources = (x_hbm, weight_hbm, bias_hbm, proj_hbm)
    targets = (x_ref, weight_ref, bias_ref, proj_ref)
    copies = [pltpu.make_async_copy(*pair, sems.at[k]) for k, pair in enumerate(zip(sources, targets))]
    for copy in copies:
        copy.start()
    length, channels = x_ref.shape
    steps = length // SEG
    head = 8
    for copy in copies[:3]:
        copy.wait()
    for lane in range(0, channels, LANES):
        block = padded.at[lane // LANES]
        block[head - (CONV - 1) : head, :] = rim_ref[:, lane : lane + LANES].astype(F32)
        block[head:, :] = x_ref[:, lane : lane + LANES].astype(F32)

    def step(i, carry):
        rows = pl.ds(pl.multiple_of(i * SEG, SEG), SEG)
        for lane in range(0, channels, LANES):
            lanes = pl.ds(lane, LANES)
            acc = jnp.broadcast_to(bias_ref[:, lanes], (SEG, LANES))
            for tap in range(CONV):
                taken = padded[
                    lane // LANES, pl.ds(i + head - (CONV - 1) + tap, SEG, stride=steps), :
                ]
                acc = acc + weight_ref[tap : tap + 1, lanes] * taken
            mixed_ref[rows, lanes] = (acc * jax.nn.sigmoid(acc)).astype(BF16).astype(F32)
        return carry

    lax.fori_loop(0, steps, step, 0)
    copies[3].wait()
    part_ref[...] = lax.dot_general(
        mixed_ref[...].astype(BF16),
        proj_ref[...],
        (((1,), (1,)), ((), ())),
        preferred_element_type=F32,
    )


def spread(target, packed_ref, first):
    packed = packed_ref[...].astype(F32)
    coef = packed[:, RANK : RANK + 2 * STATE] + packed[:, RANK + 2 * STATE :]
    for n in range(STATE):
        target[n] = jnp.broadcast_to(coef[:, first + n : first + n + 1], (coef.shape[0], LANES))


def scan_kernel(
    packed_ref,
    mixed_ref,
    rates_ref,
    proj_hbm,
    bias_hbm,
    y_ref,
    delta_ref,
    before_hbm,
    enter_hbm,
    msg_hbm,
    b_wide,
    c_wide,
    proj_ref,
    bias_ref,
    before_ref,
    enter_ref,
    msg_ref,
    in_sems,
    out_sems,
):
    length, channels = mixed_ref.shape
    steps = length // SEG
    copies = [
        pltpu.make_async_copy(proj_hbm, proj_ref, in_sems.at[0]),
        pltpu.make_async_copy(bias_hbm, bias_ref, in_sems.at[1]),
    ]
    for copy in copies:
        copy.start()
    spread(b_wide, packed_ref, 0)
    spread(c_wide, packed_ref, STATE)
    for copy in copies:
        copy.wait()
    copies = []
    raw = jnp.dot(packed_ref[:, :RANK], proj_ref[...], preferred_element_type=F32) + bias_ref[...]
    delta_ref[...] = jnp.maximum(raw, 0.0) + jnp.log1p(jnp.exp(-jnp.abs(raw)))
    row = lax.broadcasted_iota(jnp.int32, (SEG, LANES), 0)

    def shifted(value, by, fill):
        return jnp.where(row < by, fill, pltpu.roll(value, by, axis=0))

    for lane in range(0, channels, LANES):
        lanes = pl.ds(lane, LANES)
        rates = [
            jnp.broadcast_to(rates_ref[n : n + 1, lanes], (SEG, LANES)) for n in range(STATE)
        ]

        def step(i, carry):
            elapsed, states = carry
            rows = pl.ds(pl.multiple_of(i * SEG, SEG), SEG)
            delta = delta_ref[rows, lanes]
            drive = delta * mixed_ref[rows, lanes]
            fresh, terms = [], []
            for n in range(STATE):
                state = jnp.exp2(delta * rates[n]) * states[n] + drive * b_wide[n, rows, :]
                fresh.append(state)
                terms.append(state * c_wide[n, rows, :])
            while len(terms) > 1:
                terms = [a + b for a, b in zip(terms[::2], terms[1::2])]
            y_ref[rows, lanes] = terms[0]
            return elapsed + delta, tuple(fresh)

        zero = jnp.zeros((SEG, LANES), F32)
        elapsed, states = lax.fori_loop(0, steps, step, (zero, (zero,) * STATE), unroll=2)
        total = elapsed
        for by in (1, 2, 4):
            total = total + shifted(total, by, 0.0)
        before_ref[:, lanes] = shifted(total, 1, 0.0)
        last = total[SEG - 1 : SEG, :]
        for n in range(STATE):
            decay = jnp.exp2(elapsed * rates[n])
            state = states[n]
            for by in (1, 2, 4):
                state = decay * shifted(state, by, 0.0) + state
                decay = decay * shifted(decay, by, 1.0)
            enter_ref[n, :, lanes] = shifted(state, 1, 0.0)
            msg_ref[n, 0:1, lanes] = state[SEG - 1 : SEG, :]
            msg_ref[n, 1:2, lanes] = last
        block = lane // LANES
        fresh = [
            pltpu.make_async_copy(
                before_ref.at[:, lanes], before_hbm.at[:, lanes], out_sems.at[0, block]
            ),
            pltpu.make_async_copy(
                enter_ref.at[:, :, lanes], enter_hbm.at[:, :, lanes], out_sems.at[1, block]
            ),
            pltpu.make_async_copy(
                msg_ref.at[:, :, lanes], msg_hbm.at[:, :, lanes], out_sems.at[2, block]
            ),
        ]
        for copy in fresh:
            copy.start()
        copies += fresh
    for copy in copies:
        copy.wait()


def relay_kernel(place_ref, ends_ref, rates_ref, out_ref):
    rate = rates_ref[pl.ds(place_ref[0], 1), :]
    state = jnp.zeros_like(rate)
    for device in range(ends_ref.shape[0]):
        out_ref[device] = state
        state = jnp.exp2(ends_ref[device, 1:2, :] * rate) * state + ends_ref[device, 0:1, :]


def finish_kernel(
    order_ref,
    entering_ref,
    rates_ref,
    delta_ref,
    packed_ref,
    y_ref,
    mixed_ref,
    before_hbm,
    enter_hbm,
    skip_hbm,
    z_hbm,
    gated_ref,
    before_ref,
    enter_ref,
    skip_ref,
    z_ref,
    c_wide,
    z_wide,
    gated,
    sems,
):
    length, channels = mixed_ref.shape
    steps = length // SEG
    sources = (before_hbm, enter_hbm, skip_hbm, z_hbm)
    targets = (before_ref, enter_ref, skip_ref, z_ref)
    copies = [pltpu.make_async_copy(*pair, sems.at[k]) for k, pair in enumerate(zip(sources, targets))]
    for copy in copies:
        copy.start()
    spread(c_wide, packed_ref, STATE)
    for copy in copies:
        copy.wait()
    for lane in range(0, channels, LANES):
        z_wide[lane // LANES] = z_ref[:, lane : lane + LANES].astype(F32)

    for lane in range(0, channels, LANES):
        lanes = pl.ds(lane, LANES)
        rates = [
            jnp.broadcast_to(rates_ref[n : n + 1, lanes], (SEG, LANES)) for n in range(STATE)
        ]
        before = before_ref[:, lanes]
        held = [
            jnp.exp2(before * rates[n]) * entering_ref[n : n + 1, lanes] + enter_ref[n, :, lanes]
            for n in range(STATE)
        ]
        skip = skip_ref[:, lanes]

        def step(i, elapsed):
            rows = pl.ds(pl.multiple_of(i * SEG, SEG), SEG)
            apart = pl.ds(i, SEG, stride=steps)
            elapsed = elapsed + delta_ref[rows, lanes]
            terms = [
                jnp.exp2(elapsed * rates[n]) * held[n] * c_wide[n, rows, :] for n in range(STATE)
            ]
            while len(terms) > 1:
                terms = [a + b for a, b in zip(terms[::2], terms[1::2])]
            output = y_ref[rows, lanes] + terms[0] + skip * mixed_ref[rows, lanes]
            z = z_wide[lane // LANES, apart, :]
            gated[lane // LANES, apart, :] = output * (z * jax.nn.sigmoid(z))
            return elapsed

        lax.fori_loop(0, steps, step, jnp.zeros((SEG, LANES), F32), unroll=2)
    for place in range(SEG):
        rows = pl.ds(pl.multiple_of(order_ref[place] * steps, steps), steps)
        for lane in range(0, channels, LANES):
            gated_ref[place * steps : (place + 1) * steps, lane : lane + LANES] = gated[
                lane // LANES, rows, :
            ].astype(BF16)


def outward_kernel(gated_ref, proj_hbm, send_ref, keep_ref, proj, arrived):
    parts, _, width = proj_hbm.shape
    middle = send_ref.shape[0]
    for part in range(parts):
        pltpu.make_async_copy(proj_hbm.at[part], proj.at[part], arrived.at[part]).start()

    def product(part, carry):
        pltpu.make_async_copy(proj_hbm.at[part], proj.at[part], arrived.at[part]).wait()
        columns = pl.ds(pl.multiple_of(part * width, width), width)
        terms = jnp.dot(gated_ref[...], proj[part], preferred_element_type=F32)
        send_ref[:, columns] = terms[:middle].astype(BF16)
        keep_ref[:, columns] = terms[middle:]
        return carry

    lax.fori_loop(0, parts, product, 0)


def expert_kernel(rows_ref, gate_ref, up_ref, down_ref, first_ref, second_ref, inner):
    tile = 256
    middle = first_ref.shape[0]

    def widen(part, carry):
        columns = pl.ds(pl.multiple_of(part * tile, tile), tile)
        gate = jnp.dot(rows_ref[...], gate_ref[:, columns], preferred_element_type=F32)
        upper = jnp.dot(rows_ref[...], up_ref[:, columns], preferred_element_type=F32)
        inner[:, columns] = (gate * jax.nn.sigmoid(gate) * upper).astype(BF16)
        return carry

    lax.fori_loop(0, inner.shape[1] // tile, widen, 0)

    def narrow(part, carry):
        columns = pl.ds(pl.multiple_of(part * tile, tile), tile)
        piece = jnp.dot(inner[...], down_ref[:, columns], preferred_element_type=F32)
        first_ref[:, columns] = piece[:middle].astype(BF16)
        second_ref[:, columns] = piece[middle:].astype(BF16)
        return carry

    lax.fori_loop(0, first_ref.shape[1] // tile, narrow, 0)


def expert(rows, gate, up, down):
    count, features = rows.shape
    hidden = gate.shape[1]
    return pl.pallas_call(
        expert_kernel,
        out_shape=(jax.ShapeDtypeStruct((count // 2, features), BF16),) * 2,
        in_specs=[whole()] * 4,
        out_specs=[whole()] * 2,
        scratch_shapes=[pltpu.VMEM((count, hidden), BF16)],
        compiler_params=params(12),
        cost_estimate=pl.CostEstimate(
            flops=6 * count * features * hidden,
            bytes_accessed=4 * count * features,
            transcendentals=count * hidden,
        ),
        name="expert",
    )(rows, gate, up, down)


def halves(block):
    middle = block.shape[0] // 2
    return block[:middle], block[middle:]


def added(*blocks):
    total = blocks[0].astype(F32)
    for block in blocks[1:]:
        total = total + block.astype(F32)
    return total.astype(BF16)


def experts_on_grid(rows, gate, up, down):
    run = functools.partial(expert, gate=gate, up=up, down=down)
    behind = along(rows, 0, 1)
    ahead = along(rows, 0, -1)
    across = along(rows, 0, 2)
    own = jnp.concatenate([rows, behind, ahead, across], axis=0)
    behind = along(own, 1, 1)
    ahead = along(own, 1, -1)
    own_out = run(own)
    behind, ahead, own_out = lax.optimization_barrier((behind, ahead, own_out))
    far_first = along(halves(behind)[0], 1, 1)
    far_second = along(halves(ahead)[1], 1, -1)
    behind_first, behind_second = run(behind)
    early_first = along(behind_first, 1, -1)
    ahead_first, ahead_second = run(ahead)
    early_second = along(ahead_second, 1, 1)
    far_first, far_second, behind_second, ahead_first = lax.optimization_barrier(
        (far_first, far_second, behind_second, ahead_first)
    )
    across_first, across_second = run(jnp.concatenate([far_first, far_second], axis=0))
    late_first = along(added(ahead_first, along(across_first, 1, 1)), 1, 1)
    late_second = along(added(behind_second, along(across_second, 1, -1)), 1, -1)
    first = added(own_out[0], early_first, late_first)
    second = added(own_out[1], early_second, late_second)
    (kept, behind), (ahead, across) = halves(first), halves(second)
    return added(kept, along(behind, 0, -1), along(ahead, 0, 1), along(across, 0, 2))


def mixer(x_in, z_in, conv_weight, conv_bias, x_proj, dt_proj, dt_bias, a_log, d_skip, out_proj):
    length, channels = x_in.shape
    steps = length // SEG
    owners = lax.axis_size("exp")
    seqs = lax.axis_size("seq")
    columns = lax.all_gather(out_proj, "seq", axis=0)
    rates = (-jnp.exp(a_log) * LOG2E).T
    rim = passed_along(x_in[length - (CONV - 1) :], "seq", 1)
    mixed, partial = pl.pallas_call(
        conv_kernel,
        out_shape=(
            jax.ShapeDtypeStruct((length, channels), F32),
            jax.ShapeDtypeStruct((length, RANK + 2 * STATE), F32),
        ),
        in_specs=[far()] * 4 + [whole()],
        out_specs=[whole()] * 2,
        scratch_shapes=[
            pltpu.VMEM(x_in.shape, BF16),
            pltpu.VMEM(conv_weight.shape, F32),
            pltpu.VMEM((1, channels), F32),
            pltpu.VMEM(x_proj.shape[::-1], BF16),
            pltpu.VMEM((channels // LANES, length + 8, LANES), F32),
            pltpu.SemaphoreType.DMA((4,)),
        ],
        compiler_params=params(12),
        name="conv",
    )(x_in, conv_weight, conv_bias[None, :], x_proj.T, rim)
    share = lax.all_to_all(
        partial.reshape(owners, length // owners, -1), "exp", split_axis=0, concat_axis=0, tiled=True
    )
    summed = jnp.sum(share, axis=0)
    low = summed[:, :RANK].astype(BF16)
    coef = summed[:, RANK:]
    coef_high = coef.astype(BF16)
    coef_low = (coef - coef_high.astype(F32)).astype(BF16)
    packed = jnp.concatenate([low, coef_high, coef_low], axis=1)
    packed = lax.all_to_all(
        jnp.broadcast_to(packed[None], (owners,) + packed.shape),
        "exp",
        split_axis=0,
        concat_axis=0,
        tiled=True,
    ).reshape(length, -1)
    y_local, delta, before, enter, message = pl.pallas_call(
        scan_kernel,
        out_shape=(
            jax.ShapeDtypeStruct((length, channels), F32),
            jax.ShapeDtypeStruct((length, channels), F32),
            jax.ShapeDtypeStruct((SEG, channels), F32),
            jax.ShapeDtypeStruct((STATE, SEG, channels), F32),
            jax.ShapeDtypeStruct((STATE, 2, channels), F32),
        ),
        in_specs=[whole()] * 3 + [far()] * 2,
        out_specs=[whole()] * 2 + [far()] * 3,
        scratch_shapes=[
            pltpu.VMEM((STATE, length, LANES), F32),
            pltpu.VMEM((STATE, length, LANES), F32),
            pltpu.VMEM(dt_proj.shape, BF16),
            pltpu.VMEM((1, channels), F32),
            pltpu.VMEM((SEG, channels), F32),
            pltpu.VMEM((STATE, SEG, channels), F32),
            pltpu.VMEM((STATE, 2, channels), F32),
            pltpu.SemaphoreType.DMA((2,)),
            pltpu.SemaphoreType.DMA((3, channels // LANES)),
        ],
        compiler_params=params(14),
        name="scan",
    )(packed, mixed, rates, dt_proj, dt_bias[None, :])
    ends = lax.all_to_all(message, "seq", split_axis=0, concat_axis=0, tiled=True)
    place = lax.axis_index("seq").astype(jnp.int32).reshape(1)
    entering = pl.pallas_call(
        relay_kernel,
        out_shape=jax.ShapeDtypeStruct((seqs, 1, channels), F32),
        in_specs=[pl.BlockSpec(memory_space=pltpu.SMEM), whole(), whole()],
        out_specs=whole(),
        compiler_params=params(4),
        name="relay",
    )(place, ends, rates)
    entering = lax.all_to_all(entering, "seq", split_axis=0, concat_axis=0, tiled=True)
    side = owners // 2
    owner = lax.axis_index("exp").astype(jnp.int32)
    chips = (owner // 2 + jnp.arange(side, dtype=jnp.int32)) % side
    order = jnp.concatenate([chips * 2 + 1 - owner % 2, chips * 2 + owner % 2])
    gated = pl.pallas_call(
        finish_kernel,
        out_shape=jax.ShapeDtypeStruct((length, channels), BF16),
        in_specs=[pl.BlockSpec(memory_space=pltpu.SMEM)] + [whole()] * 6 + [far()] * 4,
        out_specs=whole(),
        scratch_shapes=[
            pltpu.VMEM((SEG, channels), F32),
            pltpu.VMEM((STATE, SEG, channels), F32),
            pltpu.VMEM((1, channels), F32),
            pltpu.VMEM((length, channels), BF16),
            pltpu.VMEM((STATE, length, LANES), F32),
            pltpu.VMEM((channels // LANES, length, LANES), F32),
            pltpu.VMEM((channels // LANES, length, LANES), F32),
            pltpu.SemaphoreType.DMA((4,)),
        ],
        compiler_params=params(14),
        name="finish",
    )(
        order,
        entering.reshape(STATE, channels),
        rates,
        delta,
        packed,
        y_local,
        mixed,
        before,
        enter,
        d_skip[None, :],
        z_in,
    )
    width = out_proj.shape[1]
    features = seqs * width
    send, keep = pl.pallas_call(
        outward_kernel,
        out_shape=(
            jax.ShapeDtypeStruct((length // 2, features), BF16),
            jax.ShapeDtypeStruct((length // 2, features), F32),
        ),
        in_specs=[whole(), far()],
        out_specs=[whole()] * 2,
        scratch_shapes=[
            pltpu.VMEM((seqs, channels, width), BF16),
            pltpu.SemaphoreType.DMA((seqs,)),
        ],
        compiler_params=params(50),
        name="outward",
    )(gated, columns)
    swap = [(e, e + 1 - 2 * (e % 2)) for e in range(owners)]
    sums = keep + lax.ppermute(send, "exp", swap).astype(F32)
    sums = sums.reshape(side, length // owners, features)
    total = sums[0]
    for hop in range(1, side):
        route = [(e, (e + 2 * hop) % owners) for e in range(owners)]
        total = total + lax.ppermute(sums[hop].astype(BF16), "exp", route).astype(F32)
    return total


def shards(
    x_in,
    z_in,
    conv_weight,
    conv_bias,
    x_proj,
    dt_proj,
    dt_bias,
    a_log,
    d_skip,
    out_proj,
    residual,
    expert_ids,
    gate_weights,
    w_gate,
    w_up,
    w_down,
):
    owners = lax.axis_size("exp")
    tok_rows = residual.shape[0]
    mixed = mixer(
        x_in, z_in, conv_weight, conv_bias, x_proj, dt_proj, dt_bias, a_log, d_skip, out_proj
    )
    hidden = residual.astype(jnp.float32) + mixed
    normed = (hidden * lax.rsqrt(jnp.mean(hidden * hidden, axis=-1, keepdims=True) + 1e-06)).astype(
        jnp.bfloat16
    )
    capacity = max(2, tok_rows // 4)
    slots = owners * capacity
    chosen_count = expert_ids.shape[1]
    flat_ids = expert_ids.reshape(-1)
    hits = (flat_ids[:, None] == jnp.arange(owners, dtype=jnp.int32)[None, :]).astype(jnp.int32)
    before = jnp.cumsum(hits, axis=0) - hits
    ranked = jnp.sum(before * hits, axis=1)
    valid = jnp.sum(hits, axis=1)
    target = flat_ids * capacity + ranked
    placed = (
        (target[:, None] == jnp.arange(slots, dtype=jnp.int32)[None, :]) & (valid[:, None] > 0)
    ).astype(jnp.float32)
    dispatch_table = jnp.sum(placed.reshape(tok_rows, chosen_count, slots), axis=1)
    combine_table = jnp.sum(
        (placed * gate_weights.reshape(-1)[:, None]).reshape(tok_rows, chosen_count, slots), axis=1
    )
    outgoing = jnp.einsum(
        "ts,td->sd", dispatch_table.astype(jnp.bfloat16), normed, preferred_element_type=jnp.float32
    )
    outgoing = outgoing.astype(jnp.bfloat16).reshape(owners, capacity, -1)
    arrived = lax.all_to_all(outgoing, "exp", split_axis=0, concat_axis=0, tiled=True)
    summed = experts_on_grid(arrived.reshape(slots, -1), w_gate[0], w_up[0], w_down[0])
    expert_out = summed.reshape(owners, capacity, -1)
    returned_rows = lax.all_to_all(
        expert_out, "exp", split_axis=0, concat_axis=0, tiled=True
    ).reshape(slots, -1)
    combined = jnp.dot(
        combine_table, returned_rows.astype(jnp.float32), precision=lax.Precision.HIGHEST
    )
    return hidden + combined


def solution(mesh):
    placed = (
        P("seq", "exp"),
        P("seq", "exp"),
        P(None, "exp"),
        P("exp"),
        P("exp", None),
        P(None, "exp"),
        P("exp"),
        P("exp", None),
        P("exp"),
        P("exp", "seq"),
        P(("seq", "exp"), None),
        P(("seq", "exp"), None),
        P(("seq", "exp"), None),
        P("exp", None, "seq"),
        P("exp", None, "seq"),
        P("exp", "seq", None),
    )
    return jax.shard_map(
        shards, mesh=mesh, in_specs=placed, out_specs=P(("seq", "exp"), None), check_vma=False
    )
```

```python
import functools
import math

import jax
import jax.numpy as jnp
from jax import lax
from jax.experimental import pallas as pl
from jax.experimental.pallas import tpu as pltpu
from jax.sharding import PartitionSpec as P

RANK = 256
STATE = 16
CONV = 4
SEG = 8
LANES = 128
LOG2E = math.log2(math.e)
F32 = jnp.float32
BF16 = jnp.bfloat16
MIB = 1024 * 1024


def whole():
    return pl.BlockSpec(memory_space=pltpu.VMEM)


def far():
    return pl.BlockSpec(memory_space=pltpu.HBM)


def params(mib):
    return pltpu.CompilerParams(vmem_limit_bytes=mib * MIB)


def lines(stage):
    side = math.isqrt(lax.axis_size("seq"))
    owners = lax.axis_size("exp")
    groups = []
    for owner in range(owners):
        along_x = (owner % 2 == 0) == (stage == 0)
        for fixed in range(side):
            members = [(m * side + fixed if along_x else fixed * side + m) for m in range(side)]
            groups.append([m * owners + owner for m in members])
    return groups


def along(block, stage, distance):
    route = []
    for members in lines(stage):
        count = len(members)
        route += [(members[i], members[(i + distance) % count]) for i in range(count)]
    return lax.ppermute(block, ("seq", "exp"), route)


def passed_along(block, axis, distance):
    devices = range(lax.axis_size(axis))
    route = [(i - distance, i) for i in devices if i - distance in devices]
    return lax.ppermute(block, axis, route)


def conv_kernel(
    x_hbm,
    weight_hbm,
    bias_hbm,
    proj_hbm,
    rim_ref,
    mixed_ref,
    part_ref,
    x_ref,
    weight_ref,
    bias_ref,
    proj_ref,
    padded,
    sems,
):
    sources = (x_hbm, weight_hbm, bias_hbm, proj_hbm)
    targets = (x_ref, weight_ref, bias_ref, proj_ref)
    copies = [pltpu.make_async_copy(*pair, sems.at[k]) for k, pair in enumerate(zip(sources, targets))]
    for copy in copies:
        copy.start()
    length, channels = x_ref.shape
    steps = length // SEG
    head = 8
    for copy in copies[:3]:
        copy.wait()
    for lane in range(0, channels, LANES):
        block = padded.at[lane // LANES]
        block[head - (CONV - 1) : head, :] = rim_ref[:, lane : lane + LANES].astype(F32)
        block[head:, :] = x_ref[:, lane : lane + LANES].astype(F32)

    def step(i, carry):
        rows = pl.ds(pl.multiple_of(i * SEG, SEG), SEG)
        for lane in range(0, channels, LANES):
            lanes = pl.ds(lane, LANES)
            acc = jnp.broadcast_to(bias_ref[:, lanes], (SEG, LANES))
            for tap in range(CONV):
                taken = padded[
                    lane // LANES, pl.ds(i + head - (CONV - 1) + tap, SEG, stride=steps), :
                ]
                acc = acc + weight_ref[tap : tap + 1, lanes] * taken
            mixed_ref[rows, lanes] = (acc * jax.nn.sigmoid(acc)).astype(BF16).astype(F32)
        return carry

    lax.fori_loop(0, steps, step, 0)
    copies[3].wait()
    part_ref[...] = lax.dot_general(
        mixed_ref[...].astype(BF16),
        proj_ref[...],
        (((1,), (1,)), ((), ())),
        preferred_element_type=F32,
    )


def spread(target, packed_ref, first):
    packed = packed_ref[...].astype(F32)
    coef = packed[:, RANK : RANK + 2 * STATE] + packed[:, RANK + 2 * STATE :]
    for n in range(STATE):
        target[n] = jnp.broadcast_to(coef[:, first + n : first + n + 1], (coef.shape[0], LANES))


def scan_kernel(
    packed_ref,
    mixed_ref,
    rates_ref,
    proj_hbm,
    bias_hbm,
    y_ref,
    delta_ref,
    before_hbm,
    enter_hbm,
    msg_hbm,
    b_wide,
    c_wide,
    proj_ref,
    bias_ref,
    before_ref,
    enter_ref,
    msg_ref,
    in_sems,
    out_sems,
):
    length, channels = mixed_ref.shape
    steps = length // SEG
    copies = [
        pltpu.make_async_copy(proj_hbm, proj_ref, in_sems.at[0]),
        pltpu.make_async_copy(bias_hbm, bias_ref, in_sems.at[1]),
    ]
    for copy in copies:
        copy.start()
    spread(b_wide, packed_ref, 0)
    spread(c_wide, packed_ref, STATE)
    for copy in copies:
        copy.wait()
    copies = []
    raw = jnp.dot(packed_ref[:, :RANK], proj_ref[...], preferred_element_type=F32) + bias_ref[...]
    delta_ref[...] = jnp.maximum(raw, 0.0) + jnp.log1p(jnp.exp(-jnp.abs(raw)))
    row = lax.broadcasted_iota(jnp.int32, (SEG, LANES), 0)

    def shifted(value, by, fill):
        return jnp.where(row < by, fill, pltpu.roll(value, by, axis=0))

    for lane in range(0, channels, LANES):
        lanes = pl.ds(lane, LANES)
        rates = [
            jnp.broadcast_to(rates_ref[n : n + 1, lanes], (SEG, LANES)) for n in range(STATE)
        ]

        def step(i, carry):
            elapsed, states = carry
            rows = pl.ds(pl.multiple_of(i * SEG, SEG), SEG)
            delta = delta_ref[rows, lanes]
            drive = delta * mixed_ref[rows, lanes]
            fresh, terms = [], []
            for n in range(STATE):
                state = jnp.exp2(delta * rates[n]) * states[n] + drive * b_wide[n, rows, :]
                fresh.append(state)
                terms.append(state * c_wide[n, rows, :])
            while len(terms) > 1:
                terms = [a + b for a, b in zip(terms[::2], terms[1::2])]
            y_ref[rows, lanes] = terms[0]
            return elapsed + delta, tuple(fresh)

        zero = jnp.zeros((SEG, LANES), F32)
        elapsed, states = lax.fori_loop(0, steps, step, (zero, (zero,) * STATE), unroll=2)
        total = elapsed
        for by in (1, 2, 4):
            total = total + shifted(total, by, 0.0)
        before_ref[:, lanes] = shifted(total, 1, 0.0)
        last = total[SEG - 1 : SEG, :]
        for n in range(STATE):
            decay = jnp.exp2(elapsed * rates[n])
            state = states[n]
            for by in (1, 2, 4):
                state = decay * shifted(state, by, 0.0) + state
                decay = decay * shifted(decay, by, 1.0)
            enter_ref[n, :, lanes] = shifted(state, 1, 0.0)
            msg_ref[n, 0:1, lanes] = state[SEG - 1 : SEG, :]
            msg_ref[n, 1:2, lanes] = last
        block = lane // LANES
        fresh = [
            pltpu.make_async_copy(
                before_ref.at[:, lanes], before_hbm.at[:, lanes], out_sems.at[0, block]
            ),
            pltpu.make_async_copy(
                enter_ref.at[:, :, lanes], enter_hbm.at[:, :, lanes], out_sems.at[1, block]
            ),
            pltpu.make_async_copy(
                msg_ref.at[:, :, lanes], msg_hbm.at[:, :, lanes], out_sems.at[2, block]
            ),
        ]
        for copy in fresh:
            copy.start()
        copies += fresh
    for copy in copies:
        copy.wait()


def relay_kernel(place_ref, ends_ref, rates_ref, out_ref):
    rate = rates_ref[pl.ds(place_ref[0], 1), :]
    state = jnp.zeros_like(rate)
    for device in range(ends_ref.shape[0]):
        out_ref[device] = state
        state = jnp.exp2(ends_ref[device, 1:2, :] * rate) * state + ends_ref[device, 0:1, :]


def finish_kernel(
    order_ref,
    entering_ref,
    rates_ref,
    delta_ref,
    packed_ref,
    y_ref,
    mixed_ref,
    before_hbm,
    enter_hbm,
    skip_hbm,
    z_hbm,
    gated_ref,
    before_ref,
    enter_ref,
    skip_ref,
    z_ref,
    c_wide,
    z_wide,
    gated,
    sems,
):
    length, channels = mixed_ref.shape
    steps = length // SEG
    sources = (before_hbm, enter_hbm, skip_hbm, z_hbm)
    targets = (before_ref, enter_ref, skip_ref, z_ref)
    copies = [pltpu.make_async_copy(*pair, sems.at[k]) for k, pair in enumerate(zip(sources, targets))]
    for copy in copies:
        copy.start()
    spread(c_wide, packed_ref, STATE)
    for copy in copies:
        copy.wait()
    for lane in range(0, channels, LANES):
        z_wide[lane // LANES] = z_ref[:, lane : lane + LANES].astype(F32)

    for lane in range(0, channels, LANES):
        lanes = pl.ds(lane, LANES)
        rates = [
            jnp.broadcast_to(rates_ref[n : n + 1, lanes], (SEG, LANES)) for n in range(STATE)
        ]
        before = before_ref[:, lanes]
        held = [
            jnp.exp2(before * rates[n]) * entering_ref[n : n + 1, lanes] + enter_ref[n, :, lanes]
            for n in range(STATE)
        ]
        skip = skip_ref[:, lanes]

        def step(i, elapsed):
            rows = pl.ds(pl.multiple_of(i * SEG, SEG), SEG)
            apart = pl.ds(i, SEG, stride=steps)
            elapsed = elapsed + delta_ref[rows, lanes]
            terms = [
                jnp.exp2(elapsed * rates[n]) * held[n] * c_wide[n, rows, :] for n in range(STATE)
            ]
            while len(terms) > 1:
                terms = [a + b for a, b in zip(terms[::2], terms[1::2])]
            output = y_ref[rows, lanes] + terms[0] + skip * mixed_ref[rows, lanes]
            z = z_wide[lane // LANES, apart, :]
            gated[lane // LANES, apart, :] = output * (z * jax.nn.sigmoid(z))
            return elapsed

        lax.fori_loop(0, steps, step, jnp.zeros((SEG, LANES), F32), unroll=2)
    for place in range(SEG):
        rows = pl.ds(pl.multiple_of(order_ref[place] * steps, steps), steps)
        for lane in range(0, channels, LANES):
            gated_ref[place * steps : (place + 1) * steps, lane : lane + LANES] = gated[
                lane // LANES, rows, :
            ].astype(BF16)


def outward_kernel(gated_ref, proj_hbm, send_ref, keep_ref, proj, arrived):
    parts, _, width = proj_hbm.shape
    middle = send_ref.shape[0]
    for part in range(parts):
        pltpu.make_async_copy(proj_hbm.at[part], proj.at[part], arrived.at[part]).start()

    def product(part, carry):
        pltpu.make_async_copy(proj_hbm.at[part], proj.at[part], arrived.at[part]).wait()
        columns = pl.ds(pl.multiple_of(part * width, width), width)
        terms = jnp.dot(gated_ref[...], proj[part], preferred_element_type=F32)
        send_ref[:, columns] = terms[:middle].astype(BF16)
        keep_ref[:, columns] = terms[middle:]
        return carry

    lax.fori_loop(0, parts, product, 0)


def expert_kernel(rows_ref, gate_ref, up_ref, down_ref, first_ref, second_ref, inner):
    tile = 256
    middle = first_ref.shape[0]

    def widen(part, carry):
        columns = pl.ds(pl.multiple_of(part * tile, tile), tile)
        gate = jnp.dot(rows_ref[...], gate_ref[:, columns], preferred_element_type=F32)
        upper = jnp.dot(rows_ref[...], up_ref[:, columns], preferred_element_type=F32)
        inner[:, columns] = (gate * jax.nn.sigmoid(gate) * upper).astype(BF16)
        return carry

    lax.fori_loop(0, inner.shape[1] // tile, widen, 0)

    def narrow(part, carry):
        columns = pl.ds(pl.multiple_of(part * tile, tile), tile)
        piece = jnp.dot(inner[...], down_ref[:, columns], preferred_element_type=F32)
        first_ref[:, columns] = piece[:middle].astype(BF16)
        second_ref[:, columns] = piece[middle:].astype(BF16)
        return carry

    lax.fori_loop(0, first_ref.shape[1] // tile, narrow, 0)


def expert(rows, gate, up, down):
    count, features = rows.shape
    hidden = gate.shape[1]
    return pl.pallas_call(
        expert_kernel,
        out_shape=(jax.ShapeDtypeStruct((count // 2, features), BF16),) * 2,
        in_specs=[whole()] * 4,
        out_specs=[whole()] * 2,
        scratch_shapes=[pltpu.VMEM((count, hidden), BF16)],
        compiler_params=params(12),
        cost_estimate=pl.CostEstimate(
            flops=6 * count * features * hidden,
            bytes_accessed=4 * count * features,
            transcendentals=count * hidden,
        ),
        name="expert",
    )(rows, gate, up, down)


def halves(block):
    middle = block.shape[0] // 2
    return block[:middle], block[middle:]


def added(*blocks):
    total = blocks[0].astype(F32)
    for block in blocks[1:]:
        total = total + block.astype(F32)
    return total.astype(BF16)


def experts_on_grid(rows, gate, up, down):
    run = functools.partial(expert, gate=gate, up=up, down=down)
    behind = along(rows, 0, 1)
    ahead = along(rows, 0, -1)
    across = along(rows, 0, 2)
    own = jnp.concatenate([rows, behind, ahead, across], axis=0)
    behind = along(own, 1, 1)
    ahead = along(own, 1, -1)
    own_out = run(own)
    behind, ahead, own_out = lax.optimization_barrier((behind, ahead, own_out))
    far_first = along(halves(behind)[0], 1, 1)
    far_second = along(halves(ahead)[1], 1, -1)
    behind_first, behind_second = run(behind)
    early_first = along(behind_first, 1, -1)
    ahead_first, ahead_second = run(ahead)
    early_second = along(ahead_second, 1, 1)
    far_first, far_second, behind_second, ahead_first = lax.optimization_barrier(
        (far_first, far_second, behind_second, ahead_first)
    )
    across_first, across_second = run(jnp.concatenate([far_first, far_second], axis=0))
    across_first, across_second, early_first, early_second = lax.optimization_barrier(
        (across_first, across_second, early_first, early_second)
    )
    late_first = along(added(ahead_first, along(across_first, 1, 1)), 1, 1)
    late_second = along(added(behind_second, along(across_second, 1, -1)), 1, -1)
    first = added(own_out[0], early_first, late_first)
    second = added(own_out[1], early_second, late_second)
    (kept, behind), (ahead, across) = halves(first), halves(second)
    return added(kept, along(behind, 0, -1), along(ahead, 0, 1), along(across, 0, 2))


def mixer(x_in, z_in, conv_weight, conv_bias, x_proj, dt_proj, dt_bias, a_log, d_skip, out_proj):
    length, channels = x_in.shape
    steps = length // SEG
    owners = lax.axis_size("exp")
    seqs = lax.axis_size("seq")
    columns = lax.all_gather(out_proj, "seq", axis=0)
    rates = (-jnp.exp(a_log) * LOG2E).T
    rim = passed_along(x_in[length - (CONV - 1) :], "seq", 1)
    mixed, partial = pl.pallas_call(
        conv_kernel,
        out_shape=(
            jax.ShapeDtypeStruct((length, channels), F32),
            jax.ShapeDtypeStruct((length, RANK + 2 * STATE), F32),
        ),
        in_specs=[far()] * 4 + [whole()],
        out_specs=[whole()] * 2,
        scratch_shapes=[
            pltpu.VMEM(x_in.shape, BF16),
            pltpu.VMEM(conv_weight.shape, F32),
            pltpu.VMEM((1, channels), F32),
            pltpu.VMEM(x_proj.shape[::-1], BF16),
            pltpu.VMEM((channels // LANES, length + 8, LANES), F32),
            pltpu.SemaphoreType.DMA((4,)),
        ],
        compiler_params=params(12),
        name="conv",
    )(x_in, conv_weight, conv_bias[None, :], x_proj.T, rim)
    share = lax.all_to_all(
        partial.reshape(owners, length // owners, -1), "exp", split_axis=0, concat_axis=0, tiled=True
    )
    summed = jnp.sum(share, axis=0)
    low = summed[:, :RANK].astype(BF16)
    coef = summed[:, RANK:]
    coef_high = coef.astype(BF16)
    coef_low = (coef - coef_high.astype(F32)).astype(BF16)
    packed = jnp.concatenate([low, coef_high, coef_low], axis=1)
    packed = lax.all_to_all(
        jnp.broadcast_to(packed[None], (owners,) + packed.shape),
        "exp",
        split_axis=0,
        concat_axis=0,
        tiled=True,
    ).reshape(length, -1)
    y_local, delta, before, enter, message = pl.pallas_call(
        scan_kernel,
        out_shape=(
            jax.ShapeDtypeStruct((length, channels), F32),
            jax.ShapeDtypeStruct((length, channels), F32),
            jax.ShapeDtypeStruct((SEG, channels), F32),
            jax.ShapeDtypeStruct((STATE, SEG, channels), F32),
            jax.ShapeDtypeStruct((STATE, 2, channels), F32),
        ),
        in_specs=[whole()] * 3 + [far()] * 2,
        out_specs=[whole()] * 2 + [far()] * 3,
        scratch_shapes=[
            pltpu.VMEM((STATE, length, LANES), F32),
            pltpu.VMEM((STATE, length, LANES), F32),
            pltpu.VMEM(dt_proj.shape, BF16),
            pltpu.VMEM((1, channels), F32),
            pltpu.VMEM((SEG, channels), F32),
            pltpu.VMEM((STATE, SEG, channels), F32),
            pltpu.VMEM((STATE, 2, channels), F32),
            pltpu.SemaphoreType.DMA((2,)),
            pltpu.SemaphoreType.DMA((3, channels // LANES)),
        ],
        compiler_params=params(14),
        name="scan",
    )(packed, mixed, rates, dt_proj, dt_bias[None, :])
    ends = lax.all_to_all(message, "seq", split_axis=0, concat_axis=0, tiled=True)
    place = lax.axis_index("seq").astype(jnp.int32).reshape(1)
    entering = pl.pallas_call(
        relay_kernel,
        out_shape=jax.ShapeDtypeStruct((seqs, 1, channels), F32),
        in_specs=[pl.BlockSpec(memory_space=pltpu.SMEM), whole(), whole()],
        out_specs=whole(),
        compiler_params=params(4),
        name="relay",
    )(place, ends, rates)
    entering = lax.all_to_all(entering, "seq", split_axis=0, concat_axis=0, tiled=True)
    side = owners // 2
    owner = lax.axis_index("exp").astype(jnp.int32)
    chips = (owner // 2 + jnp.arange(side, dtype=jnp.int32)) % side
    order = jnp.concatenate([chips * 2 + 1 - owner % 2, chips * 2 + owner % 2])
    gated = pl.pallas_call(
        finish_kernel,
        out_shape=jax.ShapeDtypeStruct((length, channels), BF16),
        in_specs=[pl.BlockSpec(memory_space=pltpu.SMEM)] + [whole()] * 6 + [far()] * 4,
        out_specs=whole(),
        scratch_shapes=[
            pltpu.VMEM((SEG, channels), F32),
            pltpu.VMEM((STATE, SEG, channels), F32),
            pltpu.VMEM((1, channels), F32),
            pltpu.VMEM((length, channels), BF16),
            pltpu.VMEM((STATE, length, LANES), F32),
            pltpu.VMEM((channels // LANES, length, LANES), F32),
            pltpu.VMEM((channels // LANES, length, LANES), F32),
            pltpu.SemaphoreType.DMA((4,)),
        ],
        compiler_params=params(14),
        name="finish",
    )(
        order,
        entering.reshape(STATE, channels),
        rates,
        delta,
        packed,
        y_local,
        mixed,
        before,
        enter,
        d_skip[None, :],
        z_in,
    )
    width = out_proj.shape[1]
    features = seqs * width
    send, keep = pl.pallas_call(
        outward_kernel,
        out_shape=(
            jax.ShapeDtypeStruct((length // 2, features), BF16),
            jax.ShapeDtypeStruct((length // 2, features), F32),
        ),
        in_specs=[whole(), far()],
        out_specs=[whole()] * 2,
        scratch_shapes=[
            pltpu.VMEM((seqs, channels, width), BF16),
            pltpu.SemaphoreType.DMA((seqs,)),
        ],
        compiler_params=params(50),
        name="outward",
    )(gated, columns)
    swap = [(e, e + 1 - 2 * (e % 2)) for e in range(owners)]
    sums = keep + lax.ppermute(send, "exp", swap).astype(F32)
    sums = sums.reshape(side, length // owners, features)
    total = sums[0]
    for hop in range(1, side):
        route = [(e, (e + 2 * hop) % owners) for e in range(owners)]
        total = total + lax.ppermute(sums[hop].astype(BF16), "exp", route).astype(F32)
    return total


def shards(
    x_in,
    z_in,
    conv_weight,
    conv_bias,
    x_proj,
    dt_proj,
    dt_bias,
    a_log,
    d_skip,
    out_proj,
    residual,
    expert_ids,
    gate_weights,
    w_gate,
    w_up,
    w_down,
):
    owners = lax.axis_size("exp")
    tok_rows = residual.shape[0]
    mixed = mixer(
        x_in, z_in, conv_weight, conv_bias, x_proj, dt_proj, dt_bias, a_log, d_skip, out_proj
    )
    hidden = residual.astype(jnp.float32) + mixed
    normed = (hidden * lax.rsqrt(jnp.mean(hidden * hidden, axis=-1, keepdims=True) + 1e-06)).astype(
        jnp.bfloat16
    )
    capacity = max(2, tok_rows // 4)
    slots = owners * capacity
    chosen_count = expert_ids.shape[1]
    flat_ids = expert_ids.reshape(-1)
    hits = (flat_ids[:, None] == jnp.arange(owners, dtype=jnp.int32)[None, :]).astype(jnp.int32)
    before = jnp.cumsum(hits, axis=0) - hits
    ranked = jnp.sum(before * hits, axis=1)
    valid = jnp.sum(hits, axis=1)
    target = flat_ids * capacity + ranked
    placed = (
        (target[:, None] == jnp.arange(slots, dtype=jnp.int32)[None, :]) & (valid[:, None] > 0)
    ).astype(jnp.float32)
    dispatch_table = jnp.sum(placed.reshape(tok_rows, chosen_count, slots), axis=1)
    combine_table = jnp.sum(
        (placed * gate_weights.reshape(-1)[:, None]).reshape(tok_rows, chosen_count, slots), axis=1
    )
    outgoing = jnp.einsum(
        "ts,td->sd", dispatch_table.astype(jnp.bfloat16), normed, preferred_element_type=jnp.float32
    )
    outgoing = outgoing.astype(jnp.bfloat16).reshape(owners, capacity, -1)
    arrived = lax.all_to_all(outgoing, "exp", split_axis=0, concat_axis=0, tiled=True)
    summed = experts_on_grid(arrived.reshape(slots, -1), w_gate[0], w_up[0], w_down[0])
    expert_out = summed.reshape(owners, capacity, -1)
    returned_rows = lax.all_to_all(
        expert_out, "exp", split_axis=0, concat_axis=0, tiled=True
    ).reshape(slots, -1)
    combined = jnp.dot(
        combine_table, returned_rows.astype(jnp.float32), precision=lax.Precision.HIGHEST
    )
    return hidden + combined


def solution(mesh):
    placed = (
        P("seq", "exp"),
        P("seq", "exp"),
        P(None, "exp"),
        P("exp"),
        P("exp", None),
        P(None, "exp"),
        P("exp"),
        P("exp", None),
        P("exp"),
        P("exp", "seq"),
        P(("seq", "exp"), None),
        P(("seq", "exp"), None),
        P(("seq", "exp"), None),
        P("exp", None, "seq"),
        P("exp", None, "seq"),
        P("exp", "seq", None),
    )
    return jax.shard_map(
        shards, mesh=mesh, in_specs=placed, out_specs=P(("seq", "exp"), None), check_vma=False
    )
```

```python
import functools
import math

import jax
import jax.numpy as jnp
from jax import lax
from jax.experimental import pallas as pl
from jax.experimental.pallas import tpu as pltpu
from jax.sharding import PartitionSpec as P

RANK = 256
STATE = 16
CONV = 4
SEG = 8
LANES = 128
LOG2E = math.log2(math.e)
F32 = jnp.float32
BF16 = jnp.bfloat16
MIB = 1024 * 1024


def whole():
    return pl.BlockSpec(memory_space=pltpu.VMEM)


def far():
    return pl.BlockSpec(memory_space=pltpu.HBM)


def params(mib):
    return pltpu.CompilerParams(vmem_limit_bytes=mib * MIB)


def lines(stage):
    side = math.isqrt(lax.axis_size("seq"))
    owners = lax.axis_size("exp")
    groups = []
    for owner in range(owners):
        along_x = (owner % 2 == 0) == (stage == 0)
        for fixed in range(side):
            members = [(m * side + fixed if along_x else fixed * side + m) for m in range(side)]
            groups.append([m * owners + owner for m in members])
    return groups


def along(block, stage, distance):
    route = []
    for members in lines(stage):
        count = len(members)
        route += [(members[i], members[(i + distance) % count]) for i in range(count)]
    return lax.ppermute(block, ("seq", "exp"), route)


def passed_along(block, axis, distance):
    devices = range(lax.axis_size(axis))
    route = [(i - distance, i) for i in devices if i - distance in devices]
    return lax.ppermute(block, axis, route)


def conv_kernel(
    order_ref,
    x_hbm,
    weight_hbm,
    bias_hbm,
    proj_hbm,
    rim_ref,
    mixed_ref,
    send_ref,
    keep_ref,
    x_ref,
    weight_ref,
    bias_ref,
    proj_ref,
    padded,
    part_ref,
    sems,
):
    sources = (x_hbm, weight_hbm, bias_hbm, proj_hbm)
    targets = (x_ref, weight_ref, bias_ref, proj_ref)
    copies = [pltpu.make_async_copy(*pair, sems.at[k]) for k, pair in enumerate(zip(sources, targets))]
    for copy in copies:
        copy.start()
    length, channels = x_ref.shape
    steps = length // SEG
    head = 8
    for copy in copies[:3]:
        copy.wait()
    for lane in range(0, channels, LANES):
        block = padded.at[lane // LANES]
        block[head - (CONV - 1) : head, :] = rim_ref[:, lane : lane + LANES].astype(F32)
        block[head:, :] = x_ref[:, lane : lane + LANES].astype(F32)

    def step(i, carry):
        rows = pl.ds(pl.multiple_of(i * SEG, SEG), SEG)
        for lane in range(0, channels, LANES):
            lanes = pl.ds(lane, LANES)
            acc = jnp.broadcast_to(bias_ref[:, lanes], (SEG, LANES))
            for tap in range(CONV):
                taken = padded[
                    lane // LANES, pl.ds(i + head - (CONV - 1) + tap, SEG, stride=steps), :
                ]
                acc = acc + weight_ref[tap : tap + 1, lanes] * taken
            mixed_ref[rows, lanes] = (acc * jax.nn.sigmoid(acc)).astype(BF16).astype(F32)
        return carry

    lax.fori_loop(0, steps, step, 0)
    copies[3].wait()
    part_ref[...] = lax.dot_general(
        mixed_ref[...].astype(BF16),
        proj_ref[...],
        (((1,), (1,)), ((), ())),
        preferred_element_type=F32,
    )
    half = SEG // 2
    for place in range(SEG):
        rows = pl.ds(pl.multiple_of(order_ref[place] * steps, steps), steps)
        target = send_ref if place < half else keep_ref
        first = place % half * steps
        target[first : first + steps, :] = part_ref[rows, :]


def spread(target, packed_ref, first):
    packed = packed_ref[...].astype(F32)
    coef = packed[:, RANK : RANK + 2 * STATE] + packed[:, RANK + 2 * STATE :]
    for n in range(STATE):
        target[n] = jnp.broadcast_to(coef[:, first + n : first + n + 1], (coef.shape[0], LANES))


def scan_kernel(
    order_ref,
    near_ref,
    other_ref,
    mixed_ref,
    rates_ref,
    proj_hbm,
    bias_hbm,
    packed_ref,
    y_ref,
    delta_ref,
    msg_ref,
    before_hbm,
    enter_hbm,
    b_wide,
    c_wide,
    proj_ref,
    bias_ref,
    before_ref,
    enter_ref,
    in_sems,
    out_sems,
):
    length, channels = mixed_ref.shape
    steps = length // SEG
    copies = [
        pltpu.make_async_copy(proj_hbm, proj_ref, in_sems.at[0]),
        pltpu.make_async_copy(bias_hbm, bias_ref, in_sems.at[1]),
    ]
    for copy in copies:
        copy.start()
    half = SEG // 2
    for place in range(half):
        taken = slice(place * steps, (place + 1) * steps)
        for source, slot in ((near_ref, place), (other_ref, place + half)):
            rows = pl.ds(pl.multiple_of(order_ref[slot] * steps, steps), steps)
            packed_ref[rows, :] = source[taken, :]
    spread(b_wide, packed_ref, 0)
    spread(c_wide, packed_ref, STATE)
    for copy in copies:
        copy.wait()
    copies = []
    raw = jnp.dot(packed_ref[:, :RANK], proj_ref[...], preferred_element_type=F32) + bias_ref[...]
    delta_ref[...] = jnp.maximum(raw, 0.0) + jnp.log1p(jnp.exp(-jnp.abs(raw)))
    row = lax.broadcasted_iota(jnp.int32, (SEG, LANES), 0)

    def shifted(value, by, fill):
        return jnp.where(row < by, fill, pltpu.roll(value, by, axis=0))

    for lane in range(0, channels, LANES):
        lanes = pl.ds(lane, LANES)
        rates = [
            jnp.broadcast_to(rates_ref[n : n + 1, lanes], (SEG, LANES)) for n in range(STATE)
        ]

        def step(i, carry):
            elapsed, states = carry
            rows = pl.ds(pl.multiple_of(i * SEG, SEG), SEG)
            delta = delta_ref[rows, lanes]
            drive = delta * mixed_ref[rows, lanes]
            fresh, terms = [], []
            for n in range(STATE):
                state = jnp.exp2(delta * rates[n]) * states[n] + drive * b_wide[n, rows, :]
                fresh.append(state)
                terms.append(state * c_wide[n, rows, :])
            while len(terms) > 1:
                terms = [a + b for a, b in zip(terms[::2], terms[1::2])]
            y_ref[rows, lanes] = terms[0]
            return elapsed + delta, tuple(fresh)

        zero = jnp.zeros((SEG, LANES), F32)
        elapsed, states = lax.fori_loop(0, steps, step, (zero, (zero,) * STATE), unroll=2)
        total = elapsed
        for by in (1, 2, 4):
            total = total + shifted(total, by, 0.0)
        before_ref[:, lanes] = shifted(total, 1, 0.0)
        last = total[SEG - 1 : SEG, :]
        for n in range(STATE):
            decay = jnp.exp2(elapsed * rates[n])
            state = states[n]
            for by in (1, 2, 4):
                state = decay * shifted(state, by, 0.0) + state
                decay = decay * shifted(decay, by, 1.0)
            enter_ref[n, :, lanes] = shifted(state, 1, 0.0)
            msg_ref[n : n + 1, lanes] = state[SEG - 1 : SEG, :]
        msg_ref[STATE : STATE + 1, lanes] = last
        block = lane // LANES
        fresh = [
            pltpu.make_async_copy(
                before_ref.at[:, lanes], before_hbm.at[:, lanes], out_sems.at[0, block]
            ),
            pltpu.make_async_copy(
                enter_ref.at[:, :, lanes], enter_hbm.at[:, :, lanes], out_sems.at[1, block]
            ),
        ]
        for copy in fresh:
            copy.start()
        copies += fresh
    for copy in copies:
        copy.wait()


def meet_kernel(before_ref, own_ref, got_ref, prefix_ref, rates_ref, total_ref, next_ref):
    partner_first = before_ref[0] > 0
    rates = rates_ref[...]
    own, got = own_ref[:STATE, :], got_ref[:STATE, :]
    own_delta, got_delta = own_ref[STATE : STATE + 1, :], got_ref[STATE : STATE + 1, :]
    prefix, prefix_delta = prefix_ref[:STATE, :], prefix_ref[STATE : STATE + 1, :]
    late_delta = jnp.where(partner_first, own_delta, got_delta)
    early = jnp.where(partner_first, got, own)
    late = jnp.where(partner_first, own, got)
    total_ref[:STATE, :] = jnp.exp2(late_delta * rates) * early + late
    total_ref[STATE : STATE + 1, :] = own_delta + got_delta
    joined = jnp.exp2(prefix_delta * rates) * got + prefix
    next_ref[:STATE, :] = jnp.where(partner_first, joined, prefix)
    next_ref[STATE : STATE + 1, :] = jnp.where(partner_first, prefix_delta + got_delta, prefix_delta)


def entering_state(message, rates):
    seqs = lax.axis_size("seq")
    side = math.isqrt(seqs)
    place = lax.axis_index("seq").astype(jnp.int32)
    shape = jax.ShapeDtypeStruct(message.shape, F32)
    prefix = jnp.zeros(message.shape, F32)

    def flipped(index, axis, far_step):
        x, y = index // side, index % side
        value = x if axis == "x" else y
        value = side - 1 - value if far_step else value + 1 - 2 * (value % 2)
        return value * side + y if axis == "x" else x * side + value

    for axis in ("y", "x"):
        for far_step in (False, True):
            route = [(i, flipped(i, axis, far_step)) for i in range(seqs)]
            got = lax.ppermute(message, "seq", route)
            before = (flipped(place, axis, far_step) < place).astype(jnp.int32).reshape(1)
            message, prefix = pl.pallas_call(
                meet_kernel,
                out_shape=(shape, shape),
                in_specs=[pl.BlockSpec(memory_space=pltpu.SMEM)] + [whole()] * 4,
                out_specs=[whole()] * 2,
                compiler_params=params(4),
                name="meet",
            )(before, message, got, prefix, rates)
    return prefix


def finish_kernel(
    order_ref,
    entering_ref,
    rates_ref,
    delta_ref,
    packed_ref,
    y_ref,
    mixed_ref,
    before_hbm,
    enter_hbm,
    skip_hbm,
    z_hbm,
    gated_ref,
    before_ref,
    enter_ref,
    skip_ref,
    z_ref,
    c_wide,
    z_wide,
    gated,
    sems,
):
    length, channels = mixed_ref.shape
    steps = length // SEG
    sources = (before_hbm, enter_hbm, skip_hbm, z_hbm)
    targets = (before_ref, enter_ref, skip_ref, z_ref)
    copies = [pltpu.make_async_copy(*pair, sems.at[k]) for k, pair in enumerate(zip(sources, targets))]
    for copy in copies:
        copy.start()
    spread(c_wide, packed_ref, STATE)
    for copy in copies:
        copy.wait()
    for lane in range(0, channels, LANES):
        z_wide[lane // LANES] = z_ref[:, lane : lane + LANES].astype(F32)

    for lane in range(0, channels, LANES):
        lanes = pl.ds(lane, LANES)
        rates = [
            jnp.broadcast_to(rates_ref[n : n + 1, lanes], (SEG, LANES)) for n in range(STATE)
        ]
        before = before_ref[:, lanes]
        held = [
            jnp.exp2(before * rates[n]) * entering_ref[n : n + 1, lanes] + enter_ref[n, :, lanes]
            for n in range(STATE)
        ]
        skip = skip_ref[:, lanes]

        def step(i, elapsed):
            rows = pl.ds(pl.multiple_of(i * SEG, SEG), SEG)
            apart = pl.ds(i, SEG, stride=steps)
            elapsed = elapsed + delta_ref[rows, lanes]
            terms = [
                jnp.exp2(elapsed * rates[n]) * held[n] * c_wide[n, rows, :] for n in range(STATE)
            ]
            while len(terms) > 1:
                terms = [a + b for a, b in zip(terms[::2], terms[1::2])]
            output = y_ref[rows, lanes] + terms[0] + skip * mixed_ref[rows, lanes]
            z = z_wide[lane // LANES, apart, :]
            gated[lane // LANES, apart, :] = output * (z * jax.nn.sigmoid(z))
            return elapsed

        lax.fori_loop(0, steps, step, jnp.zeros((SEG, LANES), F32), unroll=2)
    for place in range(SEG):
        rows = pl.ds(pl.multiple_of(order_ref[place] * steps, steps), steps)
        for lane in range(0, channels, LANES):
            gated_ref[place * steps : (place + 1) * steps, lane : lane + LANES] = gated[
                lane // LANES, rows, :
            ].astype(BF16)


def outward_kernel(order_ref, gated_ref, proj_hbm, send_ref, keep_ref, proj, arrived):
    parts, _, width = proj_hbm.shape
    middle = send_ref.shape[0]
    for part in range(parts):
        pltpu.make_async_copy(proj_hbm.at[part], proj.at[part], arrived.at[part]).start()

    def product(part, carry):
        pltpu.make_async_copy(proj_hbm.at[part], proj.at[part], arrived.at[part]).wait()
        columns = pl.ds(pl.multiple_of(order_ref[part] * width, width), width)
        terms = jnp.dot(gated_ref[...], proj[part], preferred_element_type=F32)
        send_ref[:, columns] = terms[:middle].astype(BF16)
        keep_ref[:, columns] = terms[middle:]
        return carry

    lax.fori_loop(0, parts, product, 0)


def expert_kernel(rows_ref, gate_ref, up_ref, down_ref, first_ref, second_ref, inner):
    tile = 256
    middle = first_ref.shape[0]

    def widen(part, carry):
        columns = pl.ds(pl.multiple_of(part * tile, tile), tile)
        gate = jnp.dot(rows_ref[...], gate_ref[:, columns], preferred_element_type=F32)
        upper = jnp.dot(rows_ref[...], up_ref[:, columns], preferred_element_type=F32)
        inner[:, columns] = (gate * jax.nn.sigmoid(gate) * upper).astype(BF16)
        return carry

    lax.fori_loop(0, inner.shape[1] // tile, widen, 0)

    def narrow(part, carry):
        columns = pl.ds(pl.multiple_of(part * tile, tile), tile)
        piece = jnp.dot(inner[...], down_ref[:, columns], preferred_element_type=F32)
        first_ref[:, columns] = piece[:middle].astype(BF16)
        second_ref[:, columns] = piece[middle:].astype(BF16)
        return carry

    lax.fori_loop(0, first_ref.shape[1] // tile, narrow, 0)


def expert(rows, gate, up, down):
    count, features = rows.shape
    hidden = gate.shape[1]
    return pl.pallas_call(
        expert_kernel,
        out_shape=(jax.ShapeDtypeStruct((count // 2, features), BF16),) * 2,
        in_specs=[whole()] * 4,
        out_specs=[whole()] * 2,
        scratch_shapes=[pltpu.VMEM((count, hidden), BF16)],
        compiler_params=params(12),
        cost_estimate=pl.CostEstimate(
            flops=6 * count * features * hidden,
            bytes_accessed=4 * count * features,
            transcendentals=count * hidden,
        ),
        name="expert",
    )(rows, gate, up, down)


def halves(block):
    middle = block.shape[0] // 2
    return block[:middle], block[middle:]


def added(*blocks):
    total = blocks[0].astype(F32)
    for block in blocks[1:]:
        total = total + block.astype(F32)
    return total.astype(BF16)


def experts_on_grid(rows, gate, up, down):
    run = functools.partial(expert, gate=gate, up=up, down=down)
    behind = along(rows, 0, 1)
    ahead = along(rows, 0, -1)
    across = along(rows, 0, 2)
    own = jnp.concatenate([rows, behind, ahead, across], axis=0)
    behind = along(own, 1, 1)
    ahead = along(own, 1, -1)
    own_out = run(own)
    behind, ahead, own_out = lax.optimization_barrier((behind, ahead, own_out))
    far_first = along(halves(behind)[0], 1, 1)
    far_second = along(halves(ahead)[1], 1, -1)
    behind_first, behind_second = run(behind)
    early_first = along(behind_first, 1, -1)
    far_first, far_second, behind_second = lax.optimization_barrier(
        (far_first, far_second, behind_second)
    )
    across_first, across_second = run(jnp.concatenate([far_first, far_second], axis=0))
    across_first, across_second, early_first = lax.optimization_barrier(
        (across_first, across_second, early_first)
    )
    from_behind = along(across_first, 1, 1)
    from_ahead = along(across_second, 1, -1)
    ahead_first, ahead_second = run(ahead)
    early_second = along(ahead_second, 1, 1)
    from_behind, from_ahead, ahead_first = lax.optimization_barrier(
        (from_behind, from_ahead, ahead_first)
    )
    late_first = along(added(ahead_first, from_behind), 1, 1)
    late_second = along(added(behind_second, from_ahead), 1, -1)
    first = added(own_out[0], early_first, late_first)
    second = added(own_out[1], early_second, late_second)
    (kept, behind), (ahead, across) = halves(first), halves(second)
    return added(kept, along(behind, 0, -1), along(ahead, 0, 1), along(across, 0, 2))


def mixer(x_in, z_in, conv_weight, conv_bias, x_proj, dt_proj, dt_bias, a_log, d_skip, out_proj):
    length, channels = x_in.shape
    steps = length // SEG
    owners = lax.axis_size("exp")
    seqs = lax.axis_size("seq")
    side = owners // 2
    owner = lax.axis_index("exp").astype(jnp.int32)
    place = lax.axis_index("seq").astype(jnp.int32)
    chip, core = owner // 2, owner % 2
    swap = [(e, e + 1 - 2 * (e % 2)) for e in range(owners)]

    def along_z(block, hop):
        return lax.ppermute(block, "exp", [(e, (e + 2 * hop) % owners) for e in range(owners)])

    hops = jnp.arange(side, dtype=jnp.int32)
    onward, back = (chip + hops) % side, (chip - hops) % side
    order = jnp.concatenate([onward * 2 + 1 - core, onward * 2 + core])
    arrival = jnp.concatenate([back * 2 + core, back * 2 + 1 - core])

    rates = (-jnp.exp(a_log) * LOG2E).T
    rim = passed_along(x_in[length - (CONV - 1) :], "seq", 1)
    block = out_proj[None]
    own_line = jnp.concatenate([block] + [along(block, 0, d) for d in (1, -1, 2)], axis=0)
    columns = lax.all_gather(
        own_line, ("seq", "exp"), axis_index_groups=lines(1), axis=0, tiled=True
    )
    grid_x, grid_y = place // side, place % side
    shift = jnp.array([0, -1, 1, 2], dtype=jnp.int32)
    fixed = jnp.arange(side, dtype=jnp.int32)[:, None]
    by_x = ((grid_x + shift) % side)[None, :] * side + fixed
    by_y = fixed * side + ((grid_y + shift) % side)[None, :]
    column_order = jnp.where(core == 0, by_x, by_y).reshape(-1)

    mixed, send, keep = pl.pallas_call(
        conv_kernel,
        out_shape=(
            jax.ShapeDtypeStruct((length, channels), F32),
            jax.ShapeDtypeStruct((length // 2, RANK + 2 * STATE), F32),
            jax.ShapeDtypeStruct((length // 2, RANK + 2 * STATE), F32),
        ),
        in_specs=[pl.BlockSpec(memory_space=pltpu.SMEM)] + [far()] * 4 + [whole()],
        out_specs=[whole()] * 3,
        scratch_shapes=[
            pltpu.VMEM(x_in.shape, BF16),
            pltpu.VMEM(conv_weight.shape, F32),
            pltpu.VMEM((1, channels), F32),
            pltpu.VMEM(x_proj.shape[::-1], BF16),
            pltpu.VMEM((channels // LANES, length + 8, LANES), F32),
            pltpu.VMEM((length, RANK + 2 * STATE), F32),
            pltpu.SemaphoreType.DMA((4,)),
        ],
        compiler_params=params(12),
        name="conv",
    )(order, x_in, conv_weight, conv_bias[None, :], x_proj.T, rim)
    sums = (keep + lax.ppermute(send, "exp", swap)).reshape(side, length // owners, -1)
    summed = sums[0]
    for hop in range(1, side):
        summed = summed + along_z(sums[hop], hop)
    coef = summed[:, RANK:]
    coef_high = coef.astype(BF16)
    coef_low = (coef - coef_high.astype(F32)).astype(BF16)
    near = jnp.concatenate([summed[:, :RANK].astype(BF16), coef_high, coef_low], axis=1)
    near = jnp.concatenate([near] + [along_z(near, hop) for hop in range(1, side)], axis=0)
    other = lax.ppermute(near, "exp", swap)
    packed, y_local, delta, message, before, enter = pl.pallas_call(
        scan_kernel,
        out_shape=(
            jax.ShapeDtypeStruct((length, RANK + 4 * STATE), BF16),
            jax.ShapeDtypeStruct((length, channels), F32),
            jax.ShapeDtypeStruct((length, channels), F32),
            jax.ShapeDtypeStruct((STATE + 1, channels), F32),
            jax.ShapeDtypeStruct((SEG, channels), F32),
            jax.ShapeDtypeStruct((STATE, SEG, channels), F32),
        ),
        in_specs=[pl.BlockSpec(memory_space=pltpu.SMEM)] + [whole()] * 4 + [far()] * 2,
        out_specs=[whole()] * 4 + [far()] * 2,
        scratch_shapes=[
            pltpu.VMEM((STATE, length, LANES), F32),
            pltpu.VMEM((STATE, length, LANES), F32),
            pltpu.VMEM(dt_proj.shape, BF16),
            pltpu.VMEM((1, channels), F32),
            pltpu.VMEM((SEG, channels), F32),
            pltpu.VMEM((STATE, SEG, channels), F32),
            pltpu.SemaphoreType.DMA((2,)),
            pltpu.SemaphoreType.DMA((2, channels // LANES)),
        ],
        compiler_params=params(14),
        name="scan",
    )(arrival, near, other, mixed, rates, dt_proj, dt_bias[None, :])
    entering = entering_state(message, rates)
    gated = pl.pallas_call(
        finish_kernel,
        out_shape=jax.ShapeDtypeStruct((length, channels), BF16),
        in_specs=[pl.BlockSpec(memory_space=pltpu.SMEM)] + [whole()] * 6 + [far()] * 4,
        out_specs=whole(),
        scratch_shapes=[
            pltpu.VMEM((SEG, channels), F32),
            pltpu.VMEM((STATE, SEG, channels), F32),
            pltpu.VMEM((1, channels), F32),
            pltpu.VMEM((length, channels), BF16),
            pltpu.VMEM((STATE, length, LANES), F32),
            pltpu.VMEM((channels // LANES, length, LANES), F32),
            pltpu.VMEM((channels // LANES, length, LANES), F32),
            pltpu.SemaphoreType.DMA((4,)),
        ],
        compiler_params=params(14),
        name="finish",
    )(
        order,
        entering,
        rates,
        delta,
        packed,
        y_local,
        mixed,
        before,
        enter,
        d_skip[None, :],
        z_in,
    )
    width = out_proj.shape[1]
    features = seqs * width
    send, keep = pl.pallas_call(
        outward_kernel,
        out_shape=(
            jax.ShapeDtypeStruct((length // 2, features), BF16),
            jax.ShapeDtypeStruct((length // 2, features), F32),
        ),
        in_specs=[pl.BlockSpec(memory_space=pltpu.SMEM), whole(), far()],
        out_specs=[whole()] * 2,
        scratch_shapes=[
            pltpu.VMEM((seqs, channels, width), BF16),
            pltpu.SemaphoreType.DMA((seqs,)),
        ],
        compiler_params=params(50),
        name="outward",
    )(column_order, gated, columns)
    sums = keep + lax.ppermute(send, "exp", swap).astype(F32)
    sums = sums.reshape(side, length // owners, features)
    total = sums[0]
    for hop in range(1, side):
        total = total + along_z(sums[hop].astype(BF16), hop).astype(F32)
    return total


def shards(
    x_in,
    z_in,
    conv_weight,
    conv_bias,
    x_proj,
    dt_proj,
    dt_bias,
    a_log,
    d_skip,
    out_proj,
    residual,
    expert_ids,
    gate_weights,
    w_gate,
    w_up,
    w_down,
):
    owners = lax.axis_size("exp")
    tok_rows = residual.shape[0]
    mixed = mixer(
        x_in, z_in, conv_weight, conv_bias, x_proj, dt_proj, dt_bias, a_log, d_skip, out_proj
    )
    hidden = residual.astype(jnp.float32) + mixed
    normed = (hidden * lax.rsqrt(jnp.mean(hidden * hidden, axis=-1, keepdims=True) + 1e-06)).astype(
        jnp.bfloat16
    )
    capacity = max(2, tok_rows // 4)
    slots = owners * capacity
    chosen_count = expert_ids.shape[1]
    flat_ids = expert_ids.reshape(-1)
    hits = (flat_ids[:, None] == jnp.arange(owners, dtype=jnp.int32)[None, :]).astype(jnp.int32)
    before = jnp.cumsum(hits, axis=0) - hits
    ranked = jnp.sum(before * hits, axis=1)
    valid = jnp.sum(hits, axis=1)
    target = flat_ids * capacity + ranked
    placed = (
        (target[:, None] == jnp.arange(slots, dtype=jnp.int32)[None, :]) & (valid[:, None] > 0)
    ).astype(jnp.float32)
    dispatch_table = jnp.sum(placed.reshape(tok_rows, chosen_count, slots), axis=1)
    combine_table = jnp.sum(
        (placed * gate_weights.reshape(-1)[:, None]).reshape(tok_rows, chosen_count, slots), axis=1
    )
    outgoing = jnp.einsum(
        "ts,td->sd", dispatch_table.astype(jnp.bfloat16), normed, preferred_element_type=jnp.float32
    )
    outgoing = outgoing.astype(jnp.bfloat16).reshape(owners, capacity, -1)
    arrived = lax.all_to_all(outgoing, "exp", split_axis=0, concat_axis=0, tiled=True)
    summed = experts_on_grid(arrived.reshape(slots, -1), w_gate[0], w_up[0], w_down[0])
    expert_out = summed.reshape(owners, capacity, -1)
    returned_rows = lax.all_to_all(
        expert_out, "exp", split_axis=0, concat_axis=0, tiled=True
    ).reshape(slots, -1)
    combined = jnp.dot(
        combine_table, returned_rows.astype(jnp.float32), precision=lax.Precision.HIGHEST
    )
    return hidden + combined


def solution(mesh):
    placed = (
        P("seq", "exp"),
        P("seq", "exp"),
        P(None, "exp"),
        P("exp"),
        P("exp", None),
        P(None, "exp"),
        P("exp"),
        P("exp", None),
        P("exp"),
        P("exp", "seq"),
        P(("seq", "exp"), None),
        P(("seq", "exp"), None),
        P(("seq", "exp"), None),
        P("exp", None, "seq"),
        P("exp", None, "seq"),
        P("exp", "seq", None),
    )
    return jax.shard_map(
        shards, mesh=mesh, in_specs=placed, out_specs=P(("seq", "exp"), None), check_vma=False
    )
```

```python
import functools
import math

import jax
import jax.numpy as jnp
from jax import lax
from jax.experimental import pallas as pl
from jax.experimental.pallas import tpu as pltpu
from jax.sharding import PartitionSpec as P

RANK = 256
STATE = 16
CONV = 4
SEG = 8
LANES = 128
LOG2E = math.log2(math.e)
F32 = jnp.float32
BF16 = jnp.bfloat16
MIB = 1024 * 1024


def whole():
    return pl.BlockSpec(memory_space=pltpu.VMEM)


def far():
    return pl.BlockSpec(memory_space=pltpu.HBM)


def params(mib):
    return pltpu.CompilerParams(vmem_limit_bytes=mib * MIB)


def lines(stage):
    side = math.isqrt(lax.axis_size("seq"))
    owners = lax.axis_size("exp")
    groups = []
    for owner in range(owners):
        along_x = (owner % 2 == 0) == (stage == 0)
        for fixed in range(side):
            members = [(m * side + fixed if along_x else fixed * side + m) for m in range(side)]
            groups.append([m * owners + owner for m in members])
    return groups


def along(block, stage, distance):
    route = []
    for members in lines(stage):
        count = len(members)
        route += [(members[i], members[(i + distance) % count]) for i in range(count)]
    return lax.ppermute(block, ("seq", "exp"), route)


def passed_along(block, axis, distance):
    devices = range(lax.axis_size(axis))
    route = [(i - distance, i) for i in devices if i - distance in devices]
    return lax.ppermute(block, axis, route)


def conv_kernel(
    order_ref,
    x_hbm,
    weight_hbm,
    bias_hbm,
    proj_hbm,
    rim_ref,
    mixed_ref,
    send_ref,
    keep_ref,
    x_ref,
    weight_ref,
    bias_ref,
    proj_ref,
    padded,
    part_ref,
    sems,
):
    sources = (x_hbm, weight_hbm, bias_hbm, proj_hbm)
    targets = (x_ref, weight_ref, bias_ref, proj_ref)
    copies = [pltpu.make_async_copy(*pair, sems.at[k]) for k, pair in enumerate(zip(sources, targets))]
    for copy in copies:
        copy.start()
    length, channels = x_ref.shape
    steps = length // SEG
    head = 8
    for copy in copies[:3]:
        copy.wait()
    for lane in range(0, channels, LANES):
        block = padded.at[lane // LANES]
        block[head - (CONV - 1) : head, :] = rim_ref[:, lane : lane + LANES].astype(F32)
        block[head:, :] = x_ref[:, lane : lane + LANES].astype(F32)

    def step(i, carry):
        rows = pl.ds(pl.multiple_of(i * SEG, SEG), SEG)
        for lane in range(0, channels, LANES):
            lanes = pl.ds(lane, LANES)
            acc = jnp.broadcast_to(bias_ref[:, lanes], (SEG, LANES))
            for tap in range(CONV):
                taken = padded[
                    lane // LANES, pl.ds(i + head - (CONV - 1) + tap, SEG, stride=steps), :
                ]
                acc = acc + weight_ref[tap : tap + 1, lanes] * taken
            mixed_ref[rows, lanes] = (acc * jax.nn.sigmoid(acc)).astype(BF16).astype(F32)
        return carry

    lax.fori_loop(0, steps, step, 0)
    copies[3].wait()
    part_ref[...] = lax.dot_general(
        mixed_ref[...].astype(BF16),
        proj_ref[...],
        (((1,), (1,)), ((), ())),
        preferred_element_type=F32,
    )
    half = SEG // 2
    for place in range(SEG):
        rows = pl.ds(pl.multiple_of(order_ref[place] * steps, steps), steps)
        target = send_ref if place < half else keep_ref
        first = place % half * steps
        target[first : first + steps, :] = part_ref[rows, :]


def spread(target, packed_ref, first):
    packed = packed_ref[...].astype(F32)
    coef = packed[:, RANK : RANK + 2 * STATE] + packed[:, RANK + 2 * STATE :]
    for n in range(STATE):
        target[n] = jnp.broadcast_to(coef[:, first + n : first + n + 1], (coef.shape[0], LANES))


def scan_kernel(
    order_ref,
    near_ref,
    other_ref,
    mixed_ref,
    rates_ref,
    proj_hbm,
    bias_hbm,
    packed_ref,
    msg_ref,
    y_hbm,
    delta_hbm,
    before_hbm,
    enter_hbm,
    b_wide,
    c_wide,
    proj_ref,
    bias_ref,
    y_ref,
    delta_ref,
    before_ref,
    enter_ref,
    in_sems,
    out_sems,
):
    length, channels = mixed_ref.shape
    steps = length // SEG
    copies = [
        pltpu.make_async_copy(proj_hbm, proj_ref, in_sems.at[0]),
        pltpu.make_async_copy(bias_hbm, bias_ref, in_sems.at[1]),
    ]
    for copy in copies:
        copy.start()
    half = SEG // 2
    for place in range(half):
        taken = slice(place * steps, (place + 1) * steps)
        for source, slot in ((near_ref, place), (other_ref, place + half)):
            rows = pl.ds(pl.multiple_of(order_ref[slot] * steps, steps), steps)
            packed_ref[rows, :] = source[taken, :]
    spread(b_wide, packed_ref, 0)
    spread(c_wide, packed_ref, STATE)
    for copy in copies:
        copy.wait()
    copies = []
    raw = jnp.dot(packed_ref[:, :RANK], proj_ref[...], preferred_element_type=F32) + bias_ref[...]
    delta_ref[...] = jnp.maximum(raw, 0.0) + jnp.log1p(jnp.exp(-jnp.abs(raw)))
    row = lax.broadcasted_iota(jnp.int32, (SEG, LANES), 0)

    def shifted(value, by, fill):
        return jnp.where(row < by, fill, pltpu.roll(value, by, axis=0))

    for lane in range(0, channels, LANES):
        lanes = pl.ds(lane, LANES)
        rates = [
            jnp.broadcast_to(rates_ref[n : n + 1, lanes], (SEG, LANES)) for n in range(STATE)
        ]

        def step(i, carry):
            elapsed, states = carry
            rows = pl.ds(pl.multiple_of(i * SEG, SEG), SEG)
            delta = delta_ref[rows, lanes]
            drive = delta * mixed_ref[rows, lanes]
            fresh, terms = [], []
            for n in range(STATE):
                state = jnp.exp2(delta * rates[n]) * states[n] + drive * b_wide[n, rows, :]
                fresh.append(state)
                terms.append(state * c_wide[n, rows, :])
            while len(terms) > 1:
                terms = [a + b for a, b in zip(terms[::2], terms[1::2])]
            y_ref[rows, lanes] = terms[0]
            return elapsed + delta, tuple(fresh)

        zero = jnp.zeros((SEG, LANES), F32)
        elapsed, states = lax.fori_loop(0, steps, step, (zero, (zero,) * STATE), unroll=2)
        total = elapsed
        for by in (1, 2, 4):
            total = total + shifted(total, by, 0.0)
        before_ref[:, lanes] = shifted(total, 1, 0.0)
        last = total[SEG - 1 : SEG, :]
        for n in range(STATE):
            decay = jnp.exp2(elapsed * rates[n])
            state = states[n]
            for by in (1, 2, 4):
                state = decay * shifted(state, by, 0.0) + state
                decay = decay * shifted(decay, by, 1.0)
            enter_ref[n, :, lanes] = shifted(state, 1, 0.0)
            msg_ref[n : n + 1, lanes] = state[SEG - 1 : SEG, :]
        msg_ref[STATE : STATE + 1, lanes] = last
        block = lane // LANES
        fresh = [
            pltpu.make_async_copy(
                before_ref.at[:, lanes], before_hbm.at[:, lanes], out_sems.at[0, block]
            ),
            pltpu.make_async_copy(
                enter_ref.at[:, :, lanes], enter_hbm.at[:, :, lanes], out_sems.at[1, block]
            ),
            pltpu.make_async_copy(y_ref.at[:, lanes], y_hbm.at[:, lanes], out_sems.at[2, block]),
            pltpu.make_async_copy(
                delta_ref.at[:, lanes], delta_hbm.at[:, lanes], out_sems.at[3, block]
            ),
        ]
        for copy in fresh:
            copy.start()
        copies += fresh
    for copy in copies:
        copy.wait()


def meet_kernel(before_ref, own_ref, got_ref, prefix_ref, rates_ref, total_ref, next_ref):
    partner_first = before_ref[0] > 0
    rates = rates_ref[...]
    own, got = own_ref[:STATE, :], got_ref[:STATE, :]
    own_delta, got_delta = own_ref[STATE : STATE + 1, :], got_ref[STATE : STATE + 1, :]
    prefix, prefix_delta = prefix_ref[:STATE, :], prefix_ref[STATE : STATE + 1, :]
    late_delta = jnp.where(partner_first, own_delta, got_delta)
    early = jnp.where(partner_first, got, own)
    late = jnp.where(partner_first, own, got)
    total_ref[:STATE, :] = jnp.exp2(late_delta * rates) * early + late
    total_ref[STATE : STATE + 1, :] = own_delta + got_delta
    joined = jnp.exp2(prefix_delta * rates) * got + prefix
    next_ref[:STATE, :] = jnp.where(partner_first, joined, prefix)
    next_ref[STATE : STATE + 1, :] = jnp.where(partner_first, prefix_delta + got_delta, prefix_delta)


def entering_state(message, rates):
    seqs = lax.axis_size("seq")
    side = math.isqrt(seqs)
    place = lax.axis_index("seq").astype(jnp.int32)
    shape = jax.ShapeDtypeStruct(message.shape, F32)
    prefix = jnp.zeros(message.shape, F32)

    def flipped(index, axis, far_step):
        x, y = index // side, index % side
        value = x if axis == "x" else y
        value = side - 1 - value if far_step else value + 1 - 2 * (value % 2)
        return value * side + y if axis == "x" else x * side + value

    for axis in ("y", "x"):
        for far_step in (False, True):
            route = [(i, flipped(i, axis, far_step)) for i in range(seqs)]
            got = lax.ppermute(message, "seq", route)
            before = (flipped(place, axis, far_step) < place).astype(jnp.int32).reshape(1)
            message, prefix = pl.pallas_call(
                meet_kernel,
                out_shape=(shape, shape),
                in_specs=[pl.BlockSpec(memory_space=pltpu.SMEM)] + [whole()] * 4,
                out_specs=[whole()] * 2,
                compiler_params=params(4),
                name="meet",
            )(before, message, got, prefix, rates)
    return prefix


def finish_kernel(
    order_ref,
    entering_ref,
    rates_ref,
    packed_ref,
    mixed_ref,
    before_hbm,
    enter_hbm,
    skip_hbm,
    z_hbm,
    y_hbm,
    delta_hbm,
    gated_ref,
    before_ref,
    enter_ref,
    skip_ref,
    z_ref,
    y_ref,
    delta_ref,
    c_wide,
    z_wide,
    gated,
    sems,
    block_sems,
):
    length, channels = mixed_ref.shape
    steps = length // SEG
    sources = (before_hbm, enter_hbm, skip_hbm, z_hbm)
    targets = (before_ref, enter_ref, skip_ref, z_ref)
    copies = [pltpu.make_async_copy(*pair, sems.at[k]) for k, pair in enumerate(zip(sources, targets))]
    for copy in copies:
        copy.start()
    blocks = []
    for lane in range(0, channels, LANES):
        lanes = pl.ds(lane, LANES)
        y_sem, delta_sem = block_sems.at[0, lane // LANES], block_sems.at[1, lane // LANES]
        pair = (
            pltpu.make_async_copy(y_hbm.at[:, lanes], y_ref.at[:, lanes], y_sem),
            pltpu.make_async_copy(delta_hbm.at[:, lanes], delta_ref.at[:, lanes], delta_sem),
        )
        for copy in pair:
            copy.start()
        blocks.append(pair)
    spread(c_wide, packed_ref, STATE)
    for copy in copies:
        copy.wait()
    for lane in range(0, channels, LANES):
        z_wide[lane // LANES] = z_ref[:, lane : lane + LANES].astype(F32)

    for lane in range(0, channels, LANES):
        lanes = pl.ds(lane, LANES)
        rates = [
            jnp.broadcast_to(rates_ref[n : n + 1, lanes], (SEG, LANES)) for n in range(STATE)
        ]
        for copy in blocks[lane // LANES]:
            copy.wait()
        before = before_ref[:, lanes]
        held = [
            jnp.exp2(before * rates[n]) * entering_ref[n : n + 1, lanes] + enter_ref[n, :, lanes]
            for n in range(STATE)
        ]
        skip = skip_ref[:, lanes]

        def step(i, elapsed):
            rows = pl.ds(pl.multiple_of(i * SEG, SEG), SEG)
            apart = pl.ds(i, SEG, stride=steps)
            elapsed = elapsed + delta_ref[rows, lanes]
            terms = [
                jnp.exp2(elapsed * rates[n]) * held[n] * c_wide[n, rows, :] for n in range(STATE)
            ]
            while len(terms) > 1:
                terms = [a + b for a, b in zip(terms[::2], terms[1::2])]
            output = y_ref[rows, lanes] + terms[0] + skip * mixed_ref[rows, lanes]
            z = z_wide[lane // LANES, apart, :]
            gated[lane // LANES, apart, :] = output * (z * jax.nn.sigmoid(z))
            return elapsed

        lax.fori_loop(0, steps, step, jnp.zeros((SEG, LANES), F32), unroll=2)
    for place in range(SEG):
        rows = pl.ds(pl.multiple_of(order_ref[place] * steps, steps), steps)
        for lane in range(0, channels, LANES):
            gated_ref[place * steps : (place + 1) * steps, lane : lane + LANES] = gated[
                lane // LANES, rows, :
            ].astype(BF16)


def outward_kernel(gated_ref, proj_hbm, send_ref, keep_ref, proj, arrived):
    parts, _, width = proj_hbm.shape
    middle = send_ref.shape[0]
    for part in range(parts):
        pltpu.make_async_copy(proj_hbm.at[part], proj.at[part], arrived.at[part]).start()

    def product(part, carry):
        pltpu.make_async_copy(proj_hbm.at[part], proj.at[part], arrived.at[part]).wait()
        columns = pl.ds(pl.multiple_of(part * width, width), width)
        terms = jnp.dot(gated_ref[...], proj[part], preferred_element_type=F32)
        send_ref[:, columns] = terms[:middle].astype(BF16)
        keep_ref[:, columns] = terms[middle:]
        return carry

    lax.fori_loop(0, parts, product, 0)


def expert_kernel(rows_ref, gate_ref, up_ref, down_ref, first_ref, second_ref, inner):
    tile = 256
    middle = first_ref.shape[0]

    def widen(part, carry):
        columns = pl.ds(pl.multiple_of(part * tile, tile), tile)
        gate = jnp.dot(rows_ref[...], gate_ref[:, columns], preferred_element_type=F32)
        upper = jnp.dot(rows_ref[...], up_ref[:, columns], preferred_element_type=F32)
        inner[:, columns] = (gate * jax.nn.sigmoid(gate) * upper).astype(BF16)
        return carry

    lax.fori_loop(0, inner.shape[1] // tile, widen, 0)

    def narrow(part, carry):
        columns = pl.ds(pl.multiple_of(part * tile, tile), tile)
        piece = jnp.dot(inner[...], down_ref[:, columns], preferred_element_type=F32)
        first_ref[:, columns] = piece[:middle].astype(BF16)
        second_ref[:, columns] = piece[middle:].astype(BF16)
        return carry

    lax.fori_loop(0, first_ref.shape[1] // tile, narrow, 0)


def expert(rows, gate, up, down):
    count, features = rows.shape
    hidden = gate.shape[1]
    return pl.pallas_call(
        expert_kernel,
        out_shape=(jax.ShapeDtypeStruct((count // 2, features), BF16),) * 2,
        in_specs=[whole()] * 4,
        out_specs=[whole()] * 2,
        scratch_shapes=[pltpu.VMEM((count, hidden), BF16)],
        compiler_params=params(12),
        cost_estimate=pl.CostEstimate(
            flops=count * features, bytes_accessed=count * features, transcendentals=count
        ),
        name="expert",
    )(rows, gate, up, down)


def halves(block):
    middle = block.shape[0] // 2
    return block[:middle], block[middle:]


def added(*blocks):
    total = blocks[0].astype(F32)
    for block in blocks[1:]:
        total = total + block.astype(F32)
    return total.astype(BF16)


def experts_on_grid(rows, gate, up, down):
    run = functools.partial(expert, gate=gate, up=up, down=down)
    behind = along(rows, 0, 1)
    ahead = along(rows, 0, -1)
    across = along(rows, 0, 2)
    own = jnp.concatenate([rows, behind, ahead, across], axis=0)
    own_first, own_second = halves(own)
    behind_first = along(own_first, 1, 1)
    ahead_second = along(own_second, 1, -1)
    behind_second = along(own_second, 1, 1)
    ahead_first = along(own_first, 1, -1)
    own_out = run(own)
    behind_first, ahead_second, own_out = lax.optimization_barrier(
        (behind_first, ahead_second, own_out)
    )
    far_first = along(behind_first, 1, 1)
    far_second = along(ahead_second, 1, -1)
    behind_out, ahead_out = run(jnp.concatenate([behind_first, ahead_second], axis=0))
    early_first = along(behind_out, 1, -1)
    early_second = along(ahead_out, 1, 1)
    behind_second, ahead_first, behind_out = lax.optimization_barrier(
        (behind_second, ahead_first, behind_out)
    )
    behind_rest, ahead_rest = run(jnp.concatenate([behind_second, ahead_first], axis=0))
    far_first, far_second, behind_rest = lax.optimization_barrier(
        (far_first, far_second, behind_rest)
    )
    across_first, across_second = run(jnp.concatenate([far_first, far_second], axis=0))
    across_first, across_second, early_first, early_second = lax.optimization_barrier(
        (across_first, across_second, early_first, early_second)
    )
    late_first = along(added(ahead_rest, along(across_first, 1, 1)), 1, 1)
    late_second = along(added(behind_rest, along(across_second, 1, -1)), 1, -1)
    first = added(own_out[0], early_first, late_first)
    second = added(own_out[1], early_second, late_second)
    (kept, behind), (ahead, across) = halves(first), halves(second)
    return added(kept, along(behind, 0, -1), along(ahead, 0, 1), along(across, 0, 2))


def mixer(x_in, z_in, conv_weight, conv_bias, x_proj, dt_proj, dt_bias, a_log, d_skip, out_proj):
    length, channels = x_in.shape
    steps = length // SEG
    owners = lax.axis_size("exp")
    seqs = lax.axis_size("seq")
    side = owners // 2
    owner = lax.axis_index("exp").astype(jnp.int32)
    chip, core = owner // 2, owner % 2
    swap = [(e, e + 1 - 2 * (e % 2)) for e in range(owners)]

    def along_z(block, hop):
        return lax.ppermute(block, "exp", [(e, (e + 2 * hop) % owners) for e in range(owners)])

    columns = lax.all_gather(out_proj, "seq", axis=0)
    hops = jnp.arange(side, dtype=jnp.int32)
    onward, back = (chip + hops) % side, (chip - hops) % side
    order = jnp.concatenate([onward * 2 + 1 - core, onward * 2 + core])
    arrival = jnp.concatenate([back * 2 + core, back * 2 + 1 - core])

    rates = (-jnp.exp(a_log) * LOG2E).T
    rim = passed_along(x_in[length - (CONV - 1) :], "seq", 1)
    mixed, send, keep = pl.pallas_call(
        conv_kernel,
        out_shape=(
            jax.ShapeDtypeStruct((length, channels), F32),
            jax.ShapeDtypeStruct((length // 2, RANK + 2 * STATE), F32),
            jax.ShapeDtypeStruct((length // 2, RANK + 2 * STATE), F32),
        ),
        in_specs=[pl.BlockSpec(memory_space=pltpu.SMEM)] + [far()] * 4 + [whole()],
        out_specs=[whole()] * 3,
        scratch_shapes=[
            pltpu.VMEM(x_in.shape, BF16),
            pltpu.VMEM(conv_weight.shape, F32),
            pltpu.VMEM((1, channels), F32),
            pltpu.VMEM(x_proj.shape[::-1], BF16),
            pltpu.VMEM((channels // LANES, length + 8, LANES), F32),
            pltpu.VMEM((length, RANK + 2 * STATE), F32),
            pltpu.SemaphoreType.DMA((4,)),
        ],
        compiler_params=params(12),
        name="conv",
    )(order, x_in, conv_weight, conv_bias[None, :], x_proj.T, rim)
    sums = (keep + lax.ppermute(send, "exp", swap)).reshape(side, length // owners, -1)
    summed = sums[0]
    for hop in range(1, side):
        summed = summed + along_z(sums[hop], hop)
    coef = summed[:, RANK:]
    coef_high = coef.astype(BF16)
    coef_low = (coef - coef_high.astype(F32)).astype(BF16)
    near = jnp.concatenate([summed[:, :RANK].astype(BF16), coef_high, coef_low], axis=1)
    near = jnp.concatenate([near] + [along_z(near, hop) for hop in range(1, side)], axis=0)
    other = lax.ppermute(near, "exp", swap)
    packed, message, y_local, delta, before, enter = pl.pallas_call(
        scan_kernel,
        out_shape=(
            jax.ShapeDtypeStruct((length, RANK + 4 * STATE), BF16),
            jax.ShapeDtypeStruct((STATE + 1, channels), F32),
            jax.ShapeDtypeStruct((length, channels), F32),
            jax.ShapeDtypeStruct((length, channels), F32),
            jax.ShapeDtypeStruct((SEG, channels), F32),
            jax.ShapeDtypeStruct((STATE, SEG, channels), F32),
        ),
        in_specs=[pl.BlockSpec(memory_space=pltpu.SMEM)] + [whole()] * 4 + [far()] * 2,
        out_specs=[whole()] * 2 + [far()] * 4,
        scratch_shapes=[
            pltpu.VMEM((STATE, length, LANES), F32),
            pltpu.VMEM((STATE, length, LANES), F32),
            pltpu.VMEM(dt_proj.shape, BF16),
            pltpu.VMEM((1, channels), F32),
            pltpu.VMEM((length, channels), F32),
            pltpu.VMEM((length, channels), F32),
            pltpu.VMEM((SEG, channels), F32),
            pltpu.VMEM((STATE, SEG, channels), F32),
            pltpu.SemaphoreType.DMA((2,)),
            pltpu.SemaphoreType.DMA((4, channels // LANES)),
        ],
        compiler_params=params(16),
        name="scan",
    )(arrival, near, other, mixed, rates, dt_proj, dt_bias[None, :])
    entering = entering_state(message, rates)
    gated = pl.pallas_call(
        finish_kernel,
        out_shape=jax.ShapeDtypeStruct((length, channels), BF16),
        in_specs=[pl.BlockSpec(memory_space=pltpu.SMEM)] + [whole()] * 4 + [far()] * 6,
        out_specs=whole(),
        scratch_shapes=[
            pltpu.VMEM((SEG, channels), F32),
            pltpu.VMEM((STATE, SEG, channels), F32),
            pltpu.VMEM((1, channels), F32),
            pltpu.VMEM((length, channels), BF16),
            pltpu.VMEM((length, channels), F32),
            pltpu.VMEM((length, channels), F32),
            pltpu.VMEM((STATE, length, LANES), F32),
            pltpu.VMEM((channels // LANES, length, LANES), F32),
            pltpu.VMEM((channels // LANES, length, LANES), F32),
            pltpu.SemaphoreType.DMA((4,)),
            pltpu.SemaphoreType.DMA((2, channels // LANES)),
        ],
        compiler_params=params(18),
        name="finish",
    )(
        order,
        entering,
        rates,
        packed,
        mixed,
        before,
        enter,
        d_skip[None, :],
        z_in,
        y_local,
        delta,
    )
    width = out_proj.shape[1]
    features = seqs * width
    send, keep = pl.pallas_call(
        outward_kernel,
        out_shape=(
            jax.ShapeDtypeStruct((length // 2, features), BF16),
            jax.ShapeDtypeStruct((length // 2, features), F32),
        ),
        in_specs=[whole(), far()],
        out_specs=[whole()] * 2,
        scratch_shapes=[
            pltpu.VMEM((seqs, channels, width), BF16),
            pltpu.SemaphoreType.DMA((seqs,)),
        ],
        compiler_params=params(50),
        name="outward",
    )(gated, columns)
    sums = keep + lax.ppermute(send, "exp", swap).astype(F32)
    sums = sums.reshape(side, length // owners, features)
    total = sums[0]
    for hop in range(1, side):
        total = total + along_z(sums[hop].astype(BF16), hop).astype(F32)
    return total


def shards(
    x_in,
    z_in,
    conv_weight,
    conv_bias,
    x_proj,
    dt_proj,
    dt_bias,
    a_log,
    d_skip,
    out_proj,
    residual,
    expert_ids,
    gate_weights,
    w_gate,
    w_up,
    w_down,
):
    owners = lax.axis_size("exp")
    tok_rows = residual.shape[0]
    mixed = mixer(
        x_in, z_in, conv_weight, conv_bias, x_proj, dt_proj, dt_bias, a_log, d_skip, out_proj
    )
    hidden = residual.astype(jnp.float32) + mixed
    normed = (hidden * lax.rsqrt(jnp.mean(hidden * hidden, axis=-1, keepdims=True) + 1e-06)).astype(
        jnp.bfloat16
    )
    capacity = max(2, tok_rows // 4)
    slots = owners * capacity
    chosen_count = expert_ids.shape[1]
    flat_ids = expert_ids.reshape(-1)
    hits = (flat_ids[:, None] == jnp.arange(owners, dtype=jnp.int32)[None, :]).astype(jnp.int32)
    before = jnp.cumsum(hits, axis=0) - hits
    ranked = jnp.sum(before * hits, axis=1)
    valid = jnp.sum(hits, axis=1)
    target = flat_ids * capacity + ranked
    placed = (
        (target[:, None] == jnp.arange(slots, dtype=jnp.int32)[None, :]) & (valid[:, None] > 0)
    ).astype(jnp.float32)
    dispatch_table = jnp.sum(placed.reshape(tok_rows, chosen_count, slots), axis=1)
    combine_table = jnp.sum(
        (placed * gate_weights.reshape(-1)[:, None]).reshape(tok_rows, chosen_count, slots), axis=1
    )
    outgoing = jnp.einsum(
        "ts,td->sd", dispatch_table.astype(jnp.bfloat16), normed, preferred_element_type=jnp.float32
    )
    outgoing = outgoing.astype(jnp.bfloat16).reshape(owners, capacity, -1)
    arrived = lax.all_to_all(outgoing, "exp", split_axis=0, concat_axis=0, tiled=True)
    summed = experts_on_grid(arrived.reshape(slots, -1), w_gate[0], w_up[0], w_down[0])
    expert_out = summed.reshape(owners, capacity, -1)
    returned_rows = lax.all_to_all(
        expert_out, "exp", split_axis=0, concat_axis=0, tiled=True
    ).reshape(slots, -1)
    combined = jnp.dot(
        combine_table, returned_rows.astype(jnp.float32), precision=lax.Precision.HIGHEST
    )
    return hidden + combined


def solution(mesh):
    placed = (
        P("seq", "exp"),
        P("seq", "exp"),
        P(None, "exp"),
        P("exp"),
        P("exp", None),
        P(None, "exp"),
        P("exp"),
        P("exp", None),
        P("exp"),
        P("exp", "seq"),
        P(("seq", "exp"), None),
        P(("seq", "exp"), None),
        P(("seq", "exp"), None),
        P("exp", None, "seq"),
        P("exp", None, "seq"),
        P("exp", "seq", None),
    )
    return jax.shard_map(
        shards, mesh=mesh, in_specs=placed, out_specs=P(("seq", "exp"), None), check_vma=False
    )
```

```python
import functools
import math

import jax
import jax.numpy as jnp
from jax import lax
from jax.experimental import pallas as pl
from jax.experimental.pallas import tpu as pltpu
from jax.sharding import PartitionSpec as P

RANK = 256
STATE = 16
CONV = 4
SEG = 8
LANES = 128
LOG2E = math.log2(math.e)
F32 = jnp.float32
BF16 = jnp.bfloat16
MIB = 1024 * 1024


def whole():
    return pl.BlockSpec(memory_space=pltpu.VMEM)


def far():
    return pl.BlockSpec(memory_space=pltpu.HBM)


def params(mib):
    return pltpu.CompilerParams(vmem_limit_bytes=mib * MIB)


def lines(stage):
    side = math.isqrt(lax.axis_size("seq"))
    owners = lax.axis_size("exp")
    groups = []
    for owner in range(owners):
        along_x = (owner % 2 == 0) == (stage == 0)
        for fixed in range(side):
            members = [(m * side + fixed if along_x else fixed * side + m) for m in range(side)]
            groups.append([m * owners + owner for m in members])
    return groups


def along(block, stage, distance):
    route = []
    for members in lines(stage):
        count = len(members)
        route += [(members[i], members[(i + distance) % count]) for i in range(count)]
    return lax.ppermute(block, ("seq", "exp"), route)


def passed_along(block, axis, distance):
    devices = range(lax.axis_size(axis))
    route = [(i - distance, i) for i in devices if i - distance in devices]
    return lax.ppermute(block, axis, route)


def conv_kernel(
    order_ref,
    x_hbm,
    proj_hbm,
    weight_ref,
    rim_ref,
    mixed_ref,
    send_ref,
    keep_ref,
    x_ref,
    proj_ref,
    padded,
    part_ref,
    sems,
):
    sources = (x_hbm, proj_hbm)
    targets = (x_ref, proj_ref)
    copies = [pltpu.make_async_copy(*pair, sems.at[k]) for k, pair in enumerate(zip(sources, targets))]
    for copy in copies:
        copy.start()
    length, channels = x_ref.shape
    steps = length // SEG
    head = 8
    copies[0].wait()
    for lane in range(0, channels, LANES):
        block = padded.at[lane // LANES]
        block[head - (CONV - 1) : head, :] = rim_ref[:, lane : lane + LANES].astype(F32)
        block[head:, :] = x_ref[:, lane : lane + LANES].astype(F32)

    def step(i, carry):
        rows = pl.ds(pl.multiple_of(i * SEG, SEG), SEG)
        for lane in range(0, channels, LANES):
            lanes = pl.ds(lane, LANES)
            acc = jnp.broadcast_to(weight_ref[CONV : CONV + 1, lanes], (SEG, LANES))
            for tap in range(CONV):
                taken = padded[
                    lane // LANES, pl.ds(i + head - (CONV - 1) + tap, SEG, stride=steps), :
                ]
                acc = acc + weight_ref[tap : tap + 1, lanes] * taken
            mixed_ref[rows, lanes] = (acc * jax.nn.sigmoid(acc)).astype(BF16).astype(F32)
        return carry

    lax.fori_loop(0, steps, step, 0)
    copies[1].wait()
    part_ref[...] = lax.dot_general(
        mixed_ref[...].astype(BF16),
        proj_ref[...],
        (((1,), (1,)), ((), ())),
        preferred_element_type=F32,
    )
    half = SEG // 2
    for place in range(SEG):
        rows = pl.ds(pl.multiple_of(order_ref[place] * steps, steps), steps)
        target = send_ref if place < half else keep_ref
        first = place % half * steps
        target[first : first + steps, :] = part_ref[rows, :]


def spread(target, packed_ref, first):
    packed = packed_ref[...].astype(F32)
    coef = packed[:, RANK : RANK + 2 * STATE] + packed[:, RANK + 2 * STATE :]
    for n in range(STATE):
        target[n] = jnp.broadcast_to(coef[:, first + n : first + n + 1], (coef.shape[0], LANES))


def scan_kernel(
    order_ref,
    near_ref,
    other_ref,
    mixed_ref,
    rates_ref,
    proj_hbm,
    bias_hbm,
    packed_ref,
    msg_ref,
    y_hbm,
    delta_hbm,
    before_hbm,
    enter_hbm,
    b_wide,
    c_wide,
    proj_ref,
    bias_ref,
    y_ref,
    delta_ref,
    before_ref,
    enter_ref,
    in_sems,
    out_sems,
):
    length, channels = mixed_ref.shape
    steps = length // SEG
    copies = [
        pltpu.make_async_copy(proj_hbm, proj_ref, in_sems.at[0]),
        pltpu.make_async_copy(bias_hbm, bias_ref, in_sems.at[1]),
    ]
    for copy in copies:
        copy.start()
    half = SEG // 2
    for place in range(half):
        taken = slice(place * steps, (place + 1) * steps)
        for source, slot in ((near_ref, place), (other_ref, place + half)):
            rows = pl.ds(pl.multiple_of(order_ref[slot] * steps, steps), steps)
            packed_ref[rows, :] = source[taken, :]
    spread(b_wide, packed_ref, 0)
    spread(c_wide, packed_ref, STATE)
    for copy in copies:
        copy.wait()
    copies = []
    raw = jnp.dot(packed_ref[:, :RANK], proj_ref[...], preferred_element_type=F32) + bias_ref[...]
    delta_ref[...] = jnp.maximum(raw, 0.0) + jnp.log1p(jnp.exp(-jnp.abs(raw)))
    row = lax.broadcasted_iota(jnp.int32, (SEG, LANES), 0)

    def shifted(value, by, fill):
        return jnp.where(row < by, fill, pltpu.roll(value, by, axis=0))

    for lane in range(0, channels, LANES):
        lanes = pl.ds(lane, LANES)
        rates = [
            jnp.broadcast_to(rates_ref[n : n + 1, lanes], (SEG, LANES)) for n in range(STATE)
        ]

        def step(i, carry):
            elapsed, states = carry
            rows = pl.ds(pl.multiple_of(i * SEG, SEG), SEG)
            delta = delta_ref[rows, lanes]
            drive = delta * mixed_ref[rows, lanes]
            fresh, terms = [], []
            for n in range(STATE):
                state = jnp.exp2(delta * rates[n]) * states[n] + drive * b_wide[n, rows, :]
                fresh.append(state)
                terms.append(state * c_wide[n, rows, :])
            while len(terms) > 1:
                terms = [a + b for a, b in zip(terms[::2], terms[1::2])]
            y_ref[rows, lanes] = terms[0]
            return elapsed + delta, tuple(fresh)

        zero = jnp.zeros((SEG, LANES), F32)
        elapsed, states = lax.fori_loop(0, steps, step, (zero, (zero,) * STATE), unroll=2)
        total = elapsed
        for by in (1, 2, 4):
            total = total + shifted(total, by, 0.0)
        before_ref[:, lanes] = shifted(total, 1, 0.0)
        last = total[SEG - 1 : SEG, :]
        for n in range(STATE):
            decay = jnp.exp2(elapsed * rates[n])
            state = states[n]
            for by in (1, 2, 4):
                state = decay * shifted(state, by, 0.0) + state
                decay = decay * shifted(decay, by, 1.0)
            enter_ref[n, :, lanes] = shifted(state, 1, 0.0)
            msg_ref[n : n + 1, lanes] = state[SEG - 1 : SEG, :]
        msg_ref[STATE : STATE + 1, lanes] = last
        block = lane // LANES
        fresh = [
            pltpu.make_async_copy(
                before_ref.at[:, lanes], before_hbm.at[:, lanes], out_sems.at[0, block]
            ),
            pltpu.make_async_copy(
                enter_ref.at[:, :, lanes], enter_hbm.at[:, :, lanes], out_sems.at[1, block]
            ),
            pltpu.make_async_copy(y_ref.at[:, lanes], y_hbm.at[:, lanes], out_sems.at[2, block]),
            pltpu.make_async_copy(
                delta_ref.at[:, lanes], delta_hbm.at[:, lanes], out_sems.at[3, block]
            ),
        ]
        for copy in fresh:
            copy.start()
        copies += fresh
    for copy in copies:
        copy.wait()


def meet_kernel(before_ref, own_ref, got_ref, prefix_ref, rates_ref, total_ref, next_ref):
    partner_first = before_ref[0] > 0
    rates = rates_ref[...]
    own, got = own_ref[:STATE, :], got_ref[:STATE, :]
    own_delta, got_delta = own_ref[STATE : STATE + 1, :], got_ref[STATE : STATE + 1, :]
    prefix, prefix_delta = prefix_ref[:STATE, :], prefix_ref[STATE : STATE + 1, :]
    late_delta = jnp.where(partner_first, own_delta, got_delta)
    early = jnp.where(partner_first, got, own)
    late = jnp.where(partner_first, own, got)
    total_ref[:STATE, :] = jnp.exp2(late_delta * rates) * early + late
    total_ref[STATE : STATE + 1, :] = own_delta + got_delta
    joined = jnp.exp2(prefix_delta * rates) * got + prefix
    next_ref[:STATE, :] = jnp.where(partner_first, joined, prefix)
    next_ref[STATE : STATE + 1, :] = jnp.where(partner_first, prefix_delta + got_delta, prefix_delta)


def entering_state(message, rates):
    seqs = lax.axis_size("seq")
    side = math.isqrt(seqs)
    place = lax.axis_index("seq").astype(jnp.int32)
    shape = jax.ShapeDtypeStruct(message.shape, F32)
    prefix = jnp.zeros(message.shape, F32)

    def flipped(index, axis, far_step):
        x, y = index // side, index % side
        value = x if axis == "x" else y
        value = side - 1 - value if far_step else value + 1 - 2 * (value % 2)
        return value * side + y if axis == "x" else x * side + value

    for axis in ("y", "x"):
        for far_step in (False, True):
            route = [(i, flipped(i, axis, far_step)) for i in range(seqs)]
            got = lax.ppermute(message, "seq", route)
            before = (flipped(place, axis, far_step) < place).astype(jnp.int32).reshape(1)
            message, prefix = pl.pallas_call(
                meet_kernel,
                out_shape=(shape, shape),
                in_specs=[pl.BlockSpec(memory_space=pltpu.SMEM)] + [whole()] * 4,
                out_specs=[whole()] * 2,
                compiler_params=params(4),
                name="meet",
            )(before, message, got, prefix, rates)
    return prefix


def finish_kernel(
    order_ref,
    entering_ref,
    rates_ref,
    packed_ref,
    mixed_ref,
    before_hbm,
    enter_hbm,
    skip_hbm,
    z_hbm,
    y_hbm,
    delta_hbm,
    gated_ref,
    before_ref,
    enter_ref,
    skip_ref,
    z_ref,
    y_ref,
    delta_ref,
    c_wide,
    z_wide,
    gated,
    sems,
    block_sems,
):
    length, channels = mixed_ref.shape
    steps = length // SEG
    sources = (before_hbm, enter_hbm, skip_hbm, z_hbm)
    targets = (before_ref, enter_ref, skip_ref, z_ref)
    copies = [pltpu.make_async_copy(*pair, sems.at[k]) for k, pair in enumerate(zip(sources, targets))]
    for copy in copies:
        copy.start()
    blocks = []
    for lane in range(0, channels, LANES):
        lanes = pl.ds(lane, LANES)
        y_sem, delta_sem = block_sems.at[0, lane // LANES], block_sems.at[1, lane // LANES]
        pair = (
            pltpu.make_async_copy(y_hbm.at[:, lanes], y_ref.at[:, lanes], y_sem),
            pltpu.make_async_copy(delta_hbm.at[:, lanes], delta_ref.at[:, lanes], delta_sem),
        )
        for copy in pair:
            copy.start()
        blocks.append(pair)
    spread(c_wide, packed_ref, STATE)
    for copy in copies:
        copy.wait()
    for lane in range(0, channels, LANES):
        z_wide[lane // LANES] = z_ref[:, lane : lane + LANES].astype(F32)

    for lane in range(0, channels, LANES):
        lanes = pl.ds(lane, LANES)
        rates = [
            jnp.broadcast_to(rates_ref[n : n + 1, lanes], (SEG, LANES)) for n in range(STATE)
        ]
        for copy in blocks[lane // LANES]:
            copy.wait()
        before = before_ref[:, lanes]
        held = [
            jnp.exp2(before * rates[n]) * entering_ref[n : n + 1, lanes] + enter_ref[n, :, lanes]
            for n in range(STATE)
        ]
        skip = skip_ref[:, lanes]

        def step(i, elapsed):
            rows = pl.ds(pl.multiple_of(i * SEG, SEG), SEG)
            apart = pl.ds(i, SEG, stride=steps)
            elapsed = elapsed + delta_ref[rows, lanes]
            terms = [
                jnp.exp2(elapsed * rates[n]) * held[n] * c_wide[n, rows, :] for n in range(STATE)
            ]
            while len(terms) > 1:
                terms = [a + b for a, b in zip(terms[::2], terms[1::2])]
            output = y_ref[rows, lanes] + terms[0] + skip * mixed_ref[rows, lanes]
            z = z_wide[lane // LANES, apart, :]
            gated[lane // LANES, apart, :] = output * (z * jax.nn.sigmoid(z))
            return elapsed

        lax.fori_loop(0, steps, step, jnp.zeros((SEG, LANES), F32), unroll=2)
    for place in range(SEG):
        rows = pl.ds(pl.multiple_of(order_ref[place] * steps, steps), steps)
        for lane in range(0, channels, LANES):
            gated_ref[place * steps : (place + 1) * steps, lane : lane + LANES] = gated[
                lane // LANES, rows, :
            ].astype(BF16)


def outward_kernel(gated_ref, proj_hbm, send_ref, keep_ref, proj, arrived):
    parts, _, width = proj_hbm.shape
    middle = send_ref.shape[0]
    for part in range(parts):
        pltpu.make_async_copy(proj_hbm.at[part], proj.at[part], arrived.at[part]).start()

    def product(part, carry):
        pltpu.make_async_copy(proj_hbm.at[part], proj.at[part], arrived.at[part]).wait()
        columns = pl.ds(pl.multiple_of(part * width, width), width)
        terms = jnp.dot(gated_ref[...], proj[part], preferred_element_type=F32)
        send_ref[:, columns] = terms[:middle].astype(BF16)
        keep_ref[:, columns] = terms[middle:]
        return carry

    lax.fori_loop(0, parts, product, 0)


def expert_kernel(rows_ref, gate_ref, up_ref, down_ref, first_ref, second_ref, inner):
    tile = 256
    middle = first_ref.shape[0]

    def widen(part, carry):
        columns = pl.ds(pl.multiple_of(part * tile, tile), tile)
        gate = jnp.dot(rows_ref[...], gate_ref[:, columns], preferred_element_type=F32)
        upper = jnp.dot(rows_ref[...], up_ref[:, columns], preferred_element_type=F32)
        inner[:, columns] = (gate * jax.nn.sigmoid(gate) * upper).astype(BF16)
        return carry

    lax.fori_loop(0, inner.shape[1] // tile, widen, 0)

    def narrow(part, carry):
        columns = pl.ds(pl.multiple_of(part * tile, tile), tile)
        piece = jnp.dot(inner[...], down_ref[:, columns], preferred_element_type=F32)
        first_ref[:, columns] = piece[:middle].astype(BF16)
        second_ref[:, columns] = piece[middle:].astype(BF16)
        return carry

    lax.fori_loop(0, first_ref.shape[1] // tile, narrow, 0)


def expert(rows, gate, up, down):
    count, features = rows.shape
    hidden = gate.shape[1]
    return pl.pallas_call(
        expert_kernel,
        out_shape=(jax.ShapeDtypeStruct((count // 2, features), BF16),) * 2,
        in_specs=[whole()] * 4,
        out_specs=[whole()] * 2,
        scratch_shapes=[pltpu.VMEM((count, hidden), BF16)],
        compiler_params=params(12),
        cost_estimate=pl.CostEstimate(
            flops=count * features, bytes_accessed=count * features, transcendentals=count
        ),
        name="expert",
    )(rows, gate, up, down)


def halves(block):
    middle = block.shape[0] // 2
    return block[:middle], block[middle:]


def added(*blocks):
    total = blocks[0].astype(F32)
    for block in blocks[1:]:
        total = total + block.astype(F32)
    return total.astype(BF16)


def experts_on_grid(rows, gate, up, down):
    run = functools.partial(expert, gate=gate, up=up, down=down)
    behind = along(rows, 0, 1)
    ahead = along(rows, 0, -1)
    across = jnp.concatenate(
        [along(halves(behind)[0], 0, 1), along(halves(ahead)[1], 0, -1)], axis=0
    )
    own_first = jnp.concatenate([rows, behind], axis=0)
    behind_first = along(own_first, 1, 1)
    across, own_first_later = lax.optimization_barrier((across, own_first))
    own_second = jnp.concatenate([ahead, across], axis=0)
    ahead_second = jnp.concatenate([along(ahead, 1, -1), along(across, 1, -1)], axis=0)
    behind_second = along(own_second, 1, 1)
    ahead_first = along(own_first_later, 1, -1)
    own_out = run(jnp.concatenate([own_first, own_second], axis=0))
    behind_first, ahead_second, own_out = lax.optimization_barrier(
        (behind_first, ahead_second, own_out)
    )
    far_first = along(behind_first, 1, 1)
    far_second = along(ahead_second, 1, -1)
    behind_out, ahead_out = run(jnp.concatenate([behind_first, ahead_second], axis=0))
    early_first = along(behind_out, 1, -1)
    early_second = along(ahead_out, 1, 1)
    behind_second, ahead_first, behind_out = lax.optimization_barrier(
        (behind_second, ahead_first, behind_out)
    )
    behind_rest, ahead_rest = run(jnp.concatenate([behind_second, ahead_first], axis=0))
    far_first, far_second, behind_rest = lax.optimization_barrier(
        (far_first, far_second, behind_rest)
    )
    across_first, across_second = run(jnp.concatenate([far_first, far_second], axis=0))
    across_first, across_second, early_first, early_second = lax.optimization_barrier(
        (across_first, across_second, early_first, early_second)
    )
    late_first = along(added(ahead_rest, along(across_first, 1, 1)), 1, 1)
    late_second = along(added(behind_rest, along(across_second, 1, -1)), 1, -1)
    kept, behind = halves(added(own_out[0], early_first, late_first))
    ahead, across = halves(added(own_out[1], early_second, late_second))
    across_first, across_second = halves(across)
    ahead_first, ahead_second = halves(ahead)
    behind_first, behind_second = halves(behind)
    ahead_first = added(ahead_first, along(across_first, 0, 1))
    behind_second = added(behind_second, along(across_second, 0, -1))
    from_behind = along(jnp.concatenate([ahead_first, ahead_second], axis=0), 0, 1)
    from_ahead = along(jnp.concatenate([behind_first, behind_second], axis=0), 0, -1)
    return added(kept, from_behind, from_ahead)


def mixer(x_in, z_in, conv_weight, conv_bias, x_proj, dt_proj, dt_bias, a_log, d_skip, out_proj):
    length, channels = x_in.shape
    steps = length // SEG
    owners = lax.axis_size("exp")
    seqs = lax.axis_size("seq")
    side = owners // 2
    owner = lax.axis_index("exp").astype(jnp.int32)
    chip, core = owner // 2, owner % 2
    swap = [(e, e + 1 - 2 * (e % 2)) for e in range(owners)]

    def along_z(block, hop):
        return lax.ppermute(block, "exp", [(e, (e + 2 * hop) % owners) for e in range(owners)])

    columns = lax.all_gather(out_proj, "seq", axis=0)
    hops = jnp.arange(side, dtype=jnp.int32)
    onward, back = (chip + hops) % side, (chip - hops) % side
    order = jnp.concatenate([onward * 2 + 1 - core, onward * 2 + core])
    arrival = jnp.concatenate([back * 2 + core, back * 2 + 1 - core])

    rates = (-jnp.exp(a_log) * LOG2E).T
    rim = passed_along(x_in[length - (CONV - 1) :], "seq", 1)
    mixed, send, keep = pl.pallas_call(
        conv_kernel,
        out_shape=(
            jax.ShapeDtypeStruct((length, channels), F32),
            jax.ShapeDtypeStruct((length // 2, RANK + 2 * STATE), F32),
            jax.ShapeDtypeStruct((length // 2, RANK + 2 * STATE), F32),
        ),
        in_specs=[pl.BlockSpec(memory_space=pltpu.SMEM)] + [far()] * 2 + [whole()] * 2,
        out_specs=[whole()] * 3,
        scratch_shapes=[
            pltpu.VMEM(x_in.shape, BF16),
            pltpu.VMEM(x_proj.shape[::-1], BF16),
            pltpu.VMEM((channels // LANES, length + 8, LANES), F32),
            pltpu.VMEM((length, RANK + 2 * STATE), F32),
            pltpu.SemaphoreType.DMA((2,)),
        ],
        compiler_params=params(59),
        name="conv",
    )(order, x_in, x_proj.T, jnp.concatenate([conv_weight, conv_bias[None, :]], axis=0), rim)
    sums = (keep + lax.ppermute(send, "exp", swap)).reshape(side, length // owners, -1)
    summed = sums[0]
    for hop in range(1, side):
        summed = summed + along_z(sums[hop], hop)
    coef = summed[:, RANK:]
    coef_high = coef.astype(BF16)
    coef_low = (coef - coef_high.astype(F32)).astype(BF16)
    near = jnp.concatenate([summed[:, :RANK].astype(BF16), coef_high, coef_low], axis=1)
    near = jnp.concatenate([near] + [along_z(near, hop) for hop in range(1, side)], axis=0)
    other = lax.ppermute(near, "exp", swap)
    packed, message, y_local, delta, before, enter = pl.pallas_call(
        scan_kernel,
        out_shape=(
            jax.ShapeDtypeStruct((length, RANK + 4 * STATE), BF16),
            jax.ShapeDtypeStruct((STATE + 1, channels), F32),
            jax.ShapeDtypeStruct((length, channels), F32),
            jax.ShapeDtypeStruct((length, channels), F32),
            jax.ShapeDtypeStruct((SEG, channels), F32),
            jax.ShapeDtypeStruct((STATE, SEG, channels), F32),
        ),
        in_specs=[pl.BlockSpec(memory_space=pltpu.SMEM)] + [whole()] * 4 + [far()] * 2,
        out_specs=[whole()] * 2 + [far()] * 4,
        scratch_shapes=[
            pltpu.VMEM((STATE, length, LANES), F32),
            pltpu.VMEM((STATE, length, LANES), F32),
            pltpu.VMEM(dt_proj.shape, BF16),
            pltpu.VMEM((1, channels), F32),
            pltpu.VMEM((length, channels), F32),
            pltpu.VMEM((length, channels), F32),
            pltpu.VMEM((SEG, channels), F32),
            pltpu.VMEM((STATE, SEG, channels), F32),
            pltpu.SemaphoreType.DMA((2,)),
            pltpu.SemaphoreType.DMA((4, channels // LANES)),
        ],
        compiler_params=params(58),
        name="scan",
    )(arrival, near, other, mixed, rates, dt_proj, dt_bias[None, :])
    entering = entering_state(message, rates)
    gated = pl.pallas_call(
        finish_kernel,
        out_shape=jax.ShapeDtypeStruct((length, channels), BF16),
        in_specs=[pl.BlockSpec(memory_space=pltpu.SMEM)] + [whole()] * 4 + [far()] * 6,
        out_specs=whole(),
        scratch_shapes=[
            pltpu.VMEM((SEG, channels), F32),
            pltpu.VMEM((STATE, SEG, channels), F32),
            pltpu.VMEM((1, channels), F32),
            pltpu.VMEM((length, channels), BF16),
            pltpu.VMEM((length, channels), F32),
            pltpu.VMEM((length, channels), F32),
            pltpu.VMEM((STATE, length, LANES), F32),
            pltpu.VMEM((channels // LANES, length, LANES), F32),
            pltpu.VMEM((channels // LANES, length, LANES), F32),
            pltpu.SemaphoreType.DMA((4,)),
            pltpu.SemaphoreType.DMA((2, channels // LANES)),
        ],
        compiler_params=params(58),
        name="finish",
    )(
        order,
        entering,
        rates,
        packed,
        mixed,
        before,
        enter,
        d_skip[None, :],
        z_in,
        y_local,
        delta,
    )
    width = out_proj.shape[1]
    features = seqs * width
    send, keep = pl.pallas_call(
        outward_kernel,
        out_shape=(
            jax.ShapeDtypeStruct((length // 2, features), BF16),
            jax.ShapeDtypeStruct((length // 2, features), F32),
        ),
        in_specs=[whole(), far()],
        out_specs=[whole()] * 2,
        scratch_shapes=[
            pltpu.VMEM((seqs, channels, width), BF16),
            pltpu.SemaphoreType.DMA((seqs,)),
        ],
        compiler_params=params(50),
        name="outward",
    )(gated, columns)
    sums = keep + lax.ppermute(send, "exp", swap).astype(F32)
    sums = sums.reshape(side, length // owners, features)
    total = sums[0]
    for hop in range(1, side):
        total = total + along_z(sums[hop].astype(BF16), hop).astype(F32)
    return total


def shards(
    x_in,
    z_in,
    conv_weight,
    conv_bias,
    x_proj,
    dt_proj,
    dt_bias,
    a_log,
    d_skip,
    out_proj,
    residual,
    expert_ids,
    gate_weights,
    w_gate,
    w_up,
    w_down,
):
    owners = lax.axis_size("exp")
    tok_rows = residual.shape[0]
    mixed = mixer(
        x_in, z_in, conv_weight, conv_bias, x_proj, dt_proj, dt_bias, a_log, d_skip, out_proj
    )
    hidden = residual.astype(jnp.float32) + mixed
    normed = (hidden * lax.rsqrt(jnp.mean(hidden * hidden, axis=-1, keepdims=True) + 1e-06)).astype(
        jnp.bfloat16
    )
    capacity = max(2, tok_rows // 4)
    slots = owners * capacity
    chosen_count = expert_ids.shape[1]
    flat_ids = expert_ids.reshape(-1)
    hits = (flat_ids[:, None] == jnp.arange(owners, dtype=jnp.int32)[None, :]).astype(jnp.int32)
    before = jnp.cumsum(hits, axis=0) - hits
    ranked = jnp.sum(before * hits, axis=1)
    valid = jnp.sum(hits, axis=1)
    target = flat_ids * capacity + ranked
    placed = (
        (target[:, None] == jnp.arange(slots, dtype=jnp.int32)[None, :]) & (valid[:, None] > 0)
    ).astype(jnp.float32)
    dispatch_table = jnp.sum(placed.reshape(tok_rows, chosen_count, slots), axis=1)
    combine_table = jnp.sum(
        (placed * gate_weights.reshape(-1)[:, None]).reshape(tok_rows, chosen_count, slots), axis=1
    )
    outgoing = jnp.einsum(
        "ts,td->sd", dispatch_table.astype(jnp.bfloat16), normed, preferred_element_type=jnp.float32
    )
    outgoing = outgoing.astype(jnp.bfloat16).reshape(owners, capacity, -1)
    arrived = lax.all_to_all(outgoing, "exp", split_axis=0, concat_axis=0, tiled=True)
    summed = experts_on_grid(arrived.reshape(slots, -1), w_gate[0], w_up[0], w_down[0])
    expert_out = summed.reshape(owners, capacity, -1)
    returned_rows = lax.all_to_all(
        expert_out, "exp", split_axis=0, concat_axis=0, tiled=True
    ).reshape(slots, -1)
    combined = jnp.dot(
        combine_table, returned_rows.astype(jnp.float32), precision=lax.Precision.HIGHEST
    )
    return hidden + combined


def solution(mesh):
    placed = (
        P("seq", "exp"),
        P("seq", "exp"),
        P(None, "exp"),
        P("exp"),
        P("exp", None),
        P(None, "exp"),
        P("exp"),
        P("exp", None),
        P("exp"),
        P("exp", "seq"),
        P(("seq", "exp"), None),
        P(("seq", "exp"), None),
        P(("seq", "exp"), None),
        P("exp", None, "seq"),
        P("exp", None, "seq"),
        P("exp", "seq", None),
    )
    return jax.shard_map(
        shards, mesh=mesh, in_specs=placed, out_specs=P(("seq", "exp"), None), check_vma=False
    )
```

```python
import functools
import math

import jax
import jax.numpy as jnp
from jax import lax
from jax.experimental import pallas as pl
from jax.experimental.pallas import tpu as pltpu
from jax.sharding import PartitionSpec as P

RANK = 256
STATE = 16
CONV = 4
SEG = 8
LANES = 128
LOG2E = math.log2(math.e)
F32 = jnp.float32
BF16 = jnp.bfloat16
MIB = 1024 * 1024


def whole():
    return pl.BlockSpec(memory_space=pltpu.VMEM)


def far():
    return pl.BlockSpec(memory_space=pltpu.HBM)


def params(mib):
    return pltpu.CompilerParams(vmem_limit_bytes=mib * MIB)


def lines(stage):
    side = math.isqrt(lax.axis_size("seq"))
    owners = lax.axis_size("exp")
    groups = []
    for owner in range(owners):
        along_x = (owner % 2 == 0) == (stage == 0)
        for fixed in range(side):
            members = [(m * side + fixed if along_x else fixed * side + m) for m in range(side)]
            groups.append([m * owners + owner for m in members])
    return groups


def along(block, stage, distance):
    route = []
    for members in lines(stage):
        count = len(members)
        route += [(members[i], members[(i + distance) % count]) for i in range(count)]
    return lax.ppermute(block, ("seq", "exp"), route)


def passed_along(block, axis, distance):
    devices = range(lax.axis_size(axis))
    route = [(i - distance, i) for i in devices if i - distance in devices]
    return lax.ppermute(block, axis, route)


def conv_kernel(
    order_ref,
    x_hbm,
    proj_hbm,
    weight_ref,
    rim_ref,
    mixed_ref,
    send_ref,
    keep_ref,
    x_ref,
    proj_ref,
    padded,
    part_ref,
    sems,
):
    sources = (x_hbm, proj_hbm)
    targets = (x_ref, proj_ref)
    copies = [pltpu.make_async_copy(*pair, sems.at[k]) for k, pair in enumerate(zip(sources, targets))]
    for copy in copies:
        copy.start()
    length, channels = x_ref.shape
    steps = length // SEG
    head = 8
    copies[0].wait()
    for lane in range(0, channels, LANES):
        block = padded.at[lane // LANES]
        block[head - (CONV - 1) : head, :] = rim_ref[:, lane : lane + LANES].astype(F32)
        block[head:, :] = x_ref[:, lane : lane + LANES].astype(F32)

    def step(i, carry):
        rows = pl.ds(pl.multiple_of(i * SEG, SEG), SEG)
        for lane in range(0, channels, LANES):
            lanes = pl.ds(lane, LANES)
            acc = jnp.broadcast_to(weight_ref[CONV : CONV + 1, lanes], (SEG, LANES))
            for tap in range(CONV):
                taken = padded[
                    lane // LANES, pl.ds(i + head - (CONV - 1) + tap, SEG, stride=steps), :
                ]
                acc = acc + weight_ref[tap : tap + 1, lanes] * taken
            mixed_ref[rows, lanes] = (acc * jax.nn.sigmoid(acc)).astype(BF16).astype(F32)
        return carry

    lax.fori_loop(0, steps, step, 0)
    copies[1].wait()
    part_ref[...] = lax.dot_general(
        mixed_ref[...].astype(BF16),
        proj_ref[...],
        (((1,), (1,)), ((), ())),
        preferred_element_type=F32,
    )
    half = SEG // 2
    for place in range(SEG):
        rows = pl.ds(pl.multiple_of(order_ref[place] * steps, steps), steps)
        target = send_ref if place < half else keep_ref
        first = place % half * steps
        target[first : first + steps, :] = part_ref[rows, :]


def spread(target, packed_ref, first):
    packed = packed_ref[...].astype(F32)
    coef = packed[:, RANK : RANK + 2 * STATE] + packed[:, RANK + 2 * STATE :]
    for n in range(STATE):
        target[n] = jnp.broadcast_to(coef[:, first + n : first + n + 1], (coef.shape[0], LANES))


def scan_kernel(
    order_ref,
    near_ref,
    other_ref,
    mixed_ref,
    rates_ref,
    proj_hbm,
    bias_hbm,
    packed_ref,
    msg_ref,
    y_ref,
    delta_ref,
    before_hbm,
    enter_hbm,
    b_wide,
    c_wide,
    proj_ref,
    bias_ref,
    ends_ref,
    deltas_ref,
    before_ref,
    enter_ref,
    in_sems,
    out_sems,
):
    length, channels = mixed_ref.shape
    steps = length // SEG
    copies = [
        pltpu.make_async_copy(proj_hbm, proj_ref, in_sems.at[0]),
        pltpu.make_async_copy(bias_hbm, bias_ref, in_sems.at[1]),
    ]
    for copy in copies:
        copy.start()
    half = SEG // 2
    for place in range(half):
        taken = slice(place * steps, (place + 1) * steps)
        for source, slot in ((near_ref, place), (other_ref, place + half)):
            rows = pl.ds(pl.multiple_of(order_ref[slot] * steps, steps), steps)
            packed_ref[rows, :] = source[taken, :]
    spread(b_wide, packed_ref, 0)
    spread(c_wide, packed_ref, STATE)
    for copy in copies:
        copy.wait()
    copies = []
    raw = jnp.dot(packed_ref[:, :RANK], proj_ref[...], preferred_element_type=F32) + bias_ref[...]
    delta_ref[...] = jnp.maximum(raw, 0.0) + jnp.log1p(jnp.exp(-jnp.abs(raw)))
    row = lax.broadcasted_iota(jnp.int32, (SEG, LANES), 0)

    def shifted(value, by, fill):
        return jnp.where(row < by, fill, pltpu.roll(value, by, axis=0))

    for lane in range(0, channels, LANES):
        lanes = pl.ds(lane, LANES)
        rates = [
            jnp.broadcast_to(rates_ref[n : n + 1, lanes], (SEG, LANES)) for n in range(STATE)
        ]

        def step(i, carry):
            elapsed, states = carry
            rows = pl.ds(pl.multiple_of(i * SEG, SEG), SEG)
            delta = delta_ref[rows, lanes]
            drive = delta * mixed_ref[rows, lanes]
            fresh, terms = [], []
            for n in range(STATE):
                state = jnp.exp2(delta * rates[n]) * states[n] + drive * b_wide[n, rows, :]
                fresh.append(state)
                terms.append(state * c_wide[n, rows, :])
            while len(terms) > 1:
                terms = [a + b for a, b in zip(terms[::2], terms[1::2])]
            y_ref[rows, lanes] = terms[0]
            return elapsed + delta, tuple(fresh)

        zero = jnp.zeros((SEG, LANES), F32)
        elapsed, states = lax.fori_loop(0, steps, step, (zero, (zero,) * STATE), unroll=2)
        total = elapsed
        for by in (1, 2, 4):
            total = total + shifted(total, by, 0.0)
        before_ref[:, lanes] = shifted(total, 1, 0.0)
        last = total[SEG - 1 : SEG, :]
        for n in range(STATE):
            decay = jnp.exp2(elapsed * rates[n])
            state = states[n]
            for by in (1, 2, 4):
                state = decay * shifted(state, by, 0.0) + state
                decay = decay * shifted(decay, by, 1.0)
            enter_ref[n, :, lanes] = shifted(state, 1, 0.0)
            ends_ref[n : n + 1, lanes] = state[SEG - 1 : SEG, :]
        block = lane // LANES
        high = last.astype(BF16).astype(F32)
        deltas_ref[block : block + 1, :] = high
        deltas_ref[SEG + block : SEG + block + 1, :] = last - high
        fresh = [
            pltpu.make_async_copy(
                before_ref.at[:, lanes], before_hbm.at[:, lanes], out_sems.at[0, block]
            ),
            pltpu.make_async_copy(
                enter_ref.at[:, :, lanes], enter_hbm.at[:, :, lanes], out_sems.at[1, block]
            ),
        ]
        for copy in fresh:
            copy.start()
        copies += fresh
    msg_ref[:, :channels] = ends_ref[...].astype(BF16)
    msg_ref[:, channels:] = deltas_ref[...].astype(BF16)
    for copy in copies:
        copy.wait()


def unpacked(message, block):
    lanes = slice(block * LANES, (block + 1) * LANES)
    tail = message[:, message.shape[1] - LANES :].astype(F32)
    delta = tail[block : block + 1] + tail[SEG + block : SEG + block + 1]
    return message[:, lanes].astype(F32), delta


def joined(run, later, rates, chosen):
    state, delta = run
    more, more_delta = later
    state = jnp.where(chosen, jnp.exp2(more_delta * rates) * state + more, state)
    return state, jnp.where(chosen, delta + more_delta, delta)


def meet_kernel(place_ref, own_ref, third_ref, second_ref, first_ref, rates_ref, msg_ref, prefix_ref):
    place = place_ref[0]
    channels = rates_ref.shape[1]
    for block in range(channels // LANES):
        lanes = slice(block * LANES, (block + 1) * LANES)
        rates = rates_ref[:, lanes]
        others = [
            (hops, unpacked(ref[...], block))
            for hops, ref in ((3, third_ref), (2, second_ref), (1, first_ref))
        ]
        run = (jnp.zeros((STATE, LANES), F32), jnp.zeros((1, LANES), F32))
        for hops, message in others:
            run = joined(run, message, rates, hops <= place)
        prefix_ref[:STATE, lanes] = run[0]
        prefix_ref[STATE : STATE + 1, lanes] = run[1]
        run = joined(run, unpacked(own_ref[...], block), rates, place >= 0)
        for hops, message in others:
            run = joined(run, message, rates, hops > place)
        state, delta = run
        high = delta.astype(BF16).astype(F32)
        msg_ref[:STATE, lanes] = state
        msg_ref[block : block + 1, channels:] = high
        msg_ref[SEG + block : SEG + block + 1, channels:] = delta - high


def ringed(message, axis):
    seqs = lax.axis_size("seq")
    side = math.isqrt(seqs)
    got = []
    for hops in range(1, side):
        route = []
        for i in range(seqs):
            x, y = i // side, i % side
            target = ((x + hops) % side, y) if axis == "x" else (x, (y + hops) % side)
            route.append((i, target[0] * side + target[1]))
        got.append(lax.ppermute(message, "seq", route))
    return got[::-1]


def finish_kernel(
    order_ref,
    place_ref,
    prefix_ref,
    third_ref,
    second_ref,
    first_ref,
    rates_ref,
    delta_ref,
    packed_ref,
    y_ref,
    mixed_ref,
    before_hbm,
    enter_hbm,
    skip_hbm,
    z_hbm,
    gated_ref,
    before_ref,
    enter_ref,
    skip_ref,
    z_ref,
    c_wide,
    z_wide,
    gated,
    entering_ref,
    sems,
):
    length, channels = mixed_ref.shape
    steps = length // SEG
    sources = (before_hbm, enter_hbm, skip_hbm, z_hbm)
    targets = (before_ref, enter_ref, skip_ref, z_ref)
    copies = [pltpu.make_async_copy(*pair, sems.at[k]) for k, pair in enumerate(zip(sources, targets))]
    for copy in copies:
        copy.start()
    for block in range(channels // LANES):
        lanes = slice(block * LANES, (block + 1) * LANES)
        rates = rates_ref[:, lanes]
        run = (jnp.zeros((STATE, LANES), F32), jnp.zeros((1, LANES), F32))
        for hops, ref in ((3, third_ref), (2, second_ref), (1, first_ref)):
            run = joined(run, unpacked(ref[...], block), rates, hops <= place_ref[0])
        near = (prefix_ref[:STATE, lanes], prefix_ref[STATE : STATE + 1, lanes])
        entering_ref[:, lanes] = joined(run, near, rates, place_ref[0] >= 0)[0]
    spread(c_wide, packed_ref, STATE)
    for copy in copies:
        copy.wait()
    for lane in range(0, channels, LANES):
        z_wide[lane // LANES] = z_ref[:, lane : lane + LANES].astype(F32)

    for lane in range(0, channels, LANES):
        lanes = pl.ds(lane, LANES)
        rates = [
            jnp.broadcast_to(rates_ref[n : n + 1, lanes], (SEG, LANES)) for n in range(STATE)
        ]
        before = before_ref[:, lanes]
        held = [
            jnp.exp2(before * rates[n]) * entering_ref[n : n + 1, lanes] + enter_ref[n, :, lanes]
            for n in range(STATE)
        ]
        skip = skip_ref[:, lanes]

        def step(i, elapsed):
            rows = pl.ds(pl.multiple_of(i * SEG, SEG), SEG)
            apart = pl.ds(i, SEG, stride=steps)
            elapsed = elapsed + delta_ref[rows, lanes]
            terms = [
                jnp.exp2(elapsed * rates[n]) * held[n] * c_wide[n, rows, :] for n in range(STATE)
            ]
            while len(terms) > 1:
                terms = [a + b for a, b in zip(terms[::2], terms[1::2])]
            output = y_ref[rows, lanes] + terms[0] + skip * mixed_ref[rows, lanes]
            z = z_wide[lane // LANES, apart, :]
            gated[lane // LANES, apart, :] = output * (z * jax.nn.sigmoid(z))
            return elapsed

        lax.fori_loop(0, steps, step, jnp.zeros((SEG, LANES), F32), unroll=2)
    for place in range(SEG):
        rows = pl.ds(pl.multiple_of(order_ref[place] * steps, steps), steps)
        for lane in range(0, channels, LANES):
            gated_ref[place * steps : (place + 1) * steps, lane : lane + LANES] = gated[
                lane // LANES, rows, :
            ].astype(BF16)


def outward_kernel(gated_ref, proj_hbm, send_ref, keep_ref, proj, arrived):
    parts, _, width = proj_hbm.shape
    middle = send_ref.shape[0]
    for part in range(parts):
        pltpu.make_async_copy(proj_hbm.at[part], proj.at[part], arrived.at[part]).start()

    def product(part, carry):
        pltpu.make_async_copy(proj_hbm.at[part], proj.at[part], arrived.at[part]).wait()
        columns = pl.ds(pl.multiple_of(part * width, width), width)
        terms = jnp.dot(gated_ref[...], proj[part], preferred_element_type=F32)
        send_ref[:, columns] = terms[:middle].astype(BF16)
        keep_ref[:, columns] = terms[middle:]
        return carry

    lax.fori_loop(0, parts, product, 0)


def expert_kernel(rows_ref, gate_ref, up_ref, down_ref, first_ref, second_ref, inner):
    tile = 256
    middle = first_ref.shape[0]

    def widen(part, carry):
        columns = pl.ds(pl.multiple_of(part * tile, tile), tile)
        gate = jnp.dot(rows_ref[...], gate_ref[:, columns], preferred_element_type=F32)
        upper = jnp.dot(rows_ref[...], up_ref[:, columns], preferred_element_type=F32)
        inner[:, columns] = (gate * jax.nn.sigmoid(gate) * upper).astype(BF16)
        return carry

    lax.fori_loop(0, inner.shape[1] // tile, widen, 0)

    def narrow(part, carry):
        columns = pl.ds(pl.multiple_of(part * tile, tile), tile)
        piece = jnp.dot(inner[...], down_ref[:, columns], preferred_element_type=F32)
        first_ref[:, columns] = piece[:middle].astype(BF16)
        second_ref[:, columns] = piece[middle:].astype(BF16)
        return carry

    lax.fori_loop(0, first_ref.shape[1] // tile, narrow, 0)


def expert(rows, gate, up, down):
    count, features = rows.shape
    hidden = gate.shape[1]
    return pl.pallas_call(
        expert_kernel,
        out_shape=(jax.ShapeDtypeStruct((count // 2, features), BF16),) * 2,
        in_specs=[whole()] * 4,
        out_specs=[whole()] * 2,
        scratch_shapes=[pltpu.VMEM((count, hidden), BF16)],
        compiler_params=params(12),
        cost_estimate=pl.CostEstimate(
            flops=count * features, bytes_accessed=count * features, transcendentals=count
        ),
        name="expert",
    )(rows, gate, up, down)


def halves(block):
    middle = block.shape[0] // 2
    return block[:middle], block[middle:]


def added(*blocks):
    total = blocks[0].astype(F32)
    for block in blocks[1:]:
        total = total + block.astype(F32)
    return total.astype(BF16)


def experts_on_grid(rows, gate, up, down):
    run = functools.partial(expert, gate=gate, up=up, down=down)
    behind = along(rows, 0, 1)
    ahead = along(rows, 0, -1)
    across = jnp.concatenate(
        [along(halves(behind)[0], 0, 1), along(halves(ahead)[1], 0, -1)], axis=0
    )
    own_first = jnp.concatenate([rows, behind], axis=0)
    behind_first = along(own_first, 1, 1)
    across, own_first_later = lax.optimization_barrier((across, own_first))
    own_second = jnp.concatenate([ahead, across], axis=0)
    ahead_second = jnp.concatenate([along(ahead, 1, -1), along(across, 1, -1)], axis=0)
    behind_second = along(own_second, 1, 1)
    ahead_first = along(own_first_later, 1, -1)
    own_out = run(jnp.concatenate([own_first, own_second], axis=0))
    behind_first, ahead_second, own_out = lax.optimization_barrier(
        (behind_first, ahead_second, own_out)
    )
    far_first = along(behind_first, 1, 1)
    far_second = along(ahead_second, 1, -1)
    behind_out, ahead_out = run(jnp.concatenate([behind_first, ahead_second], axis=0))
    early_first = along(behind_out, 1, -1)
    early_second = along(ahead_out, 1, 1)
    behind_second, ahead_first, behind_out = lax.optimization_barrier(
        (behind_second, ahead_first, behind_out)
    )
    behind_rest, ahead_rest = run(jnp.concatenate([behind_second, ahead_first], axis=0))
    far_first, far_second, behind_rest = lax.optimization_barrier(
        (far_first, far_second, behind_rest)
    )
    across_first, across_second = run(jnp.concatenate([far_first, far_second], axis=0))
    across_first, across_second, early_first, early_second = lax.optimization_barrier(
        (across_first, across_second, early_first, early_second)
    )
    late_first = along(added(ahead_rest, along(across_first, 1, 1)), 1, 1)
    late_second = along(added(behind_rest, along(across_second, 1, -1)), 1, -1)
    kept, behind = halves(added(own_out[0], early_first, late_first))
    ahead, across = halves(added(own_out[1], early_second, late_second))
    across_first, across_second = halves(across)
    ahead_first, ahead_second = halves(ahead)
    behind_first, behind_second = halves(behind)
    ahead_first = added(ahead_first, along(across_first, 0, 1))
    behind_second = added(behind_second, along(across_second, 0, -1))
    from_behind = along(jnp.concatenate([ahead_first, ahead_second], axis=0), 0, 1)
    from_ahead = along(jnp.concatenate([behind_first, behind_second], axis=0), 0, -1)
    return added(kept, from_behind, from_ahead)


def mixer(x_in, z_in, conv_weight, conv_bias, x_proj, dt_proj, dt_bias, a_log, d_skip, out_proj):
    length, channels = x_in.shape
    steps = length // SEG
    owners = lax.axis_size("exp")
    seqs = lax.axis_size("seq")
    side = owners // 2
    owner = lax.axis_index("exp").astype(jnp.int32)
    chip, core = owner // 2, owner % 2
    swap = [(e, e + 1 - 2 * (e % 2)) for e in range(owners)]

    def along_z(block, hop):
        return lax.ppermute(block, "exp", [(e, (e + 2 * hop) % owners) for e in range(owners)])

    columns = lax.all_gather(out_proj, "seq", axis=0)
    hops = jnp.arange(side, dtype=jnp.int32)
    onward, back = (chip + hops) % side, (chip - hops) % side
    order = jnp.concatenate([onward * 2 + 1 - core, onward * 2 + core])
    arrival = jnp.concatenate([back * 2 + core, back * 2 + 1 - core])

    rates = (-jnp.exp(a_log) * LOG2E).T
    rim = passed_along(x_in[length - (CONV - 1) :], "seq", 1)
    mixed, send, keep = pl.pallas_call(
        conv_kernel,
        out_shape=(
            jax.ShapeDtypeStruct((length, channels), F32),
            jax.ShapeDtypeStruct((length // 2, RANK + 2 * STATE), F32),
            jax.ShapeDtypeStruct((length // 2, RANK + 2 * STATE), F32),
        ),
        in_specs=[pl.BlockSpec(memory_space=pltpu.SMEM)] + [far()] * 2 + [whole()] * 2,
        out_specs=[whole()] * 3,
        scratch_shapes=[
            pltpu.VMEM(x_in.shape, BF16),
            pltpu.VMEM(x_proj.shape[::-1], BF16),
            pltpu.VMEM((channels // LANES, length + 8, LANES), F32),
            pltpu.VMEM((length, RANK + 2 * STATE), F32),
            pltpu.SemaphoreType.DMA((2,)),
        ],
        compiler_params=params(12),
        name="conv",
    )(order, x_in, x_proj.T, jnp.concatenate([conv_weight, conv_bias[None, :]], axis=0), rim)
    sums = (keep + lax.ppermute(send, "exp", swap)).reshape(side, length // owners, -1)
    summed = sums[0]
    for hop in range(1, side):
        summed = summed + along_z(sums[hop], hop)
    coef = summed[:, RANK:]
    coef_high = coef.astype(BF16)
    coef_low = (coef - coef_high.astype(F32)).astype(BF16)
    near = jnp.concatenate([summed[:, :RANK].astype(BF16), coef_high, coef_low], axis=1)
    near = jnp.concatenate([near] + [along_z(near, hop) for hop in range(1, side)], axis=0)
    other = lax.ppermute(near, "exp", swap)
    packed, message, y_local, delta, before, enter = pl.pallas_call(
        scan_kernel,
        out_shape=(
            jax.ShapeDtypeStruct((length, RANK + 4 * STATE), BF16),
            jax.ShapeDtypeStruct((STATE, channels + LANES), BF16),
            jax.ShapeDtypeStruct((length, channels), F32),
            jax.ShapeDtypeStruct((length, channels), F32),
            jax.ShapeDtypeStruct((SEG, channels), F32),
            jax.ShapeDtypeStruct((STATE, SEG, channels), F32),
        ),
        in_specs=[pl.BlockSpec(memory_space=pltpu.SMEM)] + [whole()] * 4 + [far()] * 2,
        out_specs=[whole()] * 4 + [far()] * 2,
        scratch_shapes=[
            pltpu.VMEM((STATE, length, LANES), F32),
            pltpu.VMEM((STATE, length, LANES), F32),
            pltpu.VMEM(dt_proj.shape, BF16),
            pltpu.VMEM((1, channels), F32),
            pltpu.VMEM((STATE, channels), F32),
            pltpu.VMEM((STATE, LANES), F32),
            pltpu.VMEM((SEG, channels), F32),
            pltpu.VMEM((STATE, SEG, channels), F32),
            pltpu.SemaphoreType.DMA((2,)),
            pltpu.SemaphoreType.DMA((2, channels // LANES)),
        ],
        compiler_params=params(14),
        name="scan",
    )(arrival, near, other, mixed, rates, dt_proj, dt_bias[None, :])
    place = lax.axis_index("seq").astype(jnp.int32).reshape(1)
    grid_side = math.isqrt(seqs)
    totals, prefix = pl.pallas_call(
        meet_kernel,
        out_shape=(
            jax.ShapeDtypeStruct((STATE, channels + LANES), F32),
            jax.ShapeDtypeStruct((STATE + 1, channels), F32),
        ),
        in_specs=[pl.BlockSpec(memory_space=pltpu.SMEM)] + [whole()] * 5,
        out_specs=[whole()] * 2,
        compiler_params=params(4),
        name="meet",
    )(place % grid_side, message, *ringed(message, "y"), rates)
    lines_before = ringed(totals.astype(BF16), "x")
    gated = pl.pallas_call(
        finish_kernel,
        out_shape=jax.ShapeDtypeStruct((length, channels), BF16),
        in_specs=[pl.BlockSpec(memory_space=pltpu.SMEM)] * 2 + [whole()] * 9 + [far()] * 4,
        out_specs=whole(),
        scratch_shapes=[
            pltpu.VMEM((SEG, channels), F32),
            pltpu.VMEM((STATE, SEG, channels), F32),
            pltpu.VMEM((1, channels), F32),
            pltpu.VMEM((length, channels), BF16),
            pltpu.VMEM((STATE, length, LANES), F32),
            pltpu.VMEM((channels // LANES, length, LANES), F32),
            pltpu.VMEM((channels // LANES, length, LANES), F32),
            pltpu.VMEM((STATE, channels), F32),
            pltpu.SemaphoreType.DMA((4,)),
        ],
        compiler_params=params(16),
        name="finish",
    )(
        order,
        place // grid_side,
        prefix,
        *lines_before,
        rates,
        delta,
        packed,
        y_local,
        mixed,
        before,
        enter,
        d_skip[None, :],
        z_in,
    )
    width = out_proj.shape[1]
    features = seqs * width
    send, keep = pl.pallas_call(
        outward_kernel,
        out_shape=(
            jax.ShapeDtypeStruct((length // 2, features), BF16),
            jax.ShapeDtypeStruct((length // 2, features), F32),
        ),
        in_specs=[whole(), far()],
        out_specs=[whole()] * 2,
        scratch_shapes=[
            pltpu.VMEM((seqs, channels, width), BF16),
            pltpu.SemaphoreType.DMA((seqs,)),
        ],
        compiler_params=params(50),
        name="outward",
    )(gated, columns)
    sums = keep + lax.ppermute(send, "exp", swap).astype(F32)
    sums = sums.reshape(side, length // owners, features)
    total = sums[0]
    for hop in range(1, side):
        total = total + along_z(sums[hop].astype(BF16), hop).astype(F32)
    return total


def shards(
    x_in,
    z_in,
    conv_weight,
    conv_bias,
    x_proj,
    dt_proj,
    dt_bias,
    a_log,
    d_skip,
    out_proj,
    residual,
    expert_ids,
    gate_weights,
    w_gate,
    w_up,
    w_down,
):
    owners = lax.axis_size("exp")
    tok_rows = residual.shape[0]
    mixed = mixer(
        x_in, z_in, conv_weight, conv_bias, x_proj, dt_proj, dt_bias, a_log, d_skip, out_proj
    )
    hidden = residual.astype(jnp.float32) + mixed
    normed = (hidden * lax.rsqrt(jnp.mean(hidden * hidden, axis=-1, keepdims=True) + 1e-06)).astype(
        jnp.bfloat16
    )
    capacity = max(2, tok_rows // 4)
    slots = owners * capacity
    chosen_count = expert_ids.shape[1]
    flat_ids = expert_ids.reshape(-1)
    hits = (flat_ids[:, None] == jnp.arange(owners, dtype=jnp.int32)[None, :]).astype(jnp.int32)
    before = jnp.cumsum(hits, axis=0) - hits
    ranked = jnp.sum(before * hits, axis=1)
    valid = jnp.sum(hits, axis=1)
    target = flat_ids * capacity + ranked
    placed = (
        (target[:, None] == jnp.arange(slots, dtype=jnp.int32)[None, :]) & (valid[:, None] > 0)
    ).astype(jnp.float32)
    dispatch_table = jnp.sum(placed.reshape(tok_rows, chosen_count, slots), axis=1)
    combine_table = jnp.sum(
        (placed * gate_weights.reshape(-1)[:, None]).reshape(tok_rows, chosen_count, slots), axis=1
    )
    outgoing = jnp.einsum(
        "ts,td->sd", dispatch_table.astype(jnp.bfloat16), normed, preferred_element_type=jnp.float32
    )
    outgoing = outgoing.astype(jnp.bfloat16).reshape(owners, capacity, -1)
    arrived = lax.all_to_all(outgoing, "exp", split_axis=0, concat_axis=0, tiled=True)
    summed = experts_on_grid(arrived.reshape(slots, -1), w_gate[0], w_up[0], w_down[0])
    expert_out = summed.reshape(owners, capacity, -1)
    returned_rows = lax.all_to_all(
        expert_out, "exp", split_axis=0, concat_axis=0, tiled=True
    ).reshape(slots, -1)
    combined = jnp.dot(
        combine_table, returned_rows.astype(jnp.float32), precision=lax.Precision.HIGHEST
    )
    return hidden + combined


def solution(mesh):
    placed = (
        P("seq", "exp"),
        P("seq", "exp"),
        P(None, "exp"),
        P("exp"),
        P("exp", None),
        P(None, "exp"),
        P("exp"),
        P("exp", None),
        P("exp"),
        P("exp", "seq"),
        P(("seq", "exp"), None),
        P(("seq", "exp"), None),
        P(("seq", "exp"), None),
        P("exp", None, "seq"),
        P("exp", None, "seq"),
        P("exp", "seq", None),
    )
    return jax.shard_map(
        shards, mesh=mesh, in_specs=placed, out_specs=P(("seq", "exp"), None), check_vma=False
    )
```

```python
import functools
import math

import jax
import jax.numpy as jnp
from jax import lax
from jax.experimental import pallas as pl
from jax.experimental.pallas import tpu as pltpu
from jax.sharding import PartitionSpec as P

RANK = 256
STATE = 16
CONV = 4
SEG = 8
LANES = 128
LOG2E = math.log2(math.e)
F32 = jnp.float32
BF16 = jnp.bfloat16
MIB = 1024 * 1024


def whole():
    return pl.BlockSpec(memory_space=pltpu.VMEM)


def far():
    return pl.BlockSpec(memory_space=pltpu.HBM)


def params(mib):
    return pltpu.CompilerParams(vmem_limit_bytes=mib * MIB)


def lines(stage):
    side = math.isqrt(lax.axis_size("seq"))
    owners = lax.axis_size("exp")
    groups = []
    for owner in range(owners):
        along_x = (owner % 2 == 0) == (stage == 0)
        for fixed in range(side):
            members = [(m * side + fixed if along_x else fixed * side + m) for m in range(side)]
            groups.append([m * owners + owner for m in members])
    return groups


def along(block, stage, distance):
    route = []
    for members in lines(stage):
        count = len(members)
        route += [(members[i], members[(i + distance) % count]) for i in range(count)]
    return lax.ppermute(block, ("seq", "exp"), route)


def passed_along(block, axis, distance):
    devices = range(lax.axis_size(axis))
    route = [(i - distance, i) for i in devices if i - distance in devices]
    return lax.ppermute(block, axis, route)


def conv_kernel(
    places_ref,
    x_hbm,
    proj_hbm,
    weight_ref,
    rim_ref,
    mixed_ref,
    send_ref,
    keep_ref,
    x_ref,
    proj_ref,
    padded,
    part_ref,
    sems,
):
    sources = (x_hbm, proj_hbm)
    targets = (x_ref, proj_ref)
    copies = [pltpu.make_async_copy(*pair, sems.at[k]) for k, pair in enumerate(zip(sources, targets))]
    for copy in copies:
        copy.start()
    length, channels = x_ref.shape
    steps = length // SEG
    head = 8
    copies[0].wait()
    for lane in range(0, channels, LANES):
        block = padded.at[lane // LANES]
        block[head - (CONV - 1) : head, :] = rim_ref[:, lane : lane + LANES].astype(F32)
        block[head:, :] = x_ref[:, lane : lane + LANES].astype(F32)

    def step(i, carry):
        rows = pl.ds(pl.multiple_of(i * SEG, SEG), SEG)
        for lane in range(0, channels, LANES):
            lanes = pl.ds(lane, LANES)
            acc = jnp.broadcast_to(weight_ref[CONV : CONV + 1, lanes], (SEG, LANES))
            for tap in range(CONV):
                taken = padded[
                    lane // LANES, pl.ds(i + head - (CONV - 1) + tap, SEG, stride=steps), :
                ]
                acc = acc + weight_ref[tap : tap + 1, lanes] * taken
            mixed_ref[rows, lanes] = (acc * jax.nn.sigmoid(acc)).astype(BF16).astype(F32)
        return carry

    lax.fori_loop(0, steps, step, 0)
    copies[1].wait()
    part_ref[...] = lax.dot_general(
        mixed_ref[...].astype(BF16),
        proj_ref[...],
        (((1,), (1,)), ((), ())),
        preferred_element_type=F32,
    )
    half = SEG // 2
    for spot in range(SEG):
        rows = pl.ds(pl.multiple_of(places_ref[spot] * steps, steps), steps)
        target = send_ref if spot < half else keep_ref
        first = spot % half * steps
        target[first : first + steps, :] = part_ref[rows, :]


def spread(target, packed_ref, first):
    packed = packed_ref[...].astype(F32)
    coef = packed[:, RANK : RANK + 2 * STATE] + packed[:, RANK + 2 * STATE :]
    for n in range(STATE):
        target[n] = jnp.broadcast_to(coef[:, first + n : first + n + 1], (coef.shape[0], LANES))


def scan_kernel(
    places_ref,
    near_ref,
    other_ref,
    mixed_ref,
    rates_ref,
    proj_hbm,
    bias_hbm,
    packed_ref,
    msg_ref,
    y_ref,
    delta_ref,
    before_hbm,
    enter_hbm,
    b_wide,
    c_wide,
    proj_ref,
    bias_ref,
    ends_ref,
    deltas_ref,
    before_ref,
    enter_ref,
    in_sems,
    out_sems,
):
    length, channels = mixed_ref.shape
    steps = length // SEG
    copies = [
        pltpu.make_async_copy(proj_hbm, proj_ref, in_sems.at[0]),
        pltpu.make_async_copy(bias_hbm, bias_ref, in_sems.at[1]),
    ]
    for copy in copies:
        copy.start()
    half = SEG // 2
    for place in range(half):
        taken = slice(place * steps, (place + 1) * steps)
        for source, slot in ((near_ref, place), (other_ref, place + half)):
            rows = pl.ds(pl.multiple_of(places_ref[SEG + slot] * steps, steps), steps)
            packed_ref[rows, :] = source[taken, :]
    spread(b_wide, packed_ref, 0)
    spread(c_wide, packed_ref, STATE)
    for copy in copies:
        copy.wait()
    copies = []
    raw = jnp.dot(packed_ref[:, :RANK], proj_ref[...], preferred_element_type=F32) + bias_ref[...]
    delta_ref[...] = jnp.maximum(raw, 0.0) + jnp.log1p(jnp.exp(-jnp.abs(raw)))
    row = lax.broadcasted_iota(jnp.int32, (SEG, LANES), 0)

    def shifted(value, by, fill):
        return jnp.where(row < by, fill, pltpu.roll(value, by, axis=0))

    for lane in range(0, channels, LANES):
        lanes = pl.ds(lane, LANES)
        rates = [
            jnp.broadcast_to(rates_ref[n : n + 1, lanes], (SEG, LANES)) for n in range(STATE)
        ]

        def step(i, carry):
            elapsed, states = carry
            rows = pl.ds(pl.multiple_of(i * SEG, SEG), SEG)
            delta = delta_ref[rows, lanes]
            drive = delta * mixed_ref[rows, lanes]
            fresh, terms = [], []
            for n in range(STATE):
                state = jnp.exp2(delta * rates[n]) * states[n] + drive * b_wide[n, rows, :]
                fresh.append(state)
                terms.append(state * c_wide[n, rows, :])
            while len(terms) > 1:
                terms = [a + b for a, b in zip(terms[::2], terms[1::2])]
            y_ref[rows, lanes] = terms[0]
            return elapsed + delta, tuple(fresh)

        zero = jnp.zeros((SEG, LANES), F32)
        elapsed, states = lax.fori_loop(0, steps, step, (zero, (zero,) * STATE), unroll=2)
        total = elapsed
        for by in (1, 2, 4):
            total = total + shifted(total, by, 0.0)
        before_ref[:, lanes] = shifted(total, 1, 0.0)
        last = total[SEG - 1 : SEG, :]
        for n in range(STATE):
            decay = jnp.exp2(elapsed * rates[n])
            state = states[n]
            for by in (1, 2, 4):
                state = decay * shifted(state, by, 0.0) + state
                decay = decay * shifted(decay, by, 1.0)
            enter_ref[n, :, lanes] = shifted(state, 1, 0.0)
            ends_ref[n : n + 1, lanes] = state[SEG - 1 : SEG, :]
        block = lane // LANES
        high = last.astype(BF16).astype(F32)
        deltas_ref[block : block + 1, :] = high
        deltas_ref[SEG + block : SEG + block + 1, :] = last - high
        fresh = [
            pltpu.make_async_copy(
                before_ref.at[:, lanes], before_hbm.at[:, lanes], out_sems.at[0, block]
            ),
            pltpu.make_async_copy(
                enter_ref.at[:, :, lanes], enter_hbm.at[:, :, lanes], out_sems.at[1, block]
            ),
        ]
        for copy in fresh:
            copy.start()
        copies += fresh
    msg_ref[:, :channels] = ends_ref[...].astype(BF16)
    msg_ref[:, channels:] = deltas_ref[...].astype(BF16)
    for copy in copies:
        copy.wait()


def unpacked(message, block):
    lanes = slice(block * LANES, (block + 1) * LANES)
    tail = message[:, message.shape[1] - LANES :].astype(F32)
    delta = tail[block : block + 1] + tail[SEG + block : SEG + block + 1]
    return message[:, lanes].astype(F32), delta


def joined(run, later, rates, chosen):
    state, delta = run
    more, more_delta = later
    state = jnp.where(chosen, jnp.exp2(more_delta * rates) * state + more, state)
    return state, jnp.where(chosen, delta + more_delta, delta)


def meet_kernel(places_ref, own_ref, third_ref, second_ref, first_ref, rates_ref, msg_ref, prefix_ref):
    place = places_ref[2 * SEG]
    channels = rates_ref.shape[1]
    for block in range(channels // LANES):
        lanes = slice(block * LANES, (block + 1) * LANES)
        rates = rates_ref[:, lanes]
        others = [
            (hops, unpacked(ref[...], block))
            for hops, ref in ((3, third_ref), (2, second_ref), (1, first_ref))
        ]
        run = (jnp.zeros((STATE, LANES), F32), jnp.zeros((1, LANES), F32))
        for hops, message in others:
            run = joined(run, message, rates, hops <= place)
        prefix_ref[:STATE, lanes] = run[0]
        prefix_ref[STATE : STATE + 1, lanes] = run[1]
        run = joined(run, unpacked(own_ref[...], block), rates, place >= 0)
        for hops, message in others:
            run = joined(run, message, rates, hops > place)
        state, delta = run
        high = delta.astype(BF16).astype(F32)
        msg_ref[:STATE, lanes] = state
        msg_ref[block : block + 1, channels:] = high
        msg_ref[SEG + block : SEG + block + 1, channels:] = delta - high


def ringed(message, axis):
    seqs = lax.axis_size("seq")
    side = math.isqrt(seqs)
    got = []
    for hops in range(1, side):
        route = []
        for i in range(seqs):
            x, y = i // side, i % side
            target = ((x + hops) % side, y) if axis == "x" else (x, (y + hops) % side)
            route.append((i, target[0] * side + target[1]))
        got.append(lax.ppermute(message, "seq", route))
    return got[::-1]


def finish_kernel(
    places_ref,
    prefix_ref,
    third_ref,
    second_ref,
    first_ref,
    rates_ref,
    delta_ref,
    packed_ref,
    y_ref,
    mixed_ref,
    before_hbm,
    enter_hbm,
    skip_hbm,
    z_hbm,
    gated_ref,
    before_ref,
    enter_ref,
    skip_ref,
    z_ref,
    c_wide,
    z_wide,
    gated,
    entering_ref,
    sems,
):
    length, channels = mixed_ref.shape
    steps = length // SEG
    sources = (before_hbm, enter_hbm, skip_hbm, z_hbm)
    targets = (before_ref, enter_ref, skip_ref, z_ref)
    copies = [pltpu.make_async_copy(*pair, sems.at[k]) for k, pair in enumerate(zip(sources, targets))]
    for copy in copies:
        copy.start()
    place = places_ref[2 * SEG + 1]
    for block in range(channels // LANES):
        lanes = slice(block * LANES, (block + 1) * LANES)
        rates = rates_ref[:, lanes]
        run = (jnp.zeros((STATE, LANES), F32), jnp.zeros((1, LANES), F32))
        for hops, ref in ((3, third_ref), (2, second_ref), (1, first_ref)):
            run = joined(run, unpacked(ref[...], block), rates, hops <= place)
        near = (prefix_ref[:STATE, lanes], prefix_ref[STATE : STATE + 1, lanes])
        entering_ref[:, lanes] = joined(run, near, rates, place >= 0)[0]
    spread(c_wide, packed_ref, STATE)
    for copy in copies:
        copy.wait()
    for lane in range(0, channels, LANES):
        z_wide[lane // LANES] = z_ref[:, lane : lane + LANES].astype(F32)

    for lane in range(0, channels, LANES):
        lanes = pl.ds(lane, LANES)
        rates = [
            jnp.broadcast_to(rates_ref[n : n + 1, lanes], (SEG, LANES)) for n in range(STATE)
        ]
        before = before_ref[:, lanes]
        held = [
            jnp.exp2(before * rates[n]) * entering_ref[n : n + 1, lanes] + enter_ref[n, :, lanes]
            for n in range(STATE)
        ]
        skip = skip_ref[:, lanes]

        def step(i, elapsed):
            rows = pl.ds(pl.multiple_of(i * SEG, SEG), SEG)
            apart = pl.ds(i, SEG, stride=steps)
            elapsed = elapsed + delta_ref[rows, lanes]
            terms = [
                jnp.exp2(elapsed * rates[n]) * held[n] * c_wide[n, rows, :] for n in range(STATE)
            ]
            while len(terms) > 1:
                terms = [a + b for a, b in zip(terms[::2], terms[1::2])]
            output = y_ref[rows, lanes] + terms[0] + skip * mixed_ref[rows, lanes]
            z = z_wide[lane // LANES, apart, :]
            gated[lane // LANES, apart, :] = output * (z * jax.nn.sigmoid(z))
            return elapsed

        lax.fori_loop(0, steps, step, jnp.zeros((SEG, LANES), F32), unroll=2)
    for spot in range(SEG):
        rows = pl.ds(pl.multiple_of(places_ref[spot] * steps, steps), steps)
        for lane in range(0, channels, LANES):
            gated_ref[spot * steps : (spot + 1) * steps, lane : lane + LANES] = gated[
                lane // LANES, rows, :
            ].astype(BF16)


def outward_kernel(gated_ref, proj_hbm, send_ref, keep_ref, proj, arrived):
    parts, _, width = proj_hbm.shape
    middle = send_ref.shape[0]
    for part in range(parts):
        pltpu.make_async_copy(proj_hbm.at[part], proj.at[part], arrived.at[part]).start()

    for part in range(parts):
        pltpu.make_async_copy(proj_hbm.at[part], proj.at[part], arrived.at[part]).wait()
        columns = slice(part * width, (part + 1) * width)
        terms = jnp.dot(gated_ref[...], proj[part], preferred_element_type=F32)
        send_ref[:, columns] = terms[:middle].astype(BF16)
        keep_ref[:, columns] = terms[middle:]


def expert_kernel(rows_ref, gate_ref, up_ref, down_ref, first_ref, second_ref, inner):
    tile = 1024
    middle = first_ref.shape[0]
    gate = jnp.dot(rows_ref[...], gate_ref[...], preferred_element_type=F32)
    upper = jnp.dot(rows_ref[...], up_ref[...], preferred_element_type=F32)
    inner[...] = (gate * jax.nn.sigmoid(gate) * upper).astype(BF16)
    for part in range(first_ref.shape[1] // tile):
        columns = slice(part * tile, (part + 1) * tile)
        piece = jnp.dot(inner[...], down_ref[:, columns], preferred_element_type=F32)
        first_ref[:, columns] = piece[:middle].astype(BF16)
        second_ref[:, columns] = piece[middle:].astype(BF16)


def expert(rows, gate, up, down):
    count, features = rows.shape
    hidden = gate.shape[1]
    return pl.pallas_call(
        expert_kernel,
        out_shape=(jax.ShapeDtypeStruct((count // 2, features), BF16),) * 2,
        in_specs=[whole()] * 4,
        out_specs=[whole()] * 2,
        scratch_shapes=[pltpu.VMEM((count, hidden), BF16)],
        compiler_params=params(12),
        cost_estimate=pl.CostEstimate(
            flops=count * features, bytes_accessed=count * features, transcendentals=count
        ),
        name="expert",
    )(rows, gate, up, down)


def halves(block):
    middle = block.shape[0] // 2
    return block[:middle], block[middle:]


def added(*blocks):
    total = blocks[0].astype(F32)
    for block in blocks[1:]:
        total = total + block.astype(F32)
    return total.astype(BF16)


def experts_on_grid(rows, gate, up, down):
    run = functools.partial(expert, gate=gate, up=up, down=down)
    behind = along(rows, 0, 1)
    ahead = along(rows, 0, -1)
    across = jnp.concatenate(
        [along(halves(behind)[0], 0, 1), along(halves(ahead)[1], 0, -1)], axis=0
    )
    own_first = jnp.concatenate([rows, behind], axis=0)
    behind_first = along(own_first, 1, 1)
    across, own_first_later = lax.optimization_barrier((across, own_first))
    own_second = jnp.concatenate([ahead, across], axis=0)
    ahead_second = jnp.concatenate([along(ahead, 1, -1), along(across, 1, -1)], axis=0)
    behind_second = along(own_second, 1, 1)
    ahead_first = along(own_first_later, 1, -1)
    far_first = along(behind_first, 1, 1)
    far_second = along(ahead_second, 1, -1)
    behind_out, ahead_out = run(jnp.concatenate([behind_first, ahead_second], axis=0))
    early_first = along(behind_out, 1, -1)
    early_second = along(ahead_out, 1, 1)
    behind_second, ahead_first, behind_out = lax.optimization_barrier(
        (behind_second, ahead_first, behind_out)
    )
    behind_rest, ahead_rest = run(jnp.concatenate([behind_second, ahead_first], axis=0))
    far_first, far_second, behind_rest = lax.optimization_barrier(
        (far_first, far_second, behind_rest)
    )
    across_first, across_second = run(jnp.concatenate([far_first, far_second], axis=0))
    across_first, across_second, early_first, early_second = lax.optimization_barrier(
        (across_first, across_second, early_first, early_second)
    )
    from_behind = along(across_first, 1, 1)
    from_ahead = along(across_second, 1, -1)
    own_out = run(jnp.concatenate([own_first, own_second], axis=0))
    from_behind, from_ahead, own_out = lax.optimization_barrier((from_behind, from_ahead, own_out))
    late_first = along(added(ahead_rest, from_behind), 1, 1)
    late_second = along(added(behind_rest, from_ahead), 1, -1)
    kept, behind = halves(added(own_out[0], early_first, late_first))
    ahead, across = halves(added(own_out[1], early_second, late_second))
    across_first, across_second = halves(across)
    ahead_first, ahead_second = halves(ahead)
    behind_first, behind_second = halves(behind)
    ahead_first = added(ahead_first, along(across_first, 0, 1))
    behind_second = added(behind_second, along(across_second, 0, -1))
    from_behind = along(jnp.concatenate([ahead_first, ahead_second], axis=0), 0, 1)
    from_ahead = along(jnp.concatenate([behind_first, behind_second], axis=0), 0, -1)
    return added(kept, from_behind, from_ahead)


def device_places():
    owners, seqs = lax.axis_size("exp"), lax.axis_size("seq")
    side, grid_side = owners // 2, math.isqrt(seqs)
    owner = lax.axis_index("exp").astype(jnp.int32)
    place = lax.axis_index("seq").astype(jnp.int32)
    chip, core = owner // 2, owner % 2
    hops = jnp.arange(side, dtype=jnp.int32)
    onward, back = (chip + hops) % side, (chip - hops) % side
    blocks = [onward * 2 + 1 - core, onward * 2 + core, back * 2 + core, back * 2 + 1 - core]
    return jnp.concatenate(blocks + [(place % grid_side)[None], (place // grid_side)[None]])


def mixer(
    places,
    tail,
    x_in,
    z_in,
    conv_weight,
    conv_bias,
    x_proj,
    dt_proj,
    dt_bias,
    a_log,
    d_skip,
    out_proj,
):
    length, channels = x_in.shape
    steps = length // SEG
    owners = lax.axis_size("exp")
    seqs = lax.axis_size("seq")
    side = owners // 2
    swap = [(e, e + 1 - 2 * (e % 2)) for e in range(owners)]

    def along_z(block, hop):
        return lax.ppermute(block, "exp", [(e, (e + 2 * hop) % owners) for e in range(owners)])

    columns = lax.all_gather(out_proj, "seq", axis=0)
    rates = (-jnp.exp(a_log) * LOG2E).T
    rim = passed_along(tail, "seq", 1)
    mixed, send, keep = pl.pallas_call(
        conv_kernel,
        out_shape=(
            jax.ShapeDtypeStruct((length, channels), F32),
            jax.ShapeDtypeStruct((length // 2, RANK + 2 * STATE), F32),
            jax.ShapeDtypeStruct((length // 2, RANK + 2 * STATE), F32),
        ),
        in_specs=[pl.BlockSpec(memory_space=pltpu.SMEM)] + [far()] * 2 + [whole()] * 2,
        out_specs=[whole()] * 3,
        scratch_shapes=[
            pltpu.VMEM(x_in.shape, BF16),
            pltpu.VMEM(x_proj.shape[::-1], BF16),
            pltpu.VMEM((channels // LANES, length + 8, LANES), F32),
            pltpu.VMEM((length, RANK + 2 * STATE), F32),
            pltpu.SemaphoreType.DMA((2,)),
        ],
        compiler_params=params(12),
        name="conv",
    )(places, x_in, x_proj.T, jnp.concatenate([conv_weight, conv_bias[None, :]], axis=0), rim)
    sums = (keep + lax.ppermute(send, "exp", swap)).reshape(side, length // owners, -1)
    summed = sums[0]
    for hop in range(1, side):
        summed = summed + along_z(sums[hop], hop)
    coef = summed[:, RANK:]
    coef_high = coef.astype(BF16)
    coef_low = (coef - coef_high.astype(F32)).astype(BF16)
    near = jnp.concatenate([summed[:, :RANK].astype(BF16), coef_high, coef_low], axis=1)
    near = jnp.concatenate([near] + [along_z(near, hop) for hop in range(1, side)], axis=0)
    other = lax.ppermute(near, "exp", swap)
    packed, message, y_local, delta, before, enter = pl.pallas_call(
        scan_kernel,
        out_shape=(
            jax.ShapeDtypeStruct((length, RANK + 4 * STATE), BF16),
            jax.ShapeDtypeStruct((STATE, channels + LANES), BF16),
            jax.ShapeDtypeStruct((length, channels), F32),
            jax.ShapeDtypeStruct((length, channels), F32),
            jax.ShapeDtypeStruct((SEG, channels), F32),
            jax.ShapeDtypeStruct((STATE, SEG, channels), F32),
        ),
        in_specs=[pl.BlockSpec(memory_space=pltpu.SMEM)] + [whole()] * 4 + [far()] * 2,
        out_specs=[whole()] * 4 + [far()] * 2,
        scratch_shapes=[
            pltpu.VMEM((STATE, length, LANES), F32),
            pltpu.VMEM((STATE, length, LANES), F32),
            pltpu.VMEM(dt_proj.shape, BF16),
            pltpu.VMEM((1, channels), F32),
            pltpu.VMEM((STATE, channels), F32),
            pltpu.VMEM((STATE, LANES), F32),
            pltpu.VMEM((SEG, channels), F32),
            pltpu.VMEM((STATE, SEG, channels), F32),
            pltpu.SemaphoreType.DMA((2,)),
            pltpu.SemaphoreType.DMA((2, channels // LANES)),
        ],
        compiler_params=params(14),
        name="scan",
    )(places, near, other, mixed, rates, dt_proj, dt_bias[None, :])
    totals, prefix = pl.pallas_call(
        meet_kernel,
        out_shape=(
            jax.ShapeDtypeStruct((STATE, channels + LANES), F32),
            jax.ShapeDtypeStruct((STATE + 1, channels), F32),
        ),
        in_specs=[pl.BlockSpec(memory_space=pltpu.SMEM)] + [whole()] * 5,
        out_specs=[whole()] * 2,
        compiler_params=params(4),
        name="meet",
    )(places, message, *ringed(message, "y"), rates)
    lines_before = ringed(totals.astype(BF16), "x")
    gated = pl.pallas_call(
        finish_kernel,
        out_shape=jax.ShapeDtypeStruct((length, channels), BF16),
        in_specs=[pl.BlockSpec(memory_space=pltpu.SMEM)] + [whole()] * 9 + [far()] * 4,
        out_specs=whole(),
        scratch_shapes=[
            pltpu.VMEM((SEG, channels), F32),
            pltpu.VMEM((STATE, SEG, channels), F32),
            pltpu.VMEM((1, channels), F32),
            pltpu.VMEM((length, channels), BF16),
            pltpu.VMEM((STATE, length, LANES), F32),
            pltpu.VMEM((channels // LANES, length, LANES), F32),
            pltpu.VMEM((channels // LANES, length, LANES), F32),
            pltpu.VMEM((STATE, channels), F32),
            pltpu.SemaphoreType.DMA((4,)),
        ],
        compiler_params=params(16),
        name="finish",
    )(
        places,
        prefix,
        *lines_before,
        rates,
        delta,
        packed,
        y_local,
        mixed,
        before,
        enter,
        d_skip[None, :],
        z_in,
    )
    width = out_proj.shape[1]
    features = seqs * width
    send, keep = pl.pallas_call(
        outward_kernel,
        out_shape=(
            jax.ShapeDtypeStruct((length // 2, features), BF16),
            jax.ShapeDtypeStruct((length // 2, features), F32),
        ),
        in_specs=[whole(), far()],
        out_specs=[whole()] * 2,
        scratch_shapes=[
            pltpu.VMEM((seqs, channels, width), BF16),
            pltpu.SemaphoreType.DMA((seqs,)),
        ],
        compiler_params=params(50),
        name="outward",
    )(gated, columns)
    sums = keep + lax.ppermute(send, "exp", swap).astype(F32)
    sums = sums.reshape(side, length // owners, features)
    total = sums[0]
    for hop in range(1, side):
        total = total + along_z(sums[hop].astype(BF16), hop).astype(F32)
    return total


def shards(
    x_in,
    z_in,
    conv_weight,
    conv_bias,
    x_proj,
    dt_proj,
    dt_bias,
    a_log,
    d_skip,
    out_proj,
    residual,
    expert_ids,
    gate_weights,
    w_gate,
    w_up,
    w_down,
):
    owners = lax.axis_size("exp")
    tok_rows = residual.shape[0]
    capacity = max(2, tok_rows // 4)
    slots = owners * capacity
    chosen_count = expert_ids.shape[1]
    flat_ids = expert_ids.reshape(-1)
    hits = (flat_ids[:, None] == jnp.arange(owners, dtype=jnp.int32)[None, :]).astype(jnp.int32)
    before = jnp.cumsum(hits, axis=0) - hits
    ranked = jnp.sum(before * hits, axis=1)
    valid = jnp.sum(hits, axis=1)
    target = flat_ids * capacity + ranked
    placed = (
        (target[:, None] == jnp.arange(slots, dtype=jnp.int32)[None, :]) & (valid[:, None] > 0)
    ).astype(jnp.float32)
    dispatch_table = jnp.sum(placed.reshape(tok_rows, chosen_count, slots), axis=1)
    combine_table = jnp.sum(
        (placed * gate_weights.reshape(-1)[:, None]).reshape(tok_rows, chosen_count, slots), axis=1
    )
    tail, places, dispatch_table, combine_table = lax.optimization_barrier(
        (x_in[-(CONV - 1) :], device_places(), dispatch_table.astype(BF16), combine_table)
    )
    mixed = mixer(
        places,
        tail,
        x_in,
        z_in,
        conv_weight,
        conv_bias,
        x_proj,
        dt_proj,
        dt_bias,
        a_log,
        d_skip,
        out_proj,
    )
    hidden = residual.astype(jnp.float32) + mixed
    normed = (hidden * lax.rsqrt(jnp.mean(hidden * hidden, axis=-1, keepdims=True) + 1e-06)).astype(
        jnp.bfloat16
    )
    outgoing = jnp.einsum(
        "ts,td->sd", dispatch_table, normed, preferred_element_type=jnp.float32
    )
    outgoing = outgoing.astype(jnp.bfloat16).reshape(owners, capacity, -1)
    arrived = lax.all_to_all(outgoing, "exp", split_axis=0, concat_axis=0, tiled=True)
    summed = experts_on_grid(arrived.reshape(slots, -1), w_gate[0], w_up[0], w_down[0])
    expert_out = summed.reshape(owners, capacity, -1)
    returned_rows = lax.all_to_all(
        expert_out, "exp", split_axis=0, concat_axis=0, tiled=True
    ).reshape(slots, -1)
    combined = jnp.dot(
        combine_table, returned_rows.astype(jnp.float32), precision=lax.Precision.HIGHEST
    )
    return hidden + combined


def solution(mesh):
    placed = (
        P("seq", "exp"),
        P("seq", "exp"),
        P(None, "exp"),
        P("exp"),
        P("exp", None),
        P(None, "exp"),
        P("exp"),
        P("exp", None),
        P("exp"),
        P("exp", "seq"),
        P(("seq", "exp"), None),
        P(("seq", "exp"), None),
        P(("seq", "exp"), None),
        P("exp", None, "seq"),
        P("exp", None, "seq"),
        P("exp", "seq", None),
    )
    return jax.shard_map(
        shards, mesh=mesh, in_specs=placed, out_specs=P(("seq", "exp"), None), check_vma=False
    )
```

```python
import functools
import math

import jax
import jax.numpy as jnp
from jax import lax
from jax.experimental import pallas as pl
from jax.experimental.pallas import tpu as pltpu
from jax.sharding import PartitionSpec as P

RANK = 256
STATE = 16
CONV = 4
SEG = 8
LANES = 128
LOG2E = math.log2(math.e)
F32 = jnp.float32
BF16 = jnp.bfloat16
MIB = 1024 * 1024


def whole():
    return pl.BlockSpec(memory_space=pltpu.VMEM)


def far():
    return pl.BlockSpec(memory_space=pltpu.HBM)


def params(mib):
    return pltpu.CompilerParams(vmem_limit_bytes=mib * MIB)


def lines(stage):
    side = math.isqrt(lax.axis_size("seq"))
    owners = lax.axis_size("exp")
    groups = []
    for owner in range(owners):
        along_x = (owner % 2 == 0) == (stage == 0)
        for fixed in range(side):
            members = [(m * side + fixed if along_x else fixed * side + m) for m in range(side)]
            groups.append([m * owners + owner for m in members])
    return groups


def along(block, stage, distance):
    route = []
    for members in lines(stage):
        count = len(members)
        route += [(members[i], members[(i + distance) % count]) for i in range(count)]
    return lax.ppermute(block, ("seq", "exp"), route)


def passed_along(block, axis, distance):
    devices = range(lax.axis_size(axis))
    route = [(i - distance, i) for i in devices if i - distance in devices]
    return lax.ppermute(block, axis, route)


def conv_kernel(
    places_ref,
    x_hbm,
    proj_hbm,
    weight_ref,
    rim_ref,
    mixed_ref,
    send_ref,
    keep_ref,
    x_ref,
    proj_ref,
    padded,
    part_ref,
    sems,
):
    sources = (x_hbm, proj_hbm)
    targets = (x_ref, proj_ref)
    copies = [pltpu.make_async_copy(*pair, sems.at[k]) for k, pair in enumerate(zip(sources, targets))]
    for copy in copies:
        copy.start()
    length, channels = x_ref.shape
    steps = length // SEG
    head = 8
    copies[0].wait()
    for lane in range(0, channels, LANES):
        block = padded.at[lane // LANES]
        block[head - (CONV - 1) : head, :] = rim_ref[:, lane : lane + LANES].astype(F32)
        block[head:, :] = x_ref[:, lane : lane + LANES].astype(F32)

    def step(i, carry):
        rows = pl.ds(pl.multiple_of(i * SEG, SEG), SEG)
        for lane in range(0, channels, LANES):
            lanes = pl.ds(lane, LANES)
            acc = jnp.broadcast_to(weight_ref[CONV : CONV + 1, lanes], (SEG, LANES))
            for tap in range(CONV):
                taken = padded[
                    lane // LANES, pl.ds(i + head - (CONV - 1) + tap, SEG, stride=steps), :
                ]
                acc = acc + weight_ref[tap : tap + 1, lanes] * taken
            mixed_ref[rows, lanes] = (acc * jax.nn.sigmoid(acc)).astype(BF16).astype(F32)
        return carry

    lax.fori_loop(0, steps, step, 0)
    copies[1].wait()
    part_ref[...] = lax.dot_general(
        mixed_ref[...].astype(BF16),
        proj_ref[...],
        (((1,), (1,)), ((), ())),
        preferred_element_type=F32,
    )
    half = SEG // 2
    for spot in range(SEG):
        rows = pl.ds(pl.multiple_of(places_ref[spot] * steps, steps), steps)
        target = send_ref if spot < half else keep_ref
        first = spot % half * steps
        target[first : first + steps, :] = part_ref[rows, :]


def spread(target, packed_ref, first):
    packed = packed_ref[...].astype(F32)
    coef = packed[:, RANK : RANK + 2 * STATE] + packed[:, RANK + 2 * STATE :]
    for n in range(STATE):
        target[n] = jnp.broadcast_to(coef[:, first + n : first + n + 1], (coef.shape[0], LANES))


def scan_kernel(
    places_ref,
    near_ref,
    other_ref,
    mixed_ref,
    rates_ref,
    proj_hbm,
    bias_hbm,
    packed_ref,
    msg_ref,
    y_ref,
    delta_ref,
    before_hbm,
    enter_hbm,
    b_wide,
    c_wide,
    proj_ref,
    bias_ref,
    ends_ref,
    deltas_ref,
    before_ref,
    enter_ref,
    in_sems,
    out_sems,
):
    length, channels = mixed_ref.shape
    steps = length // SEG
    copies = [
        pltpu.make_async_copy(proj_hbm, proj_ref, in_sems.at[0]),
        pltpu.make_async_copy(bias_hbm, bias_ref, in_sems.at[1]),
    ]
    for copy in copies:
        copy.start()
    half = SEG // 2
    for place in range(half):
        taken = slice(place * steps, (place + 1) * steps)
        for source, slot in ((near_ref, place), (other_ref, place + half)):
            rows = pl.ds(pl.multiple_of(places_ref[SEG + slot] * steps, steps), steps)
            packed_ref[rows, :] = source[taken, :]
    spread(b_wide, packed_ref, 0)
    spread(c_wide, packed_ref, STATE)
    for copy in copies:
        copy.wait()
    copies = []
    raw = jnp.dot(packed_ref[:, :RANK], proj_ref[...], preferred_element_type=F32) + bias_ref[...]
    delta_ref[...] = jnp.maximum(raw, 0.0) + jnp.log1p(jnp.exp(-jnp.abs(raw)))
    row = lax.broadcasted_iota(jnp.int32, (SEG, LANES), 0)

    def shifted(value, by, fill):
        return jnp.where(row < by, fill, pltpu.roll(value, by, axis=0))

    for lane in range(0, channels, LANES):
        lanes = pl.ds(lane, LANES)
        rates = [
            jnp.broadcast_to(rates_ref[n : n + 1, lanes], (SEG, LANES)) for n in range(STATE)
        ]

        def step(i, carry):
            elapsed, states = carry
            rows = pl.ds(pl.multiple_of(i * SEG, SEG), SEG)
            delta = delta_ref[rows, lanes]
            drive = delta * mixed_ref[rows, lanes]
            fresh, terms = [], []
            for n in range(STATE):
                state = jnp.exp2(delta * rates[n]) * states[n] + drive * b_wide[n, rows, :]
                fresh.append(state)
                terms.append(state * c_wide[n, rows, :])
            while len(terms) > 1:
                terms = [a + b for a, b in zip(terms[::2], terms[1::2])]
            y_ref[rows, lanes] = terms[0]
            return elapsed + delta, tuple(fresh)

        zero = jnp.zeros((SEG, LANES), F32)
        elapsed, states = lax.fori_loop(0, steps, step, (zero, (zero,) * STATE), unroll=2)
        total = elapsed
        for by in (1, 2, 4):
            total = total + shifted(total, by, 0.0)
        before_ref[:, lanes] = shifted(total, 1, 0.0)
        last = total[SEG - 1 : SEG, :]
        for n in range(STATE):
            decay = jnp.exp2(elapsed * rates[n])
            state = states[n]
            for by in (1, 2, 4):
                state = decay * shifted(state, by, 0.0) + state
                decay = decay * shifted(decay, by, 1.0)
            enter_ref[n, :, lanes] = shifted(state, 1, 0.0)
            ends_ref[n : n + 1, lanes] = state[SEG - 1 : SEG, :]
        block = lane // LANES
        high = last.astype(BF16).astype(F32)
        deltas_ref[block : block + 1, :] = high
        deltas_ref[SEG + block : SEG + block + 1, :] = last - high
        fresh = [
            pltpu.make_async_copy(
                before_ref.at[:, lanes], before_hbm.at[:, lanes], out_sems.at[0, block]
            ),
            pltpu.make_async_copy(
                enter_ref.at[:, :, lanes], enter_hbm.at[:, :, lanes], out_sems.at[1, block]
            ),
        ]
        for copy in fresh:
            copy.start()
        copies += fresh
    msg_ref[:, :channels] = ends_ref[...]
    msg_ref[:, channels:] = deltas_ref[...]
    for copy in copies:
        copy.wait()


def unpacked(message, block):
    lanes = slice(block * LANES, (block + 1) * LANES)
    tail = message[:, message.shape[1] - LANES :]
    delta = tail[block : block + 1] + tail[SEG + block : SEG + block + 1]
    return message[:, lanes], delta


def joined(run, later, rates, chosen):
    state, delta = run
    more, more_delta = later
    state = jnp.where(chosen, jnp.exp2(more_delta * rates) * state + more, state)
    return state, jnp.where(chosen, delta + more_delta, delta)


def meet_kernel(places_ref, own_ref, third_ref, second_ref, first_ref, rates_ref, msg_ref, prefix_ref):
    place = places_ref[2 * SEG]
    channels = rates_ref.shape[1]
    for block in range(channels // LANES):
        lanes = slice(block * LANES, (block + 1) * LANES)
        rates = rates_ref[:, lanes]
        others = [
            (hops, unpacked(ref[...], block))
            for hops, ref in ((3, third_ref), (2, second_ref), (1, first_ref))
        ]
        run = (jnp.zeros((STATE, LANES), F32), jnp.zeros((1, LANES), F32))
        for hops, message in others:
            run = joined(run, message, rates, hops <= place)
        prefix_ref[:STATE, lanes] = run[0]
        prefix_ref[STATE : STATE + 1, lanes] = run[1]
        run = joined(run, unpacked(own_ref[...], block), rates, place >= 0)
        for hops, message in others:
            run = joined(run, message, rates, hops > place)
        state, delta = run
        high = delta.astype(BF16).astype(F32)
        msg_ref[:STATE, lanes] = state
        msg_ref[block : block + 1, channels:] = high
        msg_ref[SEG + block : SEG + block + 1, channels:] = delta - high


def ringed(message, axis):
    seqs = lax.axis_size("seq")
    side = math.isqrt(seqs)
    got = []
    for hops in range(1, side):
        route = []
        for i in range(seqs):
            x, y = i // side, i % side
            target = ((x + hops) % side, y) if axis == "x" else (x, (y + hops) % side)
            route.append((i, target[0] * side + target[1]))
        got.append(lax.ppermute(message, "seq", route))
    return got[::-1]


def finish_kernel(
    places_ref,
    prefix_ref,
    third_ref,
    second_ref,
    first_ref,
    rates_ref,
    delta_ref,
    packed_ref,
    y_ref,
    mixed_ref,
    before_hbm,
    enter_hbm,
    skip_hbm,
    z_hbm,
    gated_ref,
    before_ref,
    enter_ref,
    skip_ref,
    z_ref,
    c_wide,
    z_wide,
    gated,
    entering_ref,
    sems,
):
    length, channels = mixed_ref.shape
    steps = length // SEG
    sources = (before_hbm, enter_hbm, skip_hbm, z_hbm)
    targets = (before_ref, enter_ref, skip_ref, z_ref)
    copies = [pltpu.make_async_copy(*pair, sems.at[k]) for k, pair in enumerate(zip(sources, targets))]
    for copy in copies:
        copy.start()
    place = places_ref[2 * SEG + 1]
    for block in range(channels // LANES):
        lanes = slice(block * LANES, (block + 1) * LANES)
        rates = rates_ref[:, lanes]
        run = (jnp.zeros((STATE, LANES), F32), jnp.zeros((1, LANES), F32))
        for hops, ref in ((3, third_ref), (2, second_ref), (1, first_ref)):
            run = joined(run, unpacked(ref[...], block), rates, hops <= place)
        near = (prefix_ref[:STATE, lanes], prefix_ref[STATE : STATE + 1, lanes])
        entering_ref[:, lanes] = joined(run, near, rates, place >= 0)[0]
    spread(c_wide, packed_ref, STATE)
    for copy in copies:
        copy.wait()
    for lane in range(0, channels, LANES):
        z_wide[lane // LANES] = z_ref[:, lane : lane + LANES].astype(F32)

    for lane in range(0, channels, LANES):
        lanes = pl.ds(lane, LANES)
        rates = [
            jnp.broadcast_to(rates_ref[n : n + 1, lanes], (SEG, LANES)) for n in range(STATE)
        ]
        before = before_ref[:, lanes]
        held = [
            jnp.exp2(before * rates[n]) * entering_ref[n : n + 1, lanes] + enter_ref[n, :, lanes]
            for n in range(STATE)
        ]
        skip = skip_ref[:, lanes]

        def step(i, elapsed):
            rows = pl.ds(pl.multiple_of(i * SEG, SEG), SEG)
            apart = pl.ds(i, SEG, stride=steps)
            elapsed = elapsed + delta_ref[rows, lanes]
            terms = [
                jnp.exp2(elapsed * rates[n]) * held[n] * c_wide[n, rows, :] for n in range(STATE)
            ]
            while len(terms) > 1:
                terms = [a + b for a, b in zip(terms[::2], terms[1::2])]
            output = y_ref[rows, lanes] + terms[0] + skip * mixed_ref[rows, lanes]
            z = z_wide[lane // LANES, apart, :]
            gated[lane // LANES, apart, :] = output * (z * jax.nn.sigmoid(z))
            return elapsed

        lax.fori_loop(0, steps, step, jnp.zeros((SEG, LANES), F32), unroll=2)
    for spot in range(SEG):
        rows = pl.ds(pl.multiple_of(places_ref[spot] * steps, steps), steps)
        for lane in range(0, channels, LANES):
            gated_ref[spot * steps : (spot + 1) * steps, lane : lane + LANES] = gated[
                lane // LANES, rows, :
            ].astype(BF16)


def outward_kernel(gated_ref, proj_hbm, send_ref, keep_ref, proj, arrived):
    parts, _, width = proj_hbm.shape
    middle = send_ref.shape[0]
    ahead = 4

    def fetch(part):
        return pltpu.make_async_copy(proj_hbm.at[part], proj.at[part], arrived.at[part])

    for part in range(ahead):
        fetch(part).start()

    def product(part, carry):
        fetch(part).wait()

        @pl.when(part + ahead < parts)
        def _():
            fetch(part + ahead).start()

        columns = pl.ds(pl.multiple_of(part * width, width), width)
        terms = jnp.dot(gated_ref[...], proj[part], preferred_element_type=F32)
        send_ref[:, columns] = terms[:middle].astype(BF16)
        keep_ref[:, columns] = terms[middle:]
        return carry

    lax.fori_loop(0, parts, product, 0, unroll=2)


def expert_kernel(rows_ref, gate_ref, up_ref, down_ref, first_ref, second_ref, inner):
    tile = 1024
    middle = first_ref.shape[0]
    gate = jnp.dot(rows_ref[...], gate_ref[...], preferred_element_type=F32)
    upper = jnp.dot(rows_ref[...], up_ref[...], preferred_element_type=F32)
    inner[...] = (gate * jax.nn.sigmoid(gate) * upper).astype(BF16)

    def narrow(part, carry):
        columns = pl.ds(pl.multiple_of(part * tile, tile), tile)
        piece = jnp.dot(inner[...], down_ref[:, columns], preferred_element_type=F32)
        first_ref[:, columns] = piece[:middle].astype(BF16)
        second_ref[:, columns] = piece[middle:].astype(BF16)
        return carry

    lax.fori_loop(0, first_ref.shape[1] // tile, narrow, 0)


def expert(rows, gate, up, down):
    count, features = rows.shape
    hidden = gate.shape[1]
    return pl.pallas_call(
        expert_kernel,
        out_shape=(jax.ShapeDtypeStruct((count // 2, features), BF16),) * 2,
        in_specs=[whole()] * 4,
        out_specs=[whole()] * 2,
        scratch_shapes=[pltpu.VMEM((count, hidden), BF16)],
        compiler_params=params(12),
        cost_estimate=pl.CostEstimate(
            flops=count * features, bytes_accessed=count * features, transcendentals=count
        ),
        name="expert",
    )(rows, gate, up, down)


def halves(block):
    middle = block.shape[0] // 2
    return block[:middle], block[middle:]


def added(*blocks):
    total = blocks[0].astype(F32)
    for block in blocks[1:]:
        total = total + block.astype(F32)
    return total.astype(BF16)


def experts_on_grid(rows, gate, up, down):
    run = functools.partial(expert, gate=gate, up=up, down=down)
    behind = along(rows, 0, 1)
    ahead = along(rows, 0, -1)
    across = jnp.concatenate(
        [along(halves(behind)[0], 0, 1), along(halves(ahead)[1], 0, -1)], axis=0
    )
    own_first = jnp.concatenate([rows, behind], axis=0)
    behind_first = along(own_first, 1, 1)
    across, own_first_later = lax.optimization_barrier((across, own_first))
    own_second = jnp.concatenate([ahead, across], axis=0)
    ahead_second = jnp.concatenate([along(ahead, 1, -1), along(across, 1, -1)], axis=0)
    behind_second = along(own_second, 1, 1)
    ahead_first = along(own_first_later, 1, -1)
    far_first = along(behind_first, 1, 1)
    far_second = along(ahead_second, 1, -1)
    behind_out, ahead_out = run(jnp.concatenate([behind_first, ahead_second], axis=0))
    early_first = along(behind_out, 1, -1)
    early_second = along(ahead_out, 1, 1)
    behind_second, ahead_first, behind_out = lax.optimization_barrier(
        (behind_second, ahead_first, behind_out)
    )
    behind_rest, ahead_rest = run(jnp.concatenate([behind_second, ahead_first], axis=0))
    far_first, far_second, behind_rest = lax.optimization_barrier(
        (far_first, far_second, behind_rest)
    )
    across_first, across_second = run(jnp.concatenate([far_first, far_second], axis=0))
    across_first, across_second, early_first, early_second = lax.optimization_barrier(
        (across_first, across_second, early_first, early_second)
    )
    from_behind = along(across_first, 1, 1)
    from_ahead = along(across_second, 1, -1)
    own_out = run(jnp.concatenate([own_first, own_second], axis=0))
    from_behind, from_ahead, own_out = lax.optimization_barrier((from_behind, from_ahead, own_out))
    late_first = along(added(ahead_rest, from_behind), 1, 1)
    late_second = along(added(behind_rest, from_ahead), 1, -1)
    kept, behind = halves(added(own_out[0], early_first, late_first))
    ahead, across = halves(added(own_out[1], early_second, late_second))
    across_first, across_second = halves(across)
    ahead_first, ahead_second = halves(ahead)
    behind_first, behind_second = halves(behind)
    ahead_first = added(ahead_first, along(across_first, 0, 1))
    behind_second = added(behind_second, along(across_second, 0, -1))
    from_behind = along(jnp.concatenate([ahead_first, ahead_second], axis=0), 0, 1)
    from_ahead = along(jnp.concatenate([behind_first, behind_second], axis=0), 0, -1)
    return added(kept, from_behind, from_ahead)


def device_places():
    owners, seqs = lax.axis_size("exp"), lax.axis_size("seq")
    side, grid_side = owners // 2, math.isqrt(seqs)
    owner = lax.axis_index("exp").astype(jnp.int32)
    place = lax.axis_index("seq").astype(jnp.int32)
    chip, core = owner // 2, owner % 2
    hops = jnp.arange(side, dtype=jnp.int32)
    onward, back = (chip + hops) % side, (chip - hops) % side
    blocks = [onward * 2 + 1 - core, onward * 2 + core, back * 2 + core, back * 2 + 1 - core]
    return jnp.concatenate(blocks + [(place % grid_side)[None], (place // grid_side)[None]])


def mixer(
    places,
    tail,
    x_in,
    z_in,
    conv_weight,
    conv_bias,
    x_proj,
    dt_proj,
    dt_bias,
    a_log,
    d_skip,
    out_proj,
):
    length, channels = x_in.shape
    steps = length // SEG
    owners = lax.axis_size("exp")
    seqs = lax.axis_size("seq")
    side = owners // 2
    swap = [(e, e + 1 - 2 * (e % 2)) for e in range(owners)]

    def along_z(block, hop):
        return lax.ppermute(block, "exp", [(e, (e + 2 * hop) % owners) for e in range(owners)])

    columns = lax.all_gather(out_proj, "seq", axis=0)
    rates = (-jnp.exp(a_log) * LOG2E).T
    rim = passed_along(tail, "seq", 1)
    mixed, send, keep = pl.pallas_call(
        conv_kernel,
        out_shape=(
            jax.ShapeDtypeStruct((length, channels), F32),
            jax.ShapeDtypeStruct((length // 2, RANK + 2 * STATE), F32),
            jax.ShapeDtypeStruct((length // 2, RANK + 2 * STATE), F32),
        ),
        in_specs=[pl.BlockSpec(memory_space=pltpu.SMEM)] + [far()] * 2 + [whole()] * 2,
        out_specs=[whole()] * 3,
        scratch_shapes=[
            pltpu.VMEM(x_in.shape, BF16),
            pltpu.VMEM(x_proj.shape[::-1], BF16),
            pltpu.VMEM((channels // LANES, length + 8, LANES), F32),
            pltpu.VMEM((length, RANK + 2 * STATE), F32),
            pltpu.SemaphoreType.DMA((2,)),
        ],
        compiler_params=params(12),
        name="conv",
    )(places, x_in, x_proj.T, jnp.concatenate([conv_weight, conv_bias[None, :]], axis=0), rim)
    sums = (keep + lax.ppermute(send, "exp", swap)).reshape(side, length // owners, -1)
    summed = sums[0]
    for hop in range(1, side):
        summed = summed + along_z(sums[hop], hop)
    coef = summed[:, RANK:]
    coef_high = coef.astype(BF16)
    coef_low = (coef - coef_high.astype(F32)).astype(BF16)
    near = jnp.concatenate([summed[:, :RANK].astype(BF16), coef_high, coef_low], axis=1)
    near = jnp.concatenate([near] + [along_z(near, hop) for hop in range(1, side)], axis=0)
    other = lax.ppermute(near, "exp", swap)
    packed, message, y_local, delta, before, enter = pl.pallas_call(
        scan_kernel,
        out_shape=(
            jax.ShapeDtypeStruct((length, RANK + 4 * STATE), BF16),
            jax.ShapeDtypeStruct((STATE, channels + LANES), F32),
            jax.ShapeDtypeStruct((length, channels), F32),
            jax.ShapeDtypeStruct((length, channels), F32),
            jax.ShapeDtypeStruct((SEG, channels), F32),
            jax.ShapeDtypeStruct((STATE, SEG, channels), F32),
        ),
        in_specs=[pl.BlockSpec(memory_space=pltpu.SMEM)] + [whole()] * 4 + [far()] * 2,
        out_specs=[whole()] * 4 + [far()] * 2,
        scratch_shapes=[
            pltpu.VMEM((STATE, length, LANES), F32),
            pltpu.VMEM((STATE, length, LANES), F32),
            pltpu.VMEM(dt_proj.shape, BF16),
            pltpu.VMEM((1, channels), F32),
            pltpu.VMEM((STATE, channels), F32),
            pltpu.VMEM((STATE, LANES), F32),
            pltpu.VMEM((SEG, channels), F32),
            pltpu.VMEM((STATE, SEG, channels), F32),
            pltpu.SemaphoreType.DMA((2,)),
            pltpu.SemaphoreType.DMA((2, channels // LANES)),
        ],
        compiler_params=params(14),
        name="scan",
    )(places, near, other, mixed, rates, dt_proj, dt_bias[None, :])
    totals, prefix = pl.pallas_call(
        meet_kernel,
        out_shape=(
            jax.ShapeDtypeStruct((STATE, channels + LANES), F32),
            jax.ShapeDtypeStruct((STATE + 1, channels), F32),
        ),
        in_specs=[pl.BlockSpec(memory_space=pltpu.SMEM)] + [whole()] * 5,
        out_specs=[whole()] * 2,
        compiler_params=params(4),
        name="meet",
    )(places, message, *ringed(message, "y"), rates)
    lines_before = ringed(totals, "x")
    gated = pl.pallas_call(
        finish_kernel,
        out_shape=jax.ShapeDtypeStruct((length, channels), BF16),
        in_specs=[pl.BlockSpec(memory_space=pltpu.SMEM)] + [whole()] * 9 + [far()] * 4,
        out_specs=whole(),
        scratch_shapes=[
            pltpu.VMEM((SEG, channels), F32),
            pltpu.VMEM((STATE, SEG, channels), F32),
            pltpu.VMEM((1, channels), F32),
            pltpu.VMEM((length, channels), BF16),
            pltpu.VMEM((STATE, length, LANES), F32),
            pltpu.VMEM((channels // LANES, length, LANES), F32),
            pltpu.VMEM((channels // LANES, length, LANES), F32),
            pltpu.VMEM((STATE, channels), F32),
            pltpu.SemaphoreType.DMA((4,)),
        ],
        compiler_params=params(16),
        name="finish",
    )(
        places,
        prefix,
        *lines_before,
        rates,
        delta,
        packed,
        y_local,
        mixed,
        before,
        enter,
        d_skip[None, :],
        z_in,
    )
    width = out_proj.shape[1]
    features = seqs * width
    send, keep = pl.pallas_call(
        outward_kernel,
        out_shape=(
            jax.ShapeDtypeStruct((length // 2, features), BF16),
            jax.ShapeDtypeStruct((length // 2, features), F32),
        ),
        in_specs=[whole(), far()],
        out_specs=[whole()] * 2,
        scratch_shapes=[
            pltpu.VMEM((seqs, channels, width), BF16),
            pltpu.SemaphoreType.DMA((seqs,)),
        ],
        compiler_params=params(50),
        name="outward",
    )(gated, columns)
    sums = keep + lax.ppermute(send, "exp", swap).astype(F32)
    sums = sums.reshape(side, length // owners, features)
    total = sums[0]
    for hop in range(1, side):
        total = total + along_z(sums[hop].astype(BF16), hop).astype(F32)
    return total


def shards(
    x_in,
    z_in,
    conv_weight,
    conv_bias,
    x_proj,
    dt_proj,
    dt_bias,
    a_log,
    d_skip,
    out_proj,
    residual,
    expert_ids,
    gate_weights,
    w_gate,
    w_up,
    w_down,
):
    owners = lax.axis_size("exp")
    tok_rows = residual.shape[0]
    capacity = max(2, tok_rows // 4)
    slots = owners * capacity
    chosen_count = expert_ids.shape[1]
    flat_ids = expert_ids.reshape(-1)
    hits = (flat_ids[:, None] == jnp.arange(owners, dtype=jnp.int32)[None, :]).astype(jnp.int32)
    before = jnp.cumsum(hits, axis=0) - hits
    ranked = jnp.sum(before * hits, axis=1)
    valid = jnp.sum(hits, axis=1)
    target = flat_ids * capacity + ranked
    placed = (
        (target[:, None] == jnp.arange(slots, dtype=jnp.int32)[None, :]) & (valid[:, None] > 0)
    ).astype(jnp.float32)
    dispatch_table = jnp.sum(placed.reshape(tok_rows, chosen_count, slots), axis=1)
    combine_table = jnp.sum(
        (placed * gate_weights.reshape(-1)[:, None]).reshape(tok_rows, chosen_count, slots), axis=1
    )
    tail, places, dispatch_table, combine_table = lax.optimization_barrier(
        (x_in[-(CONV - 1) :], device_places(), dispatch_table.astype(BF16), combine_table)
    )
    mixed = mixer(
        places,
        tail,
        x_in,
        z_in,
        conv_weight,
        conv_bias,
        x_proj,
        dt_proj,
        dt_bias,
        a_log,
        d_skip,
        out_proj,
    )
    hidden = residual.astype(jnp.float32) + mixed
    normed = (hidden * lax.rsqrt(jnp.mean(hidden * hidden, axis=-1, keepdims=True) + 1e-06)).astype(
        jnp.bfloat16
    )
    outgoing = jnp.einsum(
        "ts,td->sd", dispatch_table, normed, preferred_element_type=jnp.float32
    )
    outgoing = outgoing.astype(jnp.bfloat16).reshape(owners, capacity, -1)
    arrived = lax.all_to_all(outgoing, "exp", split_axis=0, concat_axis=0, tiled=True)
    summed = experts_on_grid(arrived.reshape(slots, -1), w_gate[0], w_up[0], w_down[0])
    expert_out = summed.reshape(owners, capacity, -1)
    returned_rows = lax.all_to_all(
        expert_out, "exp", split_axis=0, concat_axis=0, tiled=True
    ).reshape(slots, -1)
    combined = jnp.dot(
        combine_table, returned_rows.astype(jnp.float32), precision=lax.Precision.HIGHEST
    )
    return hidden + combined


def solution(mesh):
    placed = (
        P("seq", "exp"),
        P("seq", "exp"),
        P(None, "exp"),
        P("exp"),
        P("exp", None),
        P(None, "exp"),
        P("exp"),
        P("exp", None),
        P("exp"),
        P("exp", "seq"),
        P(("seq", "exp"), None),
        P(("seq", "exp"), None),
        P(("seq", "exp"), None),
        P("exp", None, "seq"),
        P("exp", None, "seq"),
        P("exp", "seq", None),
    )
    return jax.shard_map(
        shards, mesh=mesh, in_specs=placed, out_specs=P(("seq", "exp"), None), check_vma=False
    )
```

```python
import functools
import math

import jax
import jax.numpy as jnp
from jax import lax
from jax.experimental import pallas as pl
from jax.experimental.pallas import tpu as pltpu
from jax.sharding import PartitionSpec as P

RANK = 256
STATE = 16
CONV = 4
SEG = 8
LANES = 128
LOG2E = math.log2(math.e)
F32 = jnp.float32
BF16 = jnp.bfloat16
MIB = 1024 * 1024


def whole():
    return pl.BlockSpec(memory_space=pltpu.VMEM)


def far():
    return pl.BlockSpec(memory_space=pltpu.HBM)


def params(mib):
    return pltpu.CompilerParams(vmem_limit_bytes=mib * MIB)


def lines(stage):
    side = math.isqrt(lax.axis_size("seq"))
    owners = lax.axis_size("exp")
    groups = []
    for owner in range(owners):
        along_x = (owner % 2 == 0) == (stage == 0)
        for fixed in range(side):
            members = [(m * side + fixed if along_x else fixed * side + m) for m in range(side)]
            groups.append([m * owners + owner for m in members])
    return groups


def along(block, stage, distance):
    route = []
    for members in lines(stage):
        count = len(members)
        route += [(members[i], members[(i + distance) % count]) for i in range(count)]
    return lax.ppermute(block, ("seq", "exp"), route)


def passed_along(block, axis, distance):
    devices = range(lax.axis_size(axis))
    route = [(i - distance, i) for i in devices if i - distance in devices]
    return lax.ppermute(block, axis, route)


def conv_kernel(
    places_ref,
    x_hbm,
    proj_hbm,
    weight_ref,
    rim_ref,
    mixed_ref,
    send_ref,
    keep_ref,
    x_ref,
    proj_ref,
    padded,
    part_ref,
    sems,
):
    sources = (x_hbm, proj_hbm)
    targets = (x_ref, proj_ref)
    copies = [pltpu.make_async_copy(*pair, sems.at[k]) for k, pair in enumerate(zip(sources, targets))]
    for copy in copies:
        copy.start()
    length, channels = x_ref.shape
    steps = length // SEG
    head = 8
    copies[0].wait()
    for lane in range(0, channels, LANES):
        block = padded.at[lane // LANES]
        block[head - (CONV - 1) : head, :] = rim_ref[:, lane : lane + LANES].astype(F32)
        block[head:, :] = x_ref[:, lane : lane + LANES].astype(F32)

    def step(i, carry):
        rows = pl.ds(pl.multiple_of(i * SEG, SEG), SEG)
        for lane in range(0, channels, LANES):
            lanes = pl.ds(lane, LANES)
            acc = jnp.broadcast_to(weight_ref[CONV : CONV + 1, lanes], (SEG, LANES))
            for tap in range(CONV):
                taken = padded[
                    lane // LANES, pl.ds(i + head - (CONV - 1) + tap, SEG, stride=steps), :
                ]
                acc = acc + weight_ref[tap : tap + 1, lanes] * taken
            mixed_ref[rows, lanes] = (acc * jax.nn.sigmoid(acc)).astype(BF16).astype(F32)
        return carry

    lax.fori_loop(0, steps, step, 0)
    copies[1].wait()
    part_ref[...] = lax.dot_general(
        mixed_ref[...].astype(BF16),
        proj_ref[...],
        (((1,), (1,)), ((), ())),
        preferred_element_type=F32,
    )
    half = SEG // 2
    for spot in range(SEG):
        rows = pl.ds(pl.multiple_of(places_ref[spot] * steps, steps), steps)
        target = send_ref if spot < half else keep_ref
        first = spot % half * steps
        target[first : first + steps, :] = part_ref[rows, :]


def spread(target, packed_ref, first):
    packed = packed_ref[...].astype(F32)
    coef = packed[:, RANK : RANK + 2 * STATE] + packed[:, RANK + 2 * STATE :]
    for n in range(STATE):
        target[n] = jnp.broadcast_to(coef[:, first + n : first + n + 1], (coef.shape[0], LANES))


def scan_kernel(
    places_ref,
    near_ref,
    other_ref,
    mixed_ref,
    rates_ref,
    proj_hbm,
    bias_hbm,
    packed_ref,
    msg_ref,
    y_ref,
    delta_ref,
    before_hbm,
    enter_hbm,
    b_wide,
    c_wide,
    proj_ref,
    bias_ref,
    ends_ref,
    deltas_ref,
    before_ref,
    enter_ref,
    in_sems,
    out_sems,
):
    length, channels = mixed_ref.shape
    steps = length // SEG
    copies = [
        pltpu.make_async_copy(proj_hbm, proj_ref, in_sems.at[0]),
        pltpu.make_async_copy(bias_hbm, bias_ref, in_sems.at[1]),
    ]
    for copy in copies:
        copy.start()
    half = SEG // 2
    for place in range(half):
        taken = slice(place * steps, (place + 1) * steps)
        for source, slot in ((near_ref, place), (other_ref, place + half)):
            rows = pl.ds(pl.multiple_of(places_ref[SEG + slot] * steps, steps), steps)
            packed_ref[rows, :] = source[taken, :]
    spread(b_wide, packed_ref, 0)
    spread(c_wide, packed_ref, STATE)
    for copy in copies:
        copy.wait()
    copies = []
    raw = jnp.dot(packed_ref[:, :RANK], proj_ref[...], preferred_element_type=F32) + bias_ref[...]
    delta_ref[...] = jnp.maximum(raw, 0.0) + jnp.log1p(jnp.exp(-jnp.abs(raw)))
    row = lax.broadcasted_iota(jnp.int32, (SEG, LANES), 0)

    def shifted(value, by, fill):
        return jnp.where(row < by, fill, pltpu.roll(value, by, axis=0))

    for lane in range(0, channels, LANES):
        lanes = pl.ds(lane, LANES)
        rates = [
            jnp.broadcast_to(rates_ref[n : n + 1, lanes], (SEG, LANES)) for n in range(STATE)
        ]

        def step(i, carry):
            elapsed, states = carry
            rows = pl.ds(pl.multiple_of(i * SEG, SEG), SEG)
            delta = delta_ref[rows, lanes]
            drive = delta * mixed_ref[rows, lanes]
            fresh, terms = [], []
            for n in range(STATE):
                state = jnp.exp2(delta * rates[n]) * states[n] + drive * b_wide[n, rows, :]
                fresh.append(state)
                terms.append(state * c_wide[n, rows, :])
            while len(terms) > 1:
                terms = [a + b for a, b in zip(terms[::2], terms[1::2])]
            y_ref[rows, lanes] = terms[0]
            return elapsed + delta, tuple(fresh)

        zero = jnp.zeros((SEG, LANES), F32)
        elapsed, states = lax.fori_loop(0, steps, step, (zero, (zero,) * STATE), unroll=2)
        total = elapsed
        for by in (1, 2, 4):
            total = total + shifted(total, by, 0.0)
        before_ref[:, lanes] = shifted(total, 1, 0.0)
        last = total[SEG - 1 : SEG, :]
        for n in range(STATE):
            decay = jnp.exp2(elapsed * rates[n])
            state = states[n]
            for by in (1, 2, 4):
                state = decay * shifted(state, by, 0.0) + state
                decay = decay * shifted(decay, by, 1.0)
            enter_ref[n, :, lanes] = shifted(state, 1, 0.0)
            ends_ref[n : n + 1, lanes] = state[SEG - 1 : SEG, :]
        block = lane // LANES
        high = last.astype(BF16).astype(F32)
        deltas_ref[block : block + 1, :] = high
        deltas_ref[SEG + block : SEG + block + 1, :] = last - high
        fresh = [
            pltpu.make_async_copy(
                before_ref.at[:, lanes], before_hbm.at[:, lanes], out_sems.at[0, block]
            ),
            pltpu.make_async_copy(
                enter_ref.at[:, :, lanes], enter_hbm.at[:, :, lanes], out_sems.at[1, block]
            ),
        ]
        for copy in fresh:
            copy.start()
        copies += fresh
    msg_ref[:, :channels] = ends_ref[...].astype(BF16)
    msg_ref[:, channels:] = deltas_ref[...].astype(BF16)
    for copy in copies:
        copy.wait()


def unpacked(message, block):
    lanes = slice(block * LANES, (block + 1) * LANES)
    tail = message[:, message.shape[1] - LANES :].astype(F32)
    delta = tail[block : block + 1] + tail[SEG + block : SEG + block + 1]
    return message[:, lanes].astype(F32), delta


def joined(run, later, rates, chosen):
    state, delta = run
    more, more_delta = later
    state = jnp.where(chosen, jnp.exp2(more_delta * rates) * state + more, state)
    return state, jnp.where(chosen, delta + more_delta, delta)


def meet_kernel(places_ref, own_ref, third_ref, second_ref, first_ref, rates_ref, msg_ref, prefix_ref):
    place = places_ref[2 * SEG]
    channels = rates_ref.shape[1]
    for block in range(channels // LANES):
        lanes = slice(block * LANES, (block + 1) * LANES)
        rates = rates_ref[:, lanes]
        others = [
            (hops, unpacked(ref[...], block))
            for hops, ref in ((3, third_ref), (2, second_ref), (1, first_ref))
        ]
        run = (jnp.zeros((STATE, LANES), F32), jnp.zeros((1, LANES), F32))
        for hops, message in others:
            run = joined(run, message, rates, hops <= place)
        prefix_ref[:STATE, lanes] = run[0]
        prefix_ref[STATE : STATE + 1, lanes] = run[1]
        run = joined(run, unpacked(own_ref[...], block), rates, place >= 0)
        for hops, message in others:
            run = joined(run, message, rates, hops > place)
        state, delta = run
        high = delta.astype(BF16).astype(F32)
        msg_ref[:STATE, lanes] = state
        msg_ref[block : block + 1, channels:] = high
        msg_ref[SEG + block : SEG + block + 1, channels:] = delta - high


def ringed(message, axis):
    seqs = lax.axis_size("seq")
    side = math.isqrt(seqs)
    got = []
    for hops in range(1, side):
        route = []
        for i in range(seqs):
            x, y = i // side, i % side
            target = ((x + hops) % side, y) if axis == "x" else (x, (y + hops) % side)
            route.append((i, target[0] * side + target[1]))
        got.append(lax.ppermute(message, "seq", route))
    return got[::-1]


def finish_kernel(
    places_ref,
    prefix_ref,
    third_ref,
    second_ref,
    first_ref,
    rates_ref,
    delta_ref,
    packed_ref,
    y_ref,
    mixed_ref,
    before_hbm,
    enter_hbm,
    skip_hbm,
    z_hbm,
    gated_ref,
    before_ref,
    enter_ref,
    skip_ref,
    z_ref,
    c_wide,
    z_wide,
    gated,
    entering_ref,
    sems,
):
    length, channels = mixed_ref.shape
    steps = length // SEG
    sources = (before_hbm, enter_hbm, skip_hbm, z_hbm)
    targets = (before_ref, enter_ref, skip_ref, z_ref)
    copies = [pltpu.make_async_copy(*pair, sems.at[k]) for k, pair in enumerate(zip(sources, targets))]
    for copy in copies:
        copy.start()
    place = places_ref[2 * SEG + 1]
    for block in range(channels // LANES):
        lanes = slice(block * LANES, (block + 1) * LANES)
        rates = rates_ref[:, lanes]
        run = (jnp.zeros((STATE, LANES), F32), jnp.zeros((1, LANES), F32))
        for hops, ref in ((3, third_ref), (2, second_ref), (1, first_ref)):
            run = joined(run, unpacked(ref[...], block), rates, hops <= place)
        near = (prefix_ref[:STATE, lanes], prefix_ref[STATE : STATE + 1, lanes])
        entering_ref[:, lanes] = joined(run, near, rates, place >= 0)[0]
    spread(c_wide, packed_ref, STATE)
    for copy in copies:
        copy.wait()
    for lane in range(0, channels, LANES):
        z_wide[lane // LANES] = z_ref[:, lane : lane + LANES].astype(F32)

    for lane in range(0, channels, LANES):
        lanes = pl.ds(lane, LANES)
        rates = [
            jnp.broadcast_to(rates_ref[n : n + 1, lanes], (SEG, LANES)) for n in range(STATE)
        ]
        before = before_ref[:, lanes]
        held = [
            jnp.exp2(before * rates[n]) * entering_ref[n : n + 1, lanes] + enter_ref[n, :, lanes]
            for n in range(STATE)
        ]
        skip = skip_ref[:, lanes]

        def step(i, elapsed):
            rows = pl.ds(pl.multiple_of(i * SEG, SEG), SEG)
            apart = pl.ds(i, SEG, stride=steps)
            elapsed = elapsed + delta_ref[rows, lanes]
            terms = [
                jnp.exp2(elapsed * rates[n]) * held[n] * c_wide[n, rows, :] for n in range(STATE)
            ]
            while len(terms) > 1:
                terms = [a + b for a, b in zip(terms[::2], terms[1::2])]
            output = y_ref[rows, lanes] + terms[0] + skip * mixed_ref[rows, lanes]
            z = z_wide[lane // LANES, apart, :]
            gated[lane // LANES, apart, :] = output * (z * jax.nn.sigmoid(z))
            return elapsed

        lax.fori_loop(0, steps, step, jnp.zeros((SEG, LANES), F32), unroll=2)
    for spot in range(SEG):
        rows = pl.ds(pl.multiple_of(places_ref[spot] * steps, steps), steps)
        for lane in range(0, channels, LANES):
            gated_ref[spot * steps : (spot + 1) * steps, lane : lane + LANES] = gated[
                lane // LANES, rows, :
            ].astype(BF16)


def outward_kernel(gated_ref, proj_hbm, send_ref, keep_ref, proj, arrived):
    parts, _, width = proj_hbm.shape
    middle = send_ref.shape[0]
    group = 4

    def fetch(part):
        columns = pl.ds(pl.multiple_of(part * width, width), width)
        return pltpu.make_async_copy(proj_hbm.at[part], proj.at[:, columns], arrived.at[part])

    for part in range(2 * group):
        fetch(part).start()

    def product(step, carry):
        for part in range(group):
            fetch(step * group + part).wait()

        @pl.when(step < parts // group - 2)
        def _():
            for part in range(group):
                fetch((step + 2) * group + part).start()

        wide = group * width
        columns = pl.ds(pl.multiple_of(step * wide, wide), wide)
        terms = jnp.dot(gated_ref[...], proj[:, columns], preferred_element_type=F32)
        send_ref[:, columns] = terms[:middle].astype(BF16)
        keep_ref[:, columns] = terms[middle:]
        return carry

    lax.fori_loop(0, parts // group, product, 0)


def expert_kernel(rows_ref, gate_ref, up_ref, down_ref, first_ref, second_ref, inner):
    tile = 1024
    middle = first_ref.shape[0]
    gate = jnp.dot(rows_ref[...], gate_ref[...], preferred_element_type=F32)
    upper = jnp.dot(rows_ref[...], up_ref[...], preferred_element_type=F32)
    inner[...] = (gate * jax.nn.sigmoid(gate) * upper).astype(BF16)

    def narrow(part, carry):
        columns = pl.ds(pl.multiple_of(part * tile, tile), tile)
        piece = jnp.dot(inner[...], down_ref[:, columns], preferred_element_type=F32)
        first_ref[:, columns] = piece[:middle].astype(BF16)
        second_ref[:, columns] = piece[middle:].astype(BF16)
        return carry

    lax.fori_loop(0, first_ref.shape[1] // tile, narrow, 0)


def expert(rows, gate, up, down):
    count, features = rows.shape
    hidden = gate.shape[1]
    return pl.pallas_call(
        expert_kernel,
        out_shape=(jax.ShapeDtypeStruct((count // 2, features), BF16),) * 2,
        in_specs=[whole()] * 4,
        out_specs=[whole()] * 2,
        scratch_shapes=[pltpu.VMEM((count, hidden), BF16)],
        compiler_params=params(12),
        cost_estimate=pl.CostEstimate(
            flops=count * features, bytes_accessed=count * features, transcendentals=count
        ),
        name="expert",
    )(rows, gate, up, down)


def halves(block):
    middle = block.shape[0] // 2
    return block[:middle], block[middle:]


def added(*blocks):
    total = blocks[0].astype(F32)
    for block in blocks[1:]:
        total = total + block.astype(F32)
    return total.astype(BF16)


def experts_on_grid(rows, gate, up, down):
    run = functools.partial(expert, gate=gate, up=up, down=down)
    behind = along(rows, 0, 1)
    ahead = along(rows, 0, -1)
    rows_behind = along(rows, 1, 1)
    rows_ahead = along(rows, 1, -1)
    across = jnp.concatenate(
        [along(halves(behind)[0], 0, 1), along(halves(ahead)[1], 0, -1)], axis=0
    )
    own_first = jnp.concatenate([rows, behind], axis=0)
    behind_first = jnp.concatenate([rows_behind, along(behind, 1, 1)], axis=0)
    across, behind_later = lax.optimization_barrier((across, behind))
    own_second = jnp.concatenate([ahead, across], axis=0)
    ahead_second = jnp.concatenate([along(ahead, 1, -1), along(across, 1, -1)], axis=0)
    behind_second = along(own_second, 1, 1)
    ahead_first = jnp.concatenate([rows_ahead, along(behind_later, 1, -1)], axis=0)
    far_first = along(behind_first, 1, 1)
    far_second = along(ahead_second, 1, -1)
    behind_out, ahead_out = run(jnp.concatenate([behind_first, ahead_second], axis=0))
    early_first = along(behind_out, 1, -1)
    early_second = along(ahead_out, 1, 1)
    behind_second, ahead_first, behind_out = lax.optimization_barrier(
        (behind_second, ahead_first, behind_out)
    )
    behind_rest, ahead_rest = run(jnp.concatenate([behind_second, ahead_first], axis=0))
    far_first, far_second, behind_rest = lax.optimization_barrier(
        (far_first, far_second, behind_rest)
    )
    across_first, across_second = run(jnp.concatenate([far_first, far_second], axis=0))
    across_first, across_second, early_first, early_second = lax.optimization_barrier(
        (across_first, across_second, early_first, early_second)
    )
    from_behind = along(across_first, 1, 1)
    from_ahead = along(across_second, 1, -1)
    own_out = run(jnp.concatenate([own_first, own_second], axis=0))
    from_behind, from_ahead, own_out = lax.optimization_barrier((from_behind, from_ahead, own_out))
    late_first = along(added(ahead_rest, from_behind), 1, 1)
    late_second = along(added(behind_rest, from_ahead), 1, -1)
    kept, behind = halves(added(own_out[0], early_first, late_first))
    ahead, across = halves(added(own_out[1], early_second, late_second))
    across_first, across_second = halves(across)
    ahead_first, ahead_second = halves(ahead)
    behind_first, behind_second = halves(behind)
    ahead_first = added(ahead_first, along(across_first, 0, 1))
    behind_second = added(behind_second, along(across_second, 0, -1))
    from_behind = along(jnp.concatenate([ahead_first, ahead_second], axis=0), 0, 1)
    from_ahead = along(jnp.concatenate([behind_first, behind_second], axis=0), 0, -1)
    return added(kept, from_behind, from_ahead)


def device_places():
    owners, seqs = lax.axis_size("exp"), lax.axis_size("seq")
    side, grid_side = owners // 2, math.isqrt(seqs)
    owner = lax.axis_index("exp").astype(jnp.int32)
    place = lax.axis_index("seq").astype(jnp.int32)
    chip, core = owner // 2, owner % 2
    hops = jnp.arange(side, dtype=jnp.int32)
    onward, back = (chip + hops) % side, (chip - hops) % side
    blocks = [onward * 2 + 1 - core, onward * 2 + core, back * 2 + core, back * 2 + 1 - core]
    return jnp.concatenate(blocks + [(place % grid_side)[None], (place // grid_side)[None]])


def mixer(
    places,
    second_core,
    tail,
    x_in,
    z_in,
    conv_weight,
    conv_bias,
    x_proj,
    dt_proj,
    dt_bias,
    a_log,
    d_skip,
    out_proj,
):
    length, channels = x_in.shape
    steps = length // SEG
    owners = lax.axis_size("exp")
    seqs = lax.axis_size("seq")
    side = owners // 2
    swap = [(e, e + 1 - 2 * (e % 2)) for e in range(owners)]

    def along_z(block, hop):
        return lax.ppermute(block, "exp", [(e, (e + 2 * hop) % owners) for e in range(owners)])

    columns = lax.all_gather(out_proj, "seq", axis=0)
    rates = (-jnp.exp(a_log) * LOG2E).T
    rim = passed_along(tail, "seq", 1)
    mixed, send, keep = pl.pallas_call(
        conv_kernel,
        out_shape=(
            jax.ShapeDtypeStruct((length, channels), F32),
            jax.ShapeDtypeStruct((length // 2, RANK + 2 * STATE), F32),
            jax.ShapeDtypeStruct((length // 2, RANK + 2 * STATE), F32),
        ),
        in_specs=[pl.BlockSpec(memory_space=pltpu.SMEM)] + [far()] * 2 + [whole()] * 2,
        out_specs=[whole()] * 3,
        scratch_shapes=[
            pltpu.VMEM(x_in.shape, BF16),
            pltpu.VMEM(x_proj.shape[::-1], BF16),
            pltpu.VMEM((channels // LANES, length + 8, LANES), F32),
            pltpu.VMEM((length, RANK + 2 * STATE), F32),
            pltpu.SemaphoreType.DMA((2,)),
        ],
        compiler_params=params(12),
        name="conv",
    )(places, x_in, x_proj.T, jnp.concatenate([conv_weight, conv_bias[None, :]], axis=0), rim)
    sums = (keep + lax.ppermute(send, "exp", swap)).reshape(side, length // owners, -1)
    summed = sums[0]
    for hop in range(1, side):
        summed = summed + along_z(sums[hop], hop)
    coef = summed[:, RANK:]
    coef_high = coef.astype(BF16)
    coef_low = (coef - coef_high.astype(F32)).astype(BF16)
    near = jnp.concatenate([summed[:, :RANK].astype(BF16), coef_high, coef_low], axis=1)
    near = jnp.concatenate([near] + [along_z(near, hop) for hop in range(1, side)], axis=0)
    other = lax.ppermute(near, "exp", swap)
    packed, message, y_local, delta, before, enter = pl.pallas_call(
        scan_kernel,
        out_shape=(
            jax.ShapeDtypeStruct((length, RANK + 4 * STATE), BF16),
            jax.ShapeDtypeStruct((STATE, channels + LANES), BF16),
            jax.ShapeDtypeStruct((length, channels), F32),
            jax.ShapeDtypeStruct((length, channels), F32),
            jax.ShapeDtypeStruct((SEG, channels), F32),
            jax.ShapeDtypeStruct((STATE, SEG, channels), F32),
        ),
        in_specs=[pl.BlockSpec(memory_space=pltpu.SMEM)] + [whole()] * 4 + [far()] * 2,
        out_specs=[whole()] * 4 + [far()] * 2,
        scratch_shapes=[
            pltpu.VMEM((STATE, length, LANES), F32),
            pltpu.VMEM((STATE, length, LANES), F32),
            pltpu.VMEM(dt_proj.shape, BF16),
            pltpu.VMEM((1, channels), F32),
            pltpu.VMEM((STATE, channels), F32),
            pltpu.VMEM((STATE, LANES), F32),
            pltpu.VMEM((SEG, channels), F32),
            pltpu.VMEM((STATE, SEG, channels), F32),
            pltpu.SemaphoreType.DMA((2,)),
            pltpu.SemaphoreType.DMA((2, channels // LANES)),
        ],
        compiler_params=params(14),
        name="scan",
    )(places, near, other, mixed, rates, dt_proj, dt_bias[None, :])
    totals, prefix = pl.pallas_call(
        meet_kernel,
        out_shape=(
            jax.ShapeDtypeStruct((STATE, channels + LANES), F32),
            jax.ShapeDtypeStruct((STATE + 1, channels), F32),
        ),
        in_specs=[pl.BlockSpec(memory_space=pltpu.SMEM)] + [whole()] * 5,
        out_specs=[whole()] * 2,
        compiler_params=params(4),
        name="meet",
    )(places, message, *ringed(message, "y"), rates)
    lines_before = ringed(totals.astype(BF16), "x")
    gated = pl.pallas_call(
        finish_kernel,
        out_shape=jax.ShapeDtypeStruct((length, channels), BF16),
        in_specs=[pl.BlockSpec(memory_space=pltpu.SMEM)] + [whole()] * 9 + [far()] * 4,
        out_specs=whole(),
        scratch_shapes=[
            pltpu.VMEM((SEG, channels), F32),
            pltpu.VMEM((STATE, SEG, channels), F32),
            pltpu.VMEM((1, channels), F32),
            pltpu.VMEM((length, channels), BF16),
            pltpu.VMEM((STATE, length, LANES), F32),
            pltpu.VMEM((channels // LANES, length, LANES), F32),
            pltpu.VMEM((channels // LANES, length, LANES), F32),
            pltpu.VMEM((STATE, channels), F32),
            pltpu.SemaphoreType.DMA((4,)),
        ],
        compiler_params=params(16),
        name="finish",
    )(
        places,
        prefix,
        *lines_before,
        rates,
        delta,
        packed,
        y_local,
        mixed,
        before,
        enter,
        d_skip[None, :],
        z_in,
    )
    width = out_proj.shape[1]
    features = seqs * width
    send, keep = pl.pallas_call(
        outward_kernel,
        out_shape=(
            jax.ShapeDtypeStruct((length // 2, features), BF16),
            jax.ShapeDtypeStruct((length // 2, features), F32),
        ),
        in_specs=[whole(), far()],
        out_specs=[whole()] * 2,
        scratch_shapes=[
            pltpu.VMEM((channels, features), BF16),
            pltpu.SemaphoreType.DMA((seqs,)),
        ],
        compiler_params=params(50),
        name="outward",
    )(gated, columns)
    sums = keep + lax.ppermute(send, "exp", swap).astype(F32)
    sums = sums.reshape(side, length // owners, features)
    route = [(e, (e + (4 if e % 2 == 0 else -2)) % owners) for e in range(owners)]
    opposite = lax.ppermute(sums[2].astype(BF16), "exp", route).astype(F32)
    first = along_z(sums[1].astype(BF16), 1).astype(F32)
    last = along_z((sums[3] + opposite * second_core).astype(BF16), 3).astype(F32)
    return sums[0] + first + last + opposite * (1.0 - second_core)


def shards(
    x_in,
    z_in,
    conv_weight,
    conv_bias,
    x_proj,
    dt_proj,
    dt_bias,
    a_log,
    d_skip,
    out_proj,
    residual,
    expert_ids,
    gate_weights,
    w_gate,
    w_up,
    w_down,
):
    owners = lax.axis_size("exp")
    tok_rows = residual.shape[0]
    capacity = max(2, tok_rows // 4)
    slots = owners * capacity
    chosen_count = expert_ids.shape[1]
    flat_ids = expert_ids.reshape(-1)
    hits = (flat_ids[:, None] == jnp.arange(owners, dtype=jnp.int32)[None, :]).astype(jnp.int32)
    before = jnp.cumsum(hits, axis=0) - hits
    ranked = jnp.sum(before * hits, axis=1)
    valid = jnp.sum(hits, axis=1)
    target = flat_ids * capacity + ranked
    placed = (
        (target[:, None] == jnp.arange(slots, dtype=jnp.int32)[None, :]) & (valid[:, None] > 0)
    ).astype(jnp.float32)
    dispatch_table = jnp.sum(placed.reshape(tok_rows, chosen_count, slots), axis=1)
    combine_table = jnp.sum(
        (placed * gate_weights.reshape(-1)[:, None]).reshape(tok_rows, chosen_count, slots), axis=1
    )
    second_core = jnp.broadcast_to((lax.axis_index("exp") % 2).astype(F32), (1, residual.shape[1]))
    tail, places, second_core, dispatch_table, combine_table = lax.optimization_barrier(
        (
            x_in[-(CONV - 1) :],
            device_places(),
            second_core,
            dispatch_table.astype(BF16),
            combine_table,
        )
    )
    mixed = mixer(
        places,
        second_core,
        tail,
        x_in,
        z_in,
        conv_weight,
        conv_bias,
        x_proj,
        dt_proj,
        dt_bias,
        a_log,
        d_skip,
        out_proj,
    )
    hidden = residual.astype(jnp.float32) + mixed
    normed = (hidden * lax.rsqrt(jnp.mean(hidden * hidden, axis=-1, keepdims=True) + 1e-06)).astype(
        jnp.bfloat16
    )
    outgoing = jnp.einsum(
        "ts,td->sd", dispatch_table, normed, preferred_element_type=jnp.float32
    )
    outgoing = outgoing.astype(jnp.bfloat16).reshape(owners, capacity, -1)
    arrived = lax.all_to_all(outgoing, "exp", split_axis=0, concat_axis=0, tiled=True)
    summed = experts_on_grid(arrived.reshape(slots, -1), w_gate[0], w_up[0], w_down[0])
    expert_out = summed.reshape(owners, capacity, -1)
    returned_rows = lax.all_to_all(
        expert_out, "exp", split_axis=0, concat_axis=0, tiled=True
    ).reshape(slots, -1)
    combined = jnp.dot(
        combine_table, returned_rows.astype(jnp.float32), precision=lax.Precision.HIGHEST
    )
    return hidden + combined


def solution(mesh):
    placed = (
        P("seq", "exp"),
        P("seq", "exp"),
        P(None, "exp"),
        P("exp"),
        P("exp", None),
        P(None, "exp"),
        P("exp"),
        P("exp", None),
        P("exp"),
        P("exp", "seq"),
        P(("seq", "exp"), None),
        P(("seq", "exp"), None),
        P(("seq", "exp"), None),
        P("exp", None, "seq"),
        P("exp", None, "seq"),
        P("exp", "seq", None),
    )
    return jax.shard_map(
        shards, mesh=mesh, in_specs=placed, out_specs=P(("seq", "exp"), None), check_vma=False
    )
```

```python
import functools
import math

import jax
import jax.numpy as jnp
from jax import lax
from jax.experimental import pallas as pl
from jax.experimental.pallas import tpu as pltpu
from jax.sharding import PartitionSpec as P

RANK = 256
STATE = 16
CONV = 4
SEG = 8
LANES = 128
LOG2E = math.log2(math.e)
F32 = jnp.float32
BF16 = jnp.bfloat16
MIB = 1024 * 1024


def whole():
    return pl.BlockSpec(memory_space=pltpu.VMEM)


def far():
    return pl.BlockSpec(memory_space=pltpu.HBM)


def params(mib):
    return pltpu.CompilerParams(vmem_limit_bytes=mib * MIB)


def lines(stage):
    side = math.isqrt(lax.axis_size("seq"))
    owners = lax.axis_size("exp")
    groups = []
    for owner in range(owners):
        along_x = (owner % 2 == 0) == (stage == 0)
        for fixed in range(side):
            members = [(m * side + fixed if along_x else fixed * side + m) for m in range(side)]
            groups.append([m * owners + owner for m in members])
    return groups


def along(block, stage, distance):
    route = []
    for members in lines(stage):
        count = len(members)
        route += [(members[i], members[(i + distance) % count]) for i in range(count)]
    return lax.ppermute(block, ("seq", "exp"), route)


def passed_along(block, axis, distance):
    devices = range(lax.axis_size(axis))
    route = [(i - distance, i) for i in devices if i - distance in devices]
    return lax.ppermute(block, axis, route)


def conv_kernel(
    places_ref,
    x_hbm,
    proj_hbm,
    weight_ref,
    rim_ref,
    mixed_ref,
    send_ref,
    keep_ref,
    x_ref,
    proj_ref,
    padded,
    part_ref,
    sems,
):
    sources = (x_hbm, proj_hbm)
    targets = (x_ref, proj_ref)
    copies = [pltpu.make_async_copy(*pair, sems.at[k]) for k, pair in enumerate(zip(sources, targets))]
    for copy in copies:
        copy.start()
    length, channels = x_ref.shape
    steps = length // SEG
    head = 8
    copies[0].wait()
    for lane in range(0, channels, LANES):
        block = padded.at[lane // LANES]
        block[head - (CONV - 1) : head, :] = rim_ref[:, lane : lane + LANES].astype(F32)
        block[head:, :] = x_ref[:, lane : lane + LANES].astype(F32)

    def step(i, carry):
        rows = pl.ds(pl.multiple_of(i * SEG, SEG), SEG)
        for lane in range(0, channels, LANES):
            lanes = pl.ds(lane, LANES)
            acc = jnp.broadcast_to(weight_ref[CONV : CONV + 1, lanes], (SEG, LANES))
            for tap in range(CONV):
                taken = padded[
                    lane // LANES, pl.ds(i + head - (CONV - 1) + tap, SEG, stride=steps), :
                ]
                acc = acc + weight_ref[tap : tap + 1, lanes] * taken
            mixed_ref[rows, lanes] = (acc * jax.nn.sigmoid(acc)).astype(BF16).astype(F32)
        return carry

    lax.fori_loop(0, steps, step, 0)
    copies[1].wait()
    part_ref[...] = lax.dot_general(
        mixed_ref[...].astype(BF16),
        proj_ref[...],
        (((1,), (1,)), ((), ())),
        preferred_element_type=F32,
    )
    half = SEG // 2
    for spot in range(SEG):
        rows = pl.ds(pl.multiple_of(places_ref[spot] * steps, steps), steps)
        target = send_ref if spot < half else keep_ref
        first = spot % half * steps
        target[first : first + steps, :] = part_ref[rows, :]


def spread(target, packed_ref, first):
    packed = packed_ref[...].astype(F32)
    coef = packed[:, RANK : RANK + 2 * STATE] + packed[:, RANK + 2 * STATE :]
    for n in range(STATE):
        target[n] = jnp.broadcast_to(coef[:, first + n : first + n + 1], (coef.shape[0], LANES))


def scan_kernel(
    places_ref,
    near_ref,
    other_ref,
    mixed_ref,
    rates_ref,
    proj_hbm,
    bias_hbm,
    packed_ref,
    msg_ref,
    y_ref,
    delta_ref,
    before_hbm,
    enter_hbm,
    b_wide,
    c_wide,
    proj_ref,
    bias_ref,
    ends_ref,
    deltas_ref,
    before_ref,
    enter_ref,
    in_sems,
    out_sems,
):
    length, channels = mixed_ref.shape
    steps = length // SEG
    copies = [
        pltpu.make_async_copy(proj_hbm, proj_ref, in_sems.at[0]),
        pltpu.make_async_copy(bias_hbm, bias_ref, in_sems.at[1]),
    ]
    for copy in copies:
        copy.start()
    half = SEG // 2
    for place in range(half):
        taken = slice(place * steps, (place + 1) * steps)
        for source, slot in ((near_ref, place), (other_ref, place + half)):
            rows = pl.ds(pl.multiple_of(places_ref[SEG + slot] * steps, steps), steps)
            packed_ref[rows, :] = source[taken, :]
    spread(b_wide, packed_ref, 0)
    spread(c_wide, packed_ref, STATE)
    for copy in copies:
        copy.wait()
    copies = []
    raw = jnp.dot(packed_ref[:, :RANK], proj_ref[...], preferred_element_type=F32) + bias_ref[...]
    delta_ref[...] = jnp.maximum(raw, 0.0) + jnp.log1p(jnp.exp(-jnp.abs(raw)))
    row = lax.broadcasted_iota(jnp.int32, (SEG, LANES), 0)

    def shifted(value, by, fill):
        return jnp.where(row < by, fill, pltpu.roll(value, by, axis=0))

    for lane in range(0, channels, LANES):
        lanes = pl.ds(lane, LANES)
        rates = [
            jnp.broadcast_to(rates_ref[n : n + 1, lanes], (SEG, LANES)) for n in range(STATE)
        ]

        def step(i, carry):
            elapsed, states = carry
            rows = pl.ds(pl.multiple_of(i * SEG, SEG), SEG)
            delta = delta_ref[rows, lanes]
            drive = delta * mixed_ref[rows, lanes]
            fresh, terms = [], []
            for n in range(STATE):
                state = jnp.exp2(delta * rates[n]) * states[n] + drive * b_wide[n, rows, :]
                fresh.append(state)
                terms.append(state * c_wide[n, rows, :])
            while len(terms) > 1:
                terms = [a + b for a, b in zip(terms[::2], terms[1::2])]
            y_ref[rows, lanes] = terms[0]
            return elapsed + delta, tuple(fresh)

        zero = jnp.zeros((SEG, LANES), F32)
        elapsed, states = lax.fori_loop(0, steps, step, (zero, (zero,) * STATE), unroll=2)
        total = elapsed
        for by in (1, 2, 4):
            total = total + shifted(total, by, 0.0)
        before_ref[:, lanes] = shifted(total, 1, 0.0)
        last = total[SEG - 1 : SEG, :]
        for n in range(STATE):
            decay = jnp.exp2(elapsed * rates[n])
            state = states[n]
            for by in (1, 2, 4):
                state = decay * shifted(state, by, 0.0) + state
                decay = decay * shifted(decay, by, 1.0)
            enter_ref[n, :, lanes] = shifted(state, 1, 0.0)
            ends_ref[n : n + 1, lanes] = state[SEG - 1 : SEG, :]
        block = lane // LANES
        high = last.astype(BF16).astype(F32)
        deltas_ref[block : block + 1, :] = high
        deltas_ref[SEG + block : SEG + block + 1, :] = last - high
        fresh = [
            pltpu.make_async_copy(
                before_ref.at[:, lanes], before_hbm.at[:, lanes], out_sems.at[0, block]
            ),
            pltpu.make_async_copy(
                enter_ref.at[:, :, lanes], enter_hbm.at[:, :, lanes], out_sems.at[1, block]
            ),
        ]
        for copy in fresh:
            copy.start()
        copies += fresh
    msg_ref[:, :channels] = ends_ref[...].astype(BF16)
    msg_ref[:, channels:] = deltas_ref[...].astype(BF16)
    for copy in copies:
        copy.wait()


def unpacked(message, block):
    lanes = slice(block * LANES, (block + 1) * LANES)
    tail = message[:, message.shape[1] - LANES :].astype(F32)
    delta = tail[block : block + 1] + tail[SEG + block : SEG + block + 1]
    return message[:, lanes].astype(F32), delta


def joined(run, later, rates, chosen):
    state, delta = run
    more, more_delta = later
    state = jnp.where(chosen, jnp.exp2(more_delta * rates) * state + more, state)
    return state, jnp.where(chosen, delta + more_delta, delta)


def meet_kernel(places_ref, own_ref, third_ref, second_ref, first_ref, rates_ref, msg_ref, prefix_ref):
    place = places_ref[2 * SEG]
    channels = rates_ref.shape[1]
    for block in range(channels // LANES):
        lanes = slice(block * LANES, (block + 1) * LANES)
        rates = rates_ref[:, lanes]
        others = [
            (hops, unpacked(ref[...], block))
            for hops, ref in ((3, third_ref), (2, second_ref), (1, first_ref))
        ]
        run = (jnp.zeros((STATE, LANES), F32), jnp.zeros((1, LANES), F32))
        for hops, message in others:
            run = joined(run, message, rates, hops <= place)
        prefix_ref[:STATE, lanes] = run[0]
        prefix_ref[STATE : STATE + 1, lanes] = run[1]
        run = joined(run, unpacked(own_ref[...], block), rates, place >= 0)
        for hops, message in others:
            run = joined(run, message, rates, hops > place)
        state, delta = run
        high = delta.astype(BF16).astype(F32)
        msg_ref[:STATE, lanes] = state
        msg_ref[block : block + 1, channels:] = high
        msg_ref[SEG + block : SEG + block + 1, channels:] = delta - high


def ringed(message, axis):
    seqs = lax.axis_size("seq")
    side = math.isqrt(seqs)
    got = []
    for hops in range(1, side):
        route = []
        for i in range(seqs):
            x, y = i // side, i % side
            target = ((x + hops) % side, y) if axis == "x" else (x, (y + hops) % side)
            route.append((i, target[0] * side + target[1]))
        got.append(lax.ppermute(message, "seq", route))
    return got[::-1]


def finish_kernel(
    places_ref,
    prefix_ref,
    third_ref,
    second_ref,
    first_ref,
    rates_ref,
    delta_ref,
    packed_ref,
    y_ref,
    mixed_ref,
    before_hbm,
    enter_hbm,
    skip_hbm,
    z_hbm,
    gated_ref,
    before_ref,
    enter_ref,
    skip_ref,
    z_ref,
    c_wide,
    z_wide,
    gated,
    entering_ref,
    sems,
):
    length, channels = mixed_ref.shape
    steps = length // SEG
    sources = (before_hbm, enter_hbm, skip_hbm, z_hbm)
    targets = (before_ref, enter_ref, skip_ref, z_ref)
    copies = [pltpu.make_async_copy(*pair, sems.at[k]) for k, pair in enumerate(zip(sources, targets))]
    for copy in copies:
        copy.start()
    place = places_ref[2 * SEG + 1]
    for block in range(channels // LANES):
        lanes = slice(block * LANES, (block + 1) * LANES)
        rates = rates_ref[:, lanes]
        run = (jnp.zeros((STATE, LANES), F32), jnp.zeros((1, LANES), F32))
        for hops, ref in ((3, third_ref), (2, second_ref), (1, first_ref)):
            run = joined(run, unpacked(ref[...], block), rates, hops <= place)
        near = (prefix_ref[:STATE, lanes], prefix_ref[STATE : STATE + 1, lanes])
        entering_ref[:, lanes] = joined(run, near, rates, place >= 0)[0]
    spread(c_wide, packed_ref, STATE)
    for copy in copies:
        copy.wait()
    for lane in range(0, channels, LANES):
        z_wide[lane // LANES] = z_ref[:, lane : lane + LANES].astype(F32)

    for lane in range(0, channels, LANES):
        lanes = pl.ds(lane, LANES)
        rates = [
            jnp.broadcast_to(rates_ref[n : n + 1, lanes], (SEG, LANES)) for n in range(STATE)
        ]
        before = before_ref[:, lanes]
        held = [
            jnp.exp2(before * rates[n]) * entering_ref[n : n + 1, lanes] + enter_ref[n, :, lanes]
            for n in range(STATE)
        ]
        skip = skip_ref[:, lanes]

        def step(i, elapsed):
            rows = pl.ds(pl.multiple_of(i * SEG, SEG), SEG)
            apart = pl.ds(i, SEG, stride=steps)
            elapsed = elapsed + delta_ref[rows, lanes]
            terms = [
                jnp.exp2(elapsed * rates[n]) * held[n] * c_wide[n, rows, :] for n in range(STATE)
            ]
            while len(terms) > 1:
                terms = [a + b for a, b in zip(terms[::2], terms[1::2])]
            output = y_ref[rows, lanes] + terms[0] + skip * mixed_ref[rows, lanes]
            z = z_wide[lane // LANES, apart, :]
            gated[lane // LANES, apart, :] = output * (z * jax.nn.sigmoid(z))
            return elapsed

        lax.fori_loop(0, steps, step, jnp.zeros((SEG, LANES), F32), unroll=2)
    for spot in range(SEG):
        rows = pl.ds(pl.multiple_of(places_ref[spot] * steps, steps), steps)
        for lane in range(0, channels, LANES):
            gated_ref[spot * steps : (spot + 1) * steps, lane : lane + LANES] = gated[
                lane // LANES, rows, :
            ].astype(BF16)


def outward_kernel(gated_ref, proj_hbm, send_ref, keep_ref, proj, arrived):
    parts, _, width = proj_hbm.shape
    middle = send_ref.shape[0]
    group = 4

    def fetch(part):
        columns = pl.ds(pl.multiple_of(part * width, width), width)
        return pltpu.make_async_copy(proj_hbm.at[part], proj.at[:, columns], arrived.at[part])

    for part in range(2 * group):
        fetch(part).start()

    def product(step, carry):
        for part in range(group):
            fetch(step * group + part).wait()

        @pl.when(step < parts // group - 2)
        def _():
            for part in range(group):
                fetch((step + 2) * group + part).start()

        wide = group * width
        columns = pl.ds(pl.multiple_of(step * wide, wide), wide)
        terms = jnp.dot(gated_ref[...], proj[:, columns], preferred_element_type=F32)
        send_ref[:, columns] = terms[:middle].astype(BF16)
        keep_ref[:, columns] = terms[middle:]
        return carry

    lax.fori_loop(0, parts // group, product, 0)


def expert_kernel(rows_ref, gate_ref, up_ref, down_ref, first_ref, second_ref, inner):
    tile = 1024
    middle = first_ref.shape[0]
    gate = jnp.dot(rows_ref[...], gate_ref[...], preferred_element_type=F32)
    upper = jnp.dot(rows_ref[...], up_ref[...], preferred_element_type=F32)
    inner[...] = (gate * jax.nn.sigmoid(gate) * upper).astype(BF16)

    def narrow(part, carry):
        columns = pl.ds(pl.multiple_of(part * tile, tile), tile)
        piece = jnp.dot(inner[...], down_ref[:, columns], preferred_element_type=F32)
        first_ref[:, columns] = piece[:middle].astype(BF16)
        second_ref[:, columns] = piece[middle:].astype(BF16)
        return carry

    lax.fori_loop(0, first_ref.shape[1] // tile, narrow, 0, unroll=2)


def expert(rows, gate, up, down):
    count, features = rows.shape
    hidden = gate.shape[1]
    return pl.pallas_call(
        expert_kernel,
        out_shape=(jax.ShapeDtypeStruct((count // 2, features), BF16),) * 2,
        in_specs=[whole()] * 4,
        out_specs=[whole()] * 2,
        scratch_shapes=[pltpu.VMEM((count, hidden), BF16)],
        compiler_params=params(12),
        cost_estimate=pl.CostEstimate(
            flops=count * features, bytes_accessed=count * features, transcendentals=count
        ),
        name="expert",
    )(rows, gate, up, down)


def halves(block):
    middle = block.shape[0] // 2
    return block[:middle], block[middle:]


def added(*blocks):
    total = blocks[0].astype(F32)
    for block in blocks[1:]:
        total = total + block.astype(F32)
    return total.astype(BF16)


def experts_on_grid(rows, gate, up, down):
    run = functools.partial(expert, gate=gate, up=up, down=down)
    behind = along(rows, 0, 1)
    ahead = along(rows, 0, -1)
    across = jnp.concatenate(
        [along(halves(behind)[0], 0, 1), along(halves(ahead)[1], 0, -1)], axis=0
    )
    own_first = jnp.concatenate([rows, behind], axis=0)
    behind_first = along(own_first, 1, 1)
    across, own_first_later = lax.optimization_barrier((across, own_first))
    own_second = jnp.concatenate([ahead, across], axis=0)
    ahead_second = jnp.concatenate([along(ahead, 1, -1), along(across, 1, -1)], axis=0)
    behind_second = along(own_second, 1, 1)
    ahead_first = along(own_first_later, 1, -1)
    far_first = along(behind_first, 1, 1)
    far_second = along(ahead_second, 1, -1)
    behind_out, ahead_out = run(jnp.concatenate([behind_first, ahead_second], axis=0))
    early_first = along(behind_out, 1, -1)
    early_second = along(ahead_out, 1, 1)
    behind_second, ahead_first, behind_out = lax.optimization_barrier(
        (behind_second, ahead_first, behind_out)
    )
    behind_rest, ahead_rest = run(jnp.concatenate([behind_second, ahead_first], axis=0))
    far_first, far_second, behind_rest = lax.optimization_barrier(
        (far_first, far_second, behind_rest)
    )
    across_first, across_second = run(jnp.concatenate([far_first, far_second], axis=0))
    from_behind = along(across_first, 1, 1)
    from_ahead = along(across_second, 1, -1)
    own_out = run(jnp.concatenate([own_first, own_second], axis=0))
    from_behind, from_ahead, early_first, early_second, own_out = lax.optimization_barrier(
        (from_behind, from_ahead, early_first, early_second, own_out)
    )
    late_first = along(added(ahead_rest, from_behind), 1, 1)
    late_second = along(added(behind_rest, from_ahead), 1, -1)
    kept, behind = halves(added(own_out[0], early_first, late_first))
    ahead, across = halves(added(own_out[1], early_second, late_second))
    across_first, across_second = halves(across)
    ahead_first, ahead_second = halves(ahead)
    behind_first, behind_second = halves(behind)
    ahead_first = added(ahead_first, along(across_first, 0, 1))
    behind_second = added(behind_second, along(across_second, 0, -1))
    from_behind = along(jnp.concatenate([ahead_first, ahead_second], axis=0), 0, 1)
    from_ahead = along(jnp.concatenate([behind_first, behind_second], axis=0), 0, -1)
    return added(kept, from_behind, from_ahead)


def device_places():
    owners, seqs = lax.axis_size("exp"), lax.axis_size("seq")
    side, grid_side = owners // 2, math.isqrt(seqs)
    owner = lax.axis_index("exp").astype(jnp.int32)
    place = lax.axis_index("seq").astype(jnp.int32)
    chip, core = owner // 2, owner % 2
    hops = jnp.arange(side, dtype=jnp.int32)
    onward, back = (chip + hops) % side, (chip - hops) % side
    blocks = [onward * 2 + 1 - core, onward * 2 + core, back * 2 + core, back * 2 + 1 - core]
    return jnp.concatenate(blocks + [(place % grid_side)[None], (place // grid_side)[None]])


def mixer(
    places,
    tail,
    x_in,
    z_in,
    conv_weight,
    conv_bias,
    x_proj,
    dt_proj,
    dt_bias,
    a_log,
    d_skip,
    out_proj,
):
    length, channels = x_in.shape
    steps = length // SEG
    owners = lax.axis_size("exp")
    seqs = lax.axis_size("seq")
    side = owners // 2
    swap = [(e, e + 1 - 2 * (e % 2)) for e in range(owners)]

    def along_z(block, hop):
        return lax.ppermute(block, "exp", [(e, (e + 2 * hop) % owners) for e in range(owners)])

    columns = lax.all_gather(out_proj, "seq", axis=0)
    rates = (-jnp.exp(a_log) * LOG2E).T
    rim = passed_along(tail, "seq", 1)
    mixed, send, keep = pl.pallas_call(
        conv_kernel,
        out_shape=(
            jax.ShapeDtypeStruct((length, channels), F32),
            jax.ShapeDtypeStruct((length // 2, RANK + 2 * STATE), F32),
            jax.ShapeDtypeStruct((length // 2, RANK + 2 * STATE), F32),
        ),
        in_specs=[pl.BlockSpec(memory_space=pltpu.SMEM)] + [far()] * 2 + [whole()] * 2,
        out_specs=[whole()] * 3,
        scratch_shapes=[
            pltpu.VMEM(x_in.shape, BF16),
            pltpu.VMEM(x_proj.shape[::-1], BF16),
            pltpu.VMEM((channels // LANES, length + 8, LANES), F32),
            pltpu.VMEM((length, RANK + 2 * STATE), F32),
            pltpu.SemaphoreType.DMA((2,)),
        ],
        compiler_params=params(12),
        name="conv",
    )(places, x_in, x_proj.T, jnp.concatenate([conv_weight, conv_bias[None, :]], axis=0), rim)
    sums = (keep + lax.ppermute(send, "exp", swap)).reshape(side, length // owners, -1)
    summed = sums[0]
    for hop in range(1, side):
        summed = summed + along_z(sums[hop], hop)
    coef = summed[:, RANK:]
    coef_high = coef.astype(BF16)
    coef_low = (coef - coef_high.astype(F32)).astype(BF16)
    near = jnp.concatenate([summed[:, :RANK].astype(BF16), coef_high, coef_low], axis=1)
    near = jnp.concatenate([near] + [along_z(near, hop) for hop in range(1, side)], axis=0)
    other = lax.ppermute(near, "exp", swap)
    packed, message, y_local, delta, before, enter = pl.pallas_call(
        scan_kernel,
        out_shape=(
            jax.ShapeDtypeStruct((length, RANK + 4 * STATE), BF16),
            jax.ShapeDtypeStruct((STATE, channels + LANES), BF16),
            jax.ShapeDtypeStruct((length, channels), F32),
            jax.ShapeDtypeStruct((length, channels), F32),
            jax.ShapeDtypeStruct((SEG, channels), F32),
            jax.ShapeDtypeStruct((STATE, SEG, channels), F32),
        ),
        in_specs=[pl.BlockSpec(memory_space=pltpu.SMEM)] + [whole()] * 4 + [far()] * 2,
        out_specs=[whole()] * 4 + [far()] * 2,
        scratch_shapes=[
            pltpu.VMEM((STATE, length, LANES), F32),
            pltpu.VMEM((STATE, length, LANES), F32),
            pltpu.VMEM(dt_proj.shape, BF16),
            pltpu.VMEM((1, channels), F32),
            pltpu.VMEM((STATE, channels), F32),
            pltpu.VMEM((STATE, LANES), F32),
            pltpu.VMEM((SEG, channels), F32),
            pltpu.VMEM((STATE, SEG, channels), F32),
            pltpu.SemaphoreType.DMA((2,)),
            pltpu.SemaphoreType.DMA((2, channels // LANES)),
        ],
        compiler_params=params(14),
        name="scan",
    )(places, near, other, mixed, rates, dt_proj, dt_bias[None, :])
    totals, prefix = pl.pallas_call(
        meet_kernel,
        out_shape=(
            jax.ShapeDtypeStruct((STATE, channels + LANES), F32),
            jax.ShapeDtypeStruct((STATE + 1, channels), F32),
        ),
        in_specs=[pl.BlockSpec(memory_space=pltpu.SMEM)] + [whole()] * 5,
        out_specs=[whole()] * 2,
        compiler_params=params(4),
        name="meet",
    )(places, message, *ringed(message, "y"), rates)
    lines_before = ringed(totals.astype(BF16), "x")
    gated = pl.pallas_call(
        finish_kernel,
        out_shape=jax.ShapeDtypeStruct((length, channels), BF16),
        in_specs=[pl.BlockSpec(memory_space=pltpu.SMEM)] + [whole()] * 9 + [far()] * 4,
        out_specs=whole(),
        scratch_shapes=[
            pltpu.VMEM((SEG, channels), F32),
            pltpu.VMEM((STATE, SEG, channels), F32),
            pltpu.VMEM((1, channels), F32),
            pltpu.VMEM((length, channels), BF16),
            pltpu.VMEM((STATE, length, LANES), F32),
            pltpu.VMEM((channels // LANES, length, LANES), F32),
            pltpu.VMEM((channels // LANES, length, LANES), F32),
            pltpu.VMEM((STATE, channels), F32),
            pltpu.SemaphoreType.DMA((4,)),
        ],
        compiler_params=params(16),
        name="finish",
    )(
        places,
        prefix,
        *lines_before,
        rates,
        delta,
        packed,
        y_local,
        mixed,
        before,
        enter,
        d_skip[None, :],
        z_in,
    )
    width = out_proj.shape[1]
    features = seqs * width
    send, keep = pl.pallas_call(
        outward_kernel,
        out_shape=(
            jax.ShapeDtypeStruct((length // 2, features), BF16),
            jax.ShapeDtypeStruct((length // 2, features), F32),
        ),
        in_specs=[whole(), far()],
        out_specs=[whole()] * 2,
        scratch_shapes=[
            pltpu.VMEM((channels, features), BF16),
            pltpu.SemaphoreType.DMA((seqs,)),
        ],
        compiler_params=params(50),
        name="outward",
    )(gated, columns)
    sums = keep + lax.ppermute(send, "exp", swap).astype(F32)
    sums = sums.reshape(side, length // owners, features)
    total = sums[0]
    for hop in range(1, side):
        total = total + along_z(sums[hop].astype(BF16), hop).astype(F32)
    return total


def shards(
    x_in,
    z_in,
    conv_weight,
    conv_bias,
    x_proj,
    dt_proj,
    dt_bias,
    a_log,
    d_skip,
    out_proj,
    residual,
    expert_ids,
    gate_weights,
    w_gate,
    w_up,
    w_down,
):
    owners = lax.axis_size("exp")
    tok_rows = residual.shape[0]
    capacity = max(2, tok_rows // 4)
    slots = owners * capacity
    chosen_count = expert_ids.shape[1]
    flat_ids = expert_ids.reshape(-1)
    hits = (flat_ids[:, None] == jnp.arange(owners, dtype=jnp.int32)[None, :]).astype(jnp.int32)
    before = jnp.cumsum(hits, axis=0) - hits
    ranked = jnp.sum(before * hits, axis=1)
    valid = jnp.sum(hits, axis=1)
    target = flat_ids * capacity + ranked
    placed = (
        (target[:, None] == jnp.arange(slots, dtype=jnp.int32)[None, :]) & (valid[:, None] > 0)
    ).astype(jnp.float32)
    dispatch_table = jnp.sum(placed.reshape(tok_rows, chosen_count, slots), axis=1)
    combine_table = jnp.sum(
        (placed * gate_weights.reshape(-1)[:, None]).reshape(tok_rows, chosen_count, slots), axis=1
    )
    tail, places, dispatch_table, combine_table = lax.optimization_barrier(
        (x_in[-(CONV - 1) :], device_places(), dispatch_table.astype(BF16), combine_table)
    )
    mixed = mixer(
        places,
        tail,
        x_in,
        z_in,
        conv_weight,
        conv_bias,
        x_proj,
        dt_proj,
        dt_bias,
        a_log,
        d_skip,
        out_proj,
    )
    hidden = residual.astype(jnp.float32) + mixed
    normed = (hidden * lax.rsqrt(jnp.mean(hidden * hidden, axis=-1, keepdims=True) + 1e-06)).astype(
        jnp.bfloat16
    )
    outgoing = jnp.einsum(
        "ts,td->sd", dispatch_table, normed, preferred_element_type=jnp.float32
    )
    outgoing = outgoing.astype(jnp.bfloat16).reshape(owners, capacity, -1)
    arrived = lax.all_to_all(outgoing, "exp", split_axis=0, concat_axis=0, tiled=True)
    summed = experts_on_grid(arrived.reshape(slots, -1), w_gate[0], w_up[0], w_down[0])
    expert_out = summed.reshape(owners, capacity, -1)
    returned_rows = lax.all_to_all(
        expert_out, "exp", split_axis=0, concat_axis=0, tiled=True
    ).reshape(slots, -1)
    combined = jnp.dot(
        combine_table, returned_rows.astype(jnp.float32), precision=lax.Precision.HIGHEST
    )
    return hidden + combined


def solution(mesh):
    placed = (
        P("seq", "exp"),
        P("seq", "exp"),
        P(None, "exp"),
        P("exp"),
        P("exp", None),
        P(None, "exp"),
        P("exp"),
        P("exp", None),
        P("exp"),
        P("exp", "seq"),
        P(("seq", "exp"), None),
        P(("seq", "exp"), None),
        P(("seq", "exp"), None),
        P("exp", None, "seq"),
        P("exp", None, "seq"),
        P("exp", "seq", None),
    )
    return jax.shard_map(
        shards, mesh=mesh, in_specs=placed, out_specs=P(("seq", "exp"), None), check_vma=False
    )
```

```python
import functools
import math

import jax
import jax.numpy as jnp
from jax import lax
from jax.experimental import pallas as pl
from jax.experimental.pallas import tpu as pltpu
from jax.sharding import PartitionSpec as P

RANK = 256
STATE = 16
CONV = 4
SEG = 8
LANES = 128
LOG2E = math.log2(math.e)
F32 = jnp.float32
BF16 = jnp.bfloat16
MIB = 1024 * 1024


def whole():
    return pl.BlockSpec(memory_space=pltpu.VMEM)


def far():
    return pl.BlockSpec(memory_space=pltpu.HBM)


def params(mib):
    return pltpu.CompilerParams(vmem_limit_bytes=mib * MIB)


def lines(stage):
    side = math.isqrt(lax.axis_size("seq"))
    owners = lax.axis_size("exp")
    groups = []
    for owner in range(owners):
        along_x = (owner % 2 == 0) == (stage == 0)
        for fixed in range(side):
            members = [(m * side + fixed if along_x else fixed * side + m) for m in range(side)]
            groups.append([m * owners + owner for m in members])
    return groups


def along(block, stage, distance):
    route = []
    for members in lines(stage):
        count = len(members)
        route += [(members[i], members[(i + distance) % count]) for i in range(count)]
    return lax.ppermute(block, ("seq", "exp"), route)


def passed_along(block, axis, distance):
    devices = range(lax.axis_size(axis))
    route = [(i - distance, i) for i in devices if i - distance in devices]
    return lax.ppermute(block, axis, route)


def conv_kernel(
    places_ref,
    x_hbm,
    proj_hbm,
    weight_ref,
    rim_ref,
    mixed_ref,
    send_ref,
    keep_ref,
    x_ref,
    proj_ref,
    padded,
    part_ref,
    sems,
):
    sources = (x_hbm, proj_hbm)
    targets = (x_ref, proj_ref)
    copies = [pltpu.make_async_copy(*pair, sems.at[k]) for k, pair in enumerate(zip(sources, targets))]
    for copy in copies:
        copy.start()
    length, channels = x_ref.shape
    steps = length // SEG
    head = 8
    copies[0].wait()
    for lane in range(0, channels, LANES):
        block = padded.at[lane // LANES]
        block[head - (CONV - 1) : head, :] = rim_ref[:, lane : lane + LANES].astype(F32)
        block[head:, :] = x_ref[:, lane : lane + LANES].astype(F32)

    def step(i, carry):
        rows = pl.ds(pl.multiple_of(i * SEG, SEG), SEG)
        for lane in range(0, channels, LANES):
            lanes = pl.ds(lane, LANES)
            acc = jnp.broadcast_to(weight_ref[CONV : CONV + 1, lanes], (SEG, LANES))
            for tap in range(CONV):
                taken = padded[
                    lane // LANES, pl.ds(i + head - (CONV - 1) + tap, SEG, stride=steps), :
                ]
                acc = acc + weight_ref[tap : tap + 1, lanes] * taken
            mixed_ref[rows, lanes] = (acc * jax.nn.sigmoid(acc)).astype(BF16).astype(F32)
        return carry

    lax.fori_loop(0, steps, step, 0)
    copies[1].wait()
    part_ref[...] = lax.dot_general(
        mixed_ref[...].astype(BF16),
        proj_ref[...],
        (((1,), (1,)), ((), ())),
        preferred_element_type=F32,
    )
    half = SEG // 2
    for spot in range(SEG):
        rows = pl.ds(pl.multiple_of(places_ref[spot] * steps, steps), steps)
        target = send_ref if spot < half else keep_ref
        first = spot % half * steps
        target[first : first + steps, :] = part_ref[rows, :]


def spread(target, packed_ref, first):
    packed = packed_ref[...].astype(F32)
    coef = packed[:, RANK : RANK + 2 * STATE] + packed[:, RANK + 2 * STATE :]
    for n in range(STATE):
        target[n] = jnp.broadcast_to(coef[:, first + n : first + n + 1], (coef.shape[0], LANES))


def scan_kernel(
    places_ref,
    near_ref,
    other_ref,
    mixed_ref,
    rates_ref,
    proj_hbm,
    bias_hbm,
    packed_ref,
    msg_ref,
    y_ref,
    delta_ref,
    before_hbm,
    enter_hbm,
    b_wide,
    c_wide,
    proj_ref,
    bias_ref,
    ends_ref,
    deltas_ref,
    before_ref,
    enter_ref,
    in_sems,
    out_sems,
):
    length, channels = mixed_ref.shape
    steps = length // SEG
    copies = [
        pltpu.make_async_copy(proj_hbm, proj_ref, in_sems.at[0]),
        pltpu.make_async_copy(bias_hbm, bias_ref, in_sems.at[1]),
    ]
    for copy in copies:
        copy.start()
    half = SEG // 2
    for place in range(half):
        taken = slice(place * steps, (place + 1) * steps)
        for source, slot in ((near_ref, place), (other_ref, place + half)):
            rows = pl.ds(pl.multiple_of(places_ref[SEG + slot] * steps, steps), steps)
            packed_ref[rows, :] = source[taken, :]
    spread(b_wide, packed_ref, 0)
    spread(c_wide, packed_ref, STATE)
    for copy in copies:
        copy.wait()
    copies = []
    raw = jnp.dot(packed_ref[:, :RANK], proj_ref[...], preferred_element_type=F32) + bias_ref[...]
    delta_ref[...] = jnp.maximum(raw, 0.0) + jnp.log1p(jnp.exp(-jnp.abs(raw)))
    row = lax.broadcasted_iota(jnp.int32, (SEG, LANES), 0)

    def shifted(value, by, fill):
        return jnp.where(row < by, fill, pltpu.roll(value, by, axis=0))

    for lane in range(0, channels, LANES):
        lanes = pl.ds(lane, LANES)
        rates = [
            jnp.broadcast_to(rates_ref[n : n + 1, lanes], (SEG, LANES)) for n in range(STATE)
        ]

        def step(i, carry):
            elapsed, states = carry
            rows = pl.ds(pl.multiple_of(i * SEG, SEG), SEG)
            delta = delta_ref[rows, lanes]
            drive = delta * mixed_ref[rows, lanes]
            fresh, terms = [], []
            for n in range(STATE):
                state = jnp.exp2(delta * rates[n]) * states[n] + drive * b_wide[n, rows, :]
                fresh.append(state)
                terms.append(state * c_wide[n, rows, :])
            while len(terms) > 1:
                terms = [a + b for a, b in zip(terms[::2], terms[1::2])]
            y_ref[rows, lanes] = terms[0]
            return elapsed + delta, tuple(fresh)

        zero = jnp.zeros((SEG, LANES), F32)
        elapsed, states = lax.fori_loop(0, steps, step, (zero, (zero,) * STATE), unroll=2)
        total = elapsed
        for by in (1, 2, 4):
            total = total + shifted(total, by, 0.0)
        before_ref[:, lanes] = shifted(total, 1, 0.0)
        last = total[SEG - 1 : SEG, :]
        for n in range(STATE):
            decay = jnp.exp2(elapsed * rates[n])
            state = states[n]
            for by in (1, 2, 4):
                state = decay * shifted(state, by, 0.0) + state
                decay = decay * shifted(decay, by, 1.0)
            enter_ref[n, :, lanes] = shifted(state, 1, 0.0)
            ends_ref[n : n + 1, lanes] = state[SEG - 1 : SEG, :]
        block = lane // LANES
        high = last.astype(BF16).astype(F32)
        deltas_ref[block : block + 1, :] = high
        deltas_ref[SEG + block : SEG + block + 1, :] = last - high
        fresh = [
            pltpu.make_async_copy(
                before_ref.at[:, lanes], before_hbm.at[:, lanes], out_sems.at[0, block]
            ),
            pltpu.make_async_copy(
                enter_ref.at[:, :, lanes], enter_hbm.at[:, :, lanes], out_sems.at[1, block]
            ),
        ]
        for copy in fresh:
            copy.start()
        copies += fresh
    msg_ref[:, :channels] = ends_ref[...]
    msg_ref[:, channels:] = deltas_ref[...]
    for copy in copies:
        copy.wait()


def unpacked(message, block):
    lanes = slice(block * LANES, (block + 1) * LANES)
    tail = message[:, message.shape[1] - LANES :]
    delta = tail[block : block + 1] + tail[SEG + block : SEG + block + 1]
    return message[:, lanes], delta


def joined(run, later, rates, chosen):
    state, delta = run
    more, more_delta = later
    state = jnp.where(chosen, jnp.exp2(more_delta * rates) * state + more, state)
    return state, jnp.where(chosen, delta + more_delta, delta)


def meet_kernel(places_ref, own_ref, third_ref, second_ref, first_ref, rates_ref, msg_ref, prefix_ref):
    place = places_ref[2 * SEG]
    channels = rates_ref.shape[1]
    for block in range(channels // LANES):
        lanes = slice(block * LANES, (block + 1) * LANES)
        rates = rates_ref[:, lanes]
        others = [
            (hops, unpacked(ref[...], block))
            for hops, ref in ((3, third_ref), (2, second_ref), (1, first_ref))
        ]
        run = (jnp.zeros((STATE, LANES), F32), jnp.zeros((1, LANES), F32))
        for hops, message in others:
            run = joined(run, message, rates, hops <= place)
        prefix_ref[:STATE, lanes] = run[0]
        prefix_ref[STATE : STATE + 1, lanes] = run[1]
        run = joined(run, unpacked(own_ref[...], block), rates, place >= 0)
        for hops, message in others:
            run = joined(run, message, rates, hops > place)
        state, delta = run
        high = delta.astype(BF16).astype(F32)
        msg_ref[:STATE, lanes] = state
        msg_ref[block : block + 1, channels:] = high
        msg_ref[SEG + block : SEG + block + 1, channels:] = delta - high


def ringed(message, axis):
    seqs = lax.axis_size("seq")
    side = math.isqrt(seqs)
    got = []
    for hops in range(1, side):
        route = []
        for i in range(seqs):
            x, y = i // side, i % side
            target = ((x + hops) % side, y) if axis == "x" else (x, (y + hops) % side)
            route.append((i, target[0] * side + target[1]))
        got.append(lax.ppermute(message, "seq", route))
    return got[::-1]


def finish_kernel(
    places_ref,
    prefix_ref,
    third_ref,
    second_ref,
    first_ref,
    rates_ref,
    delta_ref,
    packed_ref,
    y_ref,
    mixed_ref,
    before_hbm,
    enter_hbm,
    skip_hbm,
    z_hbm,
    gated_ref,
    before_ref,
    enter_ref,
    skip_ref,
    z_ref,
    c_wide,
    z_wide,
    gated,
    entering_ref,
    sems,
):
    length, channels = mixed_ref.shape
    steps = length // SEG
    sources = (before_hbm, enter_hbm, skip_hbm, z_hbm)
    targets = (before_ref, enter_ref, skip_ref, z_ref)
    copies = [pltpu.make_async_copy(*pair, sems.at[k]) for k, pair in enumerate(zip(sources, targets))]
    for copy in copies:
        copy.start()
    place = places_ref[2 * SEG + 1]
    for block in range(channels // LANES):
        lanes = slice(block * LANES, (block + 1) * LANES)
        rates = rates_ref[:, lanes]
        run = (jnp.zeros((STATE, LANES), F32), jnp.zeros((1, LANES), F32))
        for hops, ref in ((3, third_ref), (2, second_ref), (1, first_ref)):
            run = joined(run, unpacked(ref[...], block), rates, hops <= place)
        near = (prefix_ref[:STATE, lanes], prefix_ref[STATE : STATE + 1, lanes])
        entering_ref[:, lanes] = joined(run, near, rates, place >= 0)[0]
    spread(c_wide, packed_ref, STATE)
    for copy in copies:
        copy.wait()
    for lane in range(0, channels, LANES):
        z_wide[lane // LANES] = z_ref[:, lane : lane + LANES].astype(F32)

    for lane in range(0, channels, LANES):
        lanes = pl.ds(lane, LANES)
        rates = [
            jnp.broadcast_to(rates_ref[n : n + 1, lanes], (SEG, LANES)) for n in range(STATE)
        ]
        before = before_ref[:, lanes]
        held = [
            jnp.exp2(before * rates[n]) * entering_ref[n : n + 1, lanes] + enter_ref[n, :, lanes]
            for n in range(STATE)
        ]
        skip = skip_ref[:, lanes]

        def step(i, elapsed):
            rows = pl.ds(pl.multiple_of(i * SEG, SEG), SEG)
            apart = pl.ds(i, SEG, stride=steps)
            elapsed = elapsed + delta_ref[rows, lanes]
            terms = [
                jnp.exp2(elapsed * rates[n]) * held[n] * c_wide[n, rows, :] for n in range(STATE)
            ]
            while len(terms) > 1:
                terms = [a + b for a, b in zip(terms[::2], terms[1::2])]
            output = y_ref[rows, lanes] + terms[0] + skip * mixed_ref[rows, lanes]
            z = z_wide[lane // LANES, apart, :]
            gated[lane // LANES, apart, :] = output * (z * jax.nn.sigmoid(z))
            return elapsed

        lax.fori_loop(0, steps, step, jnp.zeros((SEG, LANES), F32), unroll=2)
    for spot in range(SEG):
        rows = pl.ds(pl.multiple_of(places_ref[spot] * steps, steps), steps)
        for lane in range(0, channels, LANES):
            gated_ref[spot * steps : (spot + 1) * steps, lane : lane + LANES] = gated[
                lane // LANES, rows, :
            ].astype(BF16)


def outward_kernel(gated_ref, proj_hbm, send_ref, keep_ref, proj, arrived):
    parts, _, width = proj_hbm.shape
    middle = send_ref.shape[0]
    group = 4

    def fetch(part):
        columns = pl.ds(pl.multiple_of(part * width, width), width)
        return pltpu.make_async_copy(proj_hbm.at[part], proj.at[:, columns], arrived.at[part])

    for part in range(2 * group):
        fetch(part).start()

    def product(step, carry):
        for part in range(group):
            fetch(step * group + part).wait()

        @pl.when(step < parts // group - 2)
        def _():
            for part in range(group):
                fetch((step + 2) * group + part).start()

        wide = group * width
        columns = pl.ds(pl.multiple_of(step * wide, wide), wide)
        terms = jnp.dot(gated_ref[...], proj[:, columns], preferred_element_type=F32)
        send_ref[:, columns] = terms[:middle].astype(BF16)
        keep_ref[:, columns] = terms[middle:]
        return carry

    lax.fori_loop(0, parts // group, product, 0)


def expert_kernel(rows_ref, gate_ref, up_ref, down_ref, first_ref, second_ref, inner):
    tile = 1024
    middle = first_ref.shape[0]
    gate = jnp.dot(rows_ref[...], gate_ref[...], preferred_element_type=F32)
    upper = jnp.dot(rows_ref[...], up_ref[...], preferred_element_type=F32)
    inner[...] = (gate * jax.nn.sigmoid(gate) * upper).astype(BF16)

    def narrow(part, carry):
        columns = pl.ds(pl.multiple_of(part * tile, tile), tile)
        piece = jnp.dot(inner[...], down_ref[:, columns], preferred_element_type=F32)
        first_ref[:, columns] = piece[:middle].astype(BF16)
        second_ref[:, columns] = piece[middle:].astype(BF16)
        return carry

    lax.fori_loop(0, first_ref.shape[1] // tile, narrow, 0, unroll=2)


def expert(rows, gate, up, down):
    count, features = rows.shape
    hidden = gate.shape[1]
    return pl.pallas_call(
        expert_kernel,
        out_shape=(jax.ShapeDtypeStruct((count // 2, features), BF16),) * 2,
        in_specs=[whole()] * 4,
        out_specs=[whole()] * 2,
        scratch_shapes=[pltpu.VMEM((count, hidden), BF16)],
        compiler_params=params(12),
        cost_estimate=pl.CostEstimate(
            flops=count * features, bytes_accessed=count * features, transcendentals=count
        ),
        name="expert",
    )(rows, gate, up, down)


def halves(block):
    middle = block.shape[0] // 2
    return block[:middle], block[middle:]


def added(*blocks):
    total = blocks[0].astype(F32)
    for block in blocks[1:]:
        total = total + block.astype(F32)
    return total.astype(BF16)


def experts_on_grid(rows, gate, up, down):
    run = functools.partial(expert, gate=gate, up=up, down=down)
    behind = along(rows, 0, 1)
    ahead = along(rows, 0, -1)
    across = jnp.concatenate(
        [along(halves(behind)[0], 0, 1), along(halves(ahead)[1], 0, -1)], axis=0
    )
    own_first = jnp.concatenate([rows, behind], axis=0)
    behind_first = along(own_first, 1, 1)
    across, own_first_later = lax.optimization_barrier((across, own_first))
    own_second = jnp.concatenate([ahead, across], axis=0)
    ahead_second = jnp.concatenate([along(ahead, 1, -1), along(across, 1, -1)], axis=0)
    behind_second = along(own_second, 1, 1)
    ahead_first = along(own_first_later, 1, -1)
    far_first = along(behind_first, 1, 1)
    far_second = along(ahead_second, 1, -1)
    behind_out, ahead_out = run(jnp.concatenate([behind_first, ahead_second], axis=0))
    early_first = along(behind_out, 1, -1)
    early_second = along(ahead_out, 1, 1)
    behind_second, ahead_first, behind_out = lax.optimization_barrier(
        (behind_second, ahead_first, behind_out)
    )
    behind_rest, ahead_rest = run(jnp.concatenate([behind_second, ahead_first], axis=0))
    far_first, far_second, behind_rest = lax.optimization_barrier(
        (far_first, far_second, behind_rest)
    )
    across_first, across_second = run(jnp.concatenate([far_first, far_second], axis=0))
    from_behind = along(across_first, 1, 1)
    from_ahead = along(across_second, 1, -1)
    own_out = run(jnp.concatenate([own_first, own_second], axis=0))
    from_behind, from_ahead, early_first, early_second, own_out = lax.optimization_barrier(
        (from_behind, from_ahead, early_first, early_second, own_out)
    )
    late_first = along(added(ahead_rest, from_behind), 1, 1)
    late_second = along(added(behind_rest, from_ahead), 1, -1)
    kept, behind = halves(added(own_out[0], early_first, late_first))
    ahead, across = halves(added(own_out[1], early_second, late_second))
    across_first, across_second = halves(across)
    ahead_first, ahead_second = halves(ahead)
    behind_first, behind_second = halves(behind)
    ahead_first = added(ahead_first, along(across_first, 0, 1))
    behind_second = added(behind_second, along(across_second, 0, -1))
    from_behind = along(jnp.concatenate([ahead_first, ahead_second], axis=0), 0, 1)
    from_ahead = along(jnp.concatenate([behind_first, behind_second], axis=0), 0, -1)
    return added(kept, from_behind, from_ahead)


def device_places():
    owners, seqs = lax.axis_size("exp"), lax.axis_size("seq")
    side, grid_side = owners // 2, math.isqrt(seqs)
    owner = lax.axis_index("exp").astype(jnp.int32)
    place = lax.axis_index("seq").astype(jnp.int32)
    chip, core = owner // 2, owner % 2
    hops = jnp.arange(side, dtype=jnp.int32)
    onward, back = (chip + hops) % side, (chip - hops) % side
    blocks = [onward * 2 + 1 - core, onward * 2 + core, back * 2 + core, back * 2 + 1 - core]
    return jnp.concatenate(blocks + [(place % grid_side)[None], (place // grid_side)[None]])


def mixer(
    places,
    tail,
    x_in,
    z_in,
    conv_weight,
    conv_bias,
    x_proj,
    dt_proj,
    dt_bias,
    a_log,
    d_skip,
    out_proj,
):
    length, channels = x_in.shape
    steps = length // SEG
    owners = lax.axis_size("exp")
    seqs = lax.axis_size("seq")
    side = owners // 2
    swap = [(e, e + 1 - 2 * (e % 2)) for e in range(owners)]

    def along_z(block, hop):
        return lax.ppermute(block, "exp", [(e, (e + 2 * hop) % owners) for e in range(owners)])

    columns = lax.all_gather(out_proj, "seq", axis=0)
    rates = (-jnp.exp(a_log) * LOG2E).T
    rim = passed_along(tail, "seq", 1)
    mixed, send, keep = pl.pallas_call(
        conv_kernel,
        out_shape=(
            jax.ShapeDtypeStruct((length, channels), F32),
            jax.ShapeDtypeStruct((length // 2, RANK + 2 * STATE), F32),
            jax.ShapeDtypeStruct((length // 2, RANK + 2 * STATE), F32),
        ),
        in_specs=[pl.BlockSpec(memory_space=pltpu.SMEM)] + [far()] * 2 + [whole()] * 2,
        out_specs=[whole()] * 3,
        scratch_shapes=[
            pltpu.VMEM(x_in.shape, BF16),
            pltpu.VMEM(x_proj.shape[::-1], BF16),
            pltpu.VMEM((channels // LANES, length + 8, LANES), F32),
            pltpu.VMEM((length, RANK + 2 * STATE), F32),
            pltpu.SemaphoreType.DMA((2,)),
        ],
        compiler_params=params(12),
        name="conv",
    )(places, x_in, x_proj.T, jnp.concatenate([conv_weight, conv_bias[None, :]], axis=0), rim)
    sums = (keep + lax.ppermute(send, "exp", swap)).reshape(side, length // owners, -1)
    summed = sums[0]
    for hop in range(1, side):
        summed = summed + along_z(sums[hop], hop)
    coef = summed[:, RANK:]
    coef_high = coef.astype(BF16)
    coef_low = (coef - coef_high.astype(F32)).astype(BF16)
    near = jnp.concatenate([summed[:, :RANK].astype(BF16), coef_high, coef_low], axis=1)
    near = jnp.concatenate([near] + [along_z(near, hop) for hop in range(1, side)], axis=0)
    other = lax.ppermute(near, "exp", swap)
    packed, message, y_local, delta, before, enter = pl.pallas_call(
        scan_kernel,
        out_shape=(
            jax.ShapeDtypeStruct((length, RANK + 4 * STATE), BF16),
            jax.ShapeDtypeStruct((STATE, channels + LANES), F32),
            jax.ShapeDtypeStruct((length, channels), F32),
            jax.ShapeDtypeStruct((length, channels), F32),
            jax.ShapeDtypeStruct((SEG, channels), F32),
            jax.ShapeDtypeStruct((STATE, SEG, channels), F32),
        ),
        in_specs=[pl.BlockSpec(memory_space=pltpu.SMEM)] + [whole()] * 4 + [far()] * 2,
        out_specs=[whole()] * 4 + [far()] * 2,
        scratch_shapes=[
            pltpu.VMEM((STATE, length, LANES), F32),
            pltpu.VMEM((STATE, length, LANES), F32),
            pltpu.VMEM(dt_proj.shape, BF16),
            pltpu.VMEM((1, channels), F32),
            pltpu.VMEM((STATE, channels), F32),
            pltpu.VMEM((STATE, LANES), F32),
            pltpu.VMEM((SEG, channels), F32),
            pltpu.VMEM((STATE, SEG, channels), F32),
            pltpu.SemaphoreType.DMA((2,)),
            pltpu.SemaphoreType.DMA((2, channels // LANES)),
        ],
        compiler_params=params(14),
        name="scan",
    )(places, near, other, mixed, rates, dt_proj, dt_bias[None, :])
    totals, prefix = pl.pallas_call(
        meet_kernel,
        out_shape=(
            jax.ShapeDtypeStruct((STATE, channels + LANES), F32),
            jax.ShapeDtypeStruct((STATE + 1, channels), F32),
        ),
        in_specs=[pl.BlockSpec(memory_space=pltpu.SMEM)] + [whole()] * 5,
        out_specs=[whole()] * 2,
        compiler_params=params(4),
        name="meet",
    )(places, message, *ringed(message, "y"), rates)
    lines_before = ringed(totals, "x")
    gated = pl.pallas_call(
        finish_kernel,
        out_shape=jax.ShapeDtypeStruct((length, channels), BF16),
        in_specs=[pl.BlockSpec(memory_space=pltpu.SMEM)] + [whole()] * 9 + [far()] * 4,
        out_specs=whole(),
        scratch_shapes=[
            pltpu.VMEM((SEG, channels), F32),
            pltpu.VMEM((STATE, SEG, channels), F32),
            pltpu.VMEM((1, channels), F32),
            pltpu.VMEM((length, channels), BF16),
            pltpu.VMEM((STATE, length, LANES), F32),
            pltpu.VMEM((channels // LANES, length, LANES), F32),
            pltpu.VMEM((channels // LANES, length, LANES), F32),
            pltpu.VMEM((STATE, channels), F32),
            pltpu.SemaphoreType.DMA((4,)),
        ],
        compiler_params=params(16),
        name="finish",
    )(
        places,
        prefix,
        *lines_before,
        rates,
        delta,
        packed,
        y_local,
        mixed,
        before,
        enter,
        d_skip[None, :],
        z_in,
    )
    width = out_proj.shape[1]
    features = seqs * width
    send, keep = pl.pallas_call(
        outward_kernel,
        out_shape=(
            jax.ShapeDtypeStruct((length // 2, features), BF16),
            jax.ShapeDtypeStruct((length // 2, features), F32),
        ),
        in_specs=[whole(), far()],
        out_specs=[whole()] * 2,
        scratch_shapes=[
            pltpu.VMEM((channels, features), BF16),
            pltpu.SemaphoreType.DMA((seqs,)),
        ],
        compiler_params=params(50),
        name="outward",
    )(gated, columns)
    sums = keep + lax.ppermute(send, "exp", swap).astype(F32)
    sums = sums.reshape(side, length // owners, features)
    total = sums[0]
    for hop in range(1, side):
        total = total + along_z(sums[hop].astype(BF16), hop).astype(F32)
    return total


def shards(
    x_in,
    z_in,
    conv_weight,
    conv_bias,
    x_proj,
    dt_proj,
    dt_bias,
    a_log,
    d_skip,
    out_proj,
    residual,
    expert_ids,
    gate_weights,
    w_gate,
    w_up,
    w_down,
):
    owners = lax.axis_size("exp")
    tok_rows = residual.shape[0]
    capacity = max(2, tok_rows // 4)
    slots = owners * capacity
    chosen_count = expert_ids.shape[1]
    flat_ids = expert_ids.reshape(-1)
    hits = (flat_ids[:, None] == jnp.arange(owners, dtype=jnp.int32)[None, :]).astype(jnp.int32)
    before = jnp.cumsum(hits, axis=0) - hits
    ranked = jnp.sum(before * hits, axis=1)
    valid = jnp.sum(hits, axis=1)
    target = flat_ids * capacity + ranked
    placed = (
        (target[:, None] == jnp.arange(slots, dtype=jnp.int32)[None, :]) & (valid[:, None] > 0)
    ).astype(jnp.float32)
    dispatch_table = jnp.sum(placed.reshape(tok_rows, chosen_count, slots), axis=1)
    combine_table = jnp.sum(
        (placed * gate_weights.reshape(-1)[:, None]).reshape(tok_rows, chosen_count, slots), axis=1
    )
    tail, places, dispatch_table, combine_table = lax.optimization_barrier(
        (x_in[-(CONV - 1) :], device_places(), dispatch_table.astype(BF16), combine_table)
    )
    mixed = mixer(
        places,
        tail,
        x_in,
        z_in,
        conv_weight,
        conv_bias,
        x_proj,
        dt_proj,
        dt_bias,
        a_log,
        d_skip,
        out_proj,
    )
    hidden = residual.astype(jnp.float32) + mixed
    normed = (hidden * lax.rsqrt(jnp.mean(hidden * hidden, axis=-1, keepdims=True) + 1e-06)).astype(
        jnp.bfloat16
    )
    outgoing = jnp.einsum(
        "ts,td->sd", dispatch_table, normed, preferred_element_type=jnp.float32
    )
    outgoing = outgoing.astype(jnp.bfloat16).reshape(owners, capacity, -1)
    arrived = lax.all_to_all(outgoing, "exp", split_axis=0, concat_axis=0, tiled=True)
    summed = experts_on_grid(arrived.reshape(slots, -1), w_gate[0], w_up[0], w_down[0])
    expert_out = summed.reshape(owners, capacity, -1)
    returned_rows = lax.all_to_all(
        expert_out, "exp", split_axis=0, concat_axis=0, tiled=True
    ).reshape(slots, -1)
    combined = jnp.dot(
        combine_table, returned_rows.astype(jnp.float32), precision=lax.Precision.HIGHEST
    )
    return hidden + combined


def solution(mesh):
    placed = (
        P("seq", "exp"),
        P("seq", "exp"),
        P(None, "exp"),
        P("exp"),
        P("exp", None),
        P(None, "exp"),
        P("exp"),
        P("exp", None),
        P("exp"),
        P("exp", "seq"),
        P(("seq", "exp"), None),
        P(("seq", "exp"), None),
        P(("seq", "exp"), None),
        P("exp", None, "seq"),
        P("exp", None, "seq"),
        P("exp", "seq", None),
    )
    return jax.shard_map(
        shards, mesh=mesh, in_specs=placed, out_specs=P(("seq", "exp"), None), check_vma=False
    )
```

```python
import functools
import math

import jax
import jax.numpy as jnp
from jax import lax
from jax.experimental import pallas as pl
from jax.experimental.pallas import tpu as pltpu
from jax.sharding import PartitionSpec as P

RANK = 256
STATE = 16
CONV = 4
SEG = 8
LANES = 128
LOG2E = math.log2(math.e)
F32 = jnp.float32
BF16 = jnp.bfloat16
MIB = 1024 * 1024


def whole():
    return pl.BlockSpec(memory_space=pltpu.VMEM)


def far():
    return pl.BlockSpec(memory_space=pltpu.HBM)


def params(mib):
    return pltpu.CompilerParams(vmem_limit_bytes=mib * MIB)


def lines(stage):
    side = math.isqrt(lax.axis_size("seq"))
    owners = lax.axis_size("exp")
    groups = []
    for owner in range(owners):
        along_x = (owner % 2 == 0) == (stage == 0)
        for fixed in range(side):
            members = [(m * side + fixed if along_x else fixed * side + m) for m in range(side)]
            groups.append([m * owners + owner for m in members])
    return groups


def along(block, stage, distance):
    route = []
    for members in lines(stage):
        count = len(members)
        route += [(members[i], members[(i + distance) % count]) for i in range(count)]
    return lax.ppermute(block, ("seq", "exp"), route)


def passed_along(block, axis, distance):
    devices = range(lax.axis_size(axis))
    route = [(i - distance, i) for i in devices if i - distance in devices]
    return lax.ppermute(block, axis, route)


def conv_kernel(
    places_ref,
    x_hbm,
    proj_hbm,
    weight_ref,
    rim_ref,
    mixed_ref,
    send_ref,
    keep_ref,
    x_ref,
    proj_ref,
    padded,
    part_ref,
    sems,
):
    sources = (x_hbm, proj_hbm)
    targets = (x_ref, proj_ref)
    copies = [pltpu.make_async_copy(*pair, sems.at[k]) for k, pair in enumerate(zip(sources, targets))]
    for copy in copies:
        copy.start()
    length, channels = x_ref.shape
    steps = length // SEG
    head = 8
    copies[0].wait()
    for lane in range(0, channels, LANES):
        block = padded.at[lane // LANES]
        block[head - (CONV - 1) : head, :] = rim_ref[:, lane : lane + LANES].astype(F32)
        block[head:, :] = x_ref[:, lane : lane + LANES].astype(F32)

    def step(i, carry):
        rows = pl.ds(pl.multiple_of(i * SEG, SEG), SEG)
        for lane in range(0, channels, LANES):
            lanes = pl.ds(lane, LANES)
            acc = jnp.broadcast_to(weight_ref[CONV : CONV + 1, lanes], (SEG, LANES))
            for tap in range(CONV):
                taken = padded[
                    lane // LANES, pl.ds(i + head - (CONV - 1) + tap, SEG, stride=steps), :
                ]
                acc = acc + weight_ref[tap : tap + 1, lanes] * taken
            mixed_ref[rows, lanes] = (acc * jax.nn.sigmoid(acc)).astype(BF16).astype(F32)
        return carry

    lax.fori_loop(0, steps, step, 0)
    copies[1].wait()
    part_ref[...] = lax.dot_general(
        mixed_ref[...].astype(BF16),
        proj_ref[...],
        (((1,), (1,)), ((), ())),
        preferred_element_type=F32,
    )
    half = SEG // 2
    for spot in range(SEG):
        rows = pl.ds(pl.multiple_of(places_ref[spot] * steps, steps), steps)
        target = send_ref if spot < half else keep_ref
        first = spot % half * steps
        target[first : first + steps, :] = part_ref[rows, :]


def spread(target, packed_ref, first):
    packed = packed_ref[...].astype(F32)
    coef = packed[:, RANK : RANK + 2 * STATE] + packed[:, RANK + 2 * STATE :]
    for n in range(STATE):
        target[n] = jnp.broadcast_to(coef[:, first + n : first + n + 1], (coef.shape[0], LANES))


def scan_kernel(
    places_ref,
    near_ref,
    other_ref,
    mixed_ref,
    rates_ref,
    proj_hbm,
    bias_hbm,
    packed_ref,
    msg_ref,
    y_ref,
    delta_ref,
    before_hbm,
    enter_hbm,
    b_wide,
    c_wide,
    proj_ref,
    bias_ref,
    ends_ref,
    deltas_ref,
    before_ref,
    enter_ref,
    in_sems,
    out_sems,
):
    length, channels = mixed_ref.shape
    steps = length // SEG
    copies = [
        pltpu.make_async_copy(proj_hbm, proj_ref, in_sems.at[0]),
        pltpu.make_async_copy(bias_hbm, bias_ref, in_sems.at[1]),
    ]
    for copy in copies:
        copy.start()
    half = SEG // 2
    for place in range(half):
        taken = slice(place * steps, (place + 1) * steps)
        for source, slot in ((near_ref, place), (other_ref, place + half)):
            rows = pl.ds(pl.multiple_of(places_ref[SEG + slot] * steps, steps), steps)
            packed_ref[rows, :] = source[taken, :]
    spread(b_wide, packed_ref, 0)
    spread(c_wide, packed_ref, STATE)
    for copy in copies:
        copy.wait()
    copies = []
    raw = jnp.dot(packed_ref[:, :RANK], proj_ref[...], preferred_element_type=F32) + bias_ref[...]
    delta_ref[...] = jnp.maximum(raw, 0.0) + jnp.log1p(jnp.exp(-jnp.abs(raw)))
    row = lax.broadcasted_iota(jnp.int32, (SEG, LANES), 0)

    def shifted(value, by, fill):
        return jnp.where(row < by, fill, pltpu.roll(value, by, axis=0))

    for lane in range(0, channels, LANES):
        lanes = pl.ds(lane, LANES)
        rates = [
            jnp.broadcast_to(rates_ref[n : n + 1, lanes], (SEG, LANES)) for n in range(STATE)
        ]

        def step(i, carry):
            elapsed, states = carry
            rows = pl.ds(pl.multiple_of(i * SEG, SEG), SEG)
            delta = delta_ref[rows, lanes]
            drive = delta * mixed_ref[rows, lanes]
            fresh, terms = [], []
            for n in range(STATE):
                state = jnp.exp2(delta * rates[n]) * states[n] + drive * b_wide[n, rows, :]
                fresh.append(state)
                terms.append(state * c_wide[n, rows, :])
            while len(terms) > 1:
                terms = [a + b for a, b in zip(terms[::2], terms[1::2])]
            y_ref[rows, lanes] = terms[0]
            return elapsed + delta, tuple(fresh)

        zero = jnp.zeros((SEG, LANES), F32)
        elapsed, states = lax.fori_loop(0, steps, step, (zero, (zero,) * STATE))
        total = elapsed
        for by in (1, 2, 4):
            total = total + shifted(total, by, 0.0)
        before_ref[:, lanes] = shifted(total, 1, 0.0)
        last = total[SEG - 1 : SEG, :]
        for n in range(STATE):
            decay = jnp.exp2(elapsed * rates[n])
            state = states[n]
            for by in (1, 2, 4):
                state = decay * shifted(state, by, 0.0) + state
                decay = decay * shifted(decay, by, 1.0)
            enter_ref[n, :, lanes] = shifted(state, 1, 0.0)
            ends_ref[n : n + 1, lanes] = state[SEG - 1 : SEG, :]
        block = lane // LANES
        high = last.astype(BF16).astype(F32)
        deltas_ref[block : block + 1, :] = high
        deltas_ref[SEG + block : SEG + block + 1, :] = last - high
        fresh = [
            pltpu.make_async_copy(
                before_ref.at[:, lanes], before_hbm.at[:, lanes], out_sems.at[0, block]
            ),
            pltpu.make_async_copy(
                enter_ref.at[:, :, lanes], enter_hbm.at[:, :, lanes], out_sems.at[1, block]
            ),
        ]
        for copy in fresh:
            copy.start()
        copies += fresh
    msg_ref[:, :channels] = ends_ref[...].astype(BF16)
    msg_ref[:, channels:] = deltas_ref[...].astype(BF16)
    for copy in copies:
        copy.wait()


def unpacked(message, block):
    lanes = slice(block * LANES, (block + 1) * LANES)
    tail = message[:, message.shape[1] - LANES :].astype(F32)
    delta = tail[block : block + 1] + tail[SEG + block : SEG + block + 1]
    return message[:, lanes].astype(F32), delta


def joined(run, later, rates, chosen):
    state, delta = run
    more, more_delta = later
    state = jnp.where(chosen, jnp.exp2(more_delta * rates) * state + more, state)
    return state, jnp.where(chosen, delta + more_delta, delta)


def meet_kernel(places_ref, own_ref, third_ref, second_ref, first_ref, rates_ref, msg_ref, prefix_ref):
    place = places_ref[2 * SEG]
    channels = rates_ref.shape[1]
    for block in range(channels // LANES):
        lanes = slice(block * LANES, (block + 1) * LANES)
        rates = rates_ref[:, lanes]
        others = [
            (hops, unpacked(ref[...], block))
            for hops, ref in ((3, third_ref), (2, second_ref), (1, first_ref))
        ]
        run = (jnp.zeros((STATE, LANES), F32), jnp.zeros((1, LANES), F32))
        for hops, message in others:
            run = joined(run, message, rates, hops <= place)
        prefix_ref[:STATE, lanes] = run[0]
        prefix_ref[STATE : STATE + 1, lanes] = run[1]
        run = joined(run, unpacked(own_ref[...], block), rates, place >= 0)
        for hops, message in others:
            run = joined(run, message, rates, hops > place)
        state, delta = run
        high = delta.astype(BF16).astype(F32)
        msg_ref[:STATE, lanes] = state
        msg_ref[block : block + 1, channels:] = high
        msg_ref[SEG + block : SEG + block + 1, channels:] = delta - high


def ringed(message, axis):
    seqs = lax.axis_size("seq")
    side = math.isqrt(seqs)
    got = []
    for hops in range(1, side):
        route = []
        for i in range(seqs):
            x, y = i // side, i % side
            target = ((x + hops) % side, y) if axis == "x" else (x, (y + hops) % side)
            route.append((i, target[0] * side + target[1]))
        got.append(lax.ppermute(message, "seq", route))
    return got[::-1]


def finish_kernel(
    places_ref,
    prefix_ref,
    third_ref,
    second_ref,
    first_ref,
    rates_ref,
    delta_ref,
    packed_ref,
    y_ref,
    mixed_ref,
    before_hbm,
    enter_hbm,
    skip_hbm,
    z_hbm,
    gated_ref,
    before_ref,
    enter_ref,
    skip_ref,
    z_ref,
    c_wide,
    z_wide,
    gated,
    entering_ref,
    sems,
):
    length, channels = mixed_ref.shape
    steps = length // SEG
    sources = (before_hbm, enter_hbm, skip_hbm, z_hbm)
    targets = (before_ref, enter_ref, skip_ref, z_ref)
    copies = [pltpu.make_async_copy(*pair, sems.at[k]) for k, pair in enumerate(zip(sources, targets))]
    for copy in copies:
        copy.start()
    place = places_ref[2 * SEG + 1]
    for block in range(channels // LANES):
        lanes = slice(block * LANES, (block + 1) * LANES)
        rates = rates_ref[:, lanes]
        run = (jnp.zeros((STATE, LANES), F32), jnp.zeros((1, LANES), F32))
        for hops, ref in ((3, third_ref), (2, second_ref), (1, first_ref)):
            run = joined(run, unpacked(ref[...], block), rates, hops <= place)
        near = (prefix_ref[:STATE, lanes], prefix_ref[STATE : STATE + 1, lanes])
        entering_ref[:, lanes] = joined(run, near, rates, place >= 0)[0]
    spread(c_wide, packed_ref, STATE)
    for copy in copies:
        copy.wait()
    for lane in range(0, channels, LANES):
        z_wide[lane // LANES] = z_ref[:, lane : lane + LANES].astype(F32)

    for lane in range(0, channels, LANES):
        lanes = pl.ds(lane, LANES)
        rates = [
            jnp.broadcast_to(rates_ref[n : n + 1, lanes], (SEG, LANES)) for n in range(STATE)
        ]
        before = before_ref[:, lanes]
        held = [
            jnp.exp2(before * rates[n]) * entering_ref[n : n + 1, lanes] + enter_ref[n, :, lanes]
            for n in range(STATE)
        ]
        skip = skip_ref[:, lanes]

        def step(i, elapsed):
            rows = pl.ds(pl.multiple_of(i * SEG, SEG), SEG)
            apart = pl.ds(i, SEG, stride=steps)
            elapsed = elapsed + delta_ref[rows, lanes]
            terms = [
                jnp.exp2(elapsed * rates[n]) * held[n] * c_wide[n, rows, :] for n in range(STATE)
            ]
            while len(terms) > 1:
                terms = [a + b for a, b in zip(terms[::2], terms[1::2])]
            output = y_ref[rows, lanes] + terms[0] + skip * mixed_ref[rows, lanes]
            z = z_wide[lane // LANES, apart, :]
            gated[lane // LANES, apart, :] = output * (z * jax.nn.sigmoid(z))
            return elapsed

        lax.fori_loop(0, steps, step, jnp.zeros((SEG, LANES), F32))
    for spot in range(SEG):
        rows = pl.ds(pl.multiple_of(places_ref[spot] * steps, steps), steps)
        for lane in range(0, channels, LANES):
            gated_ref[spot * steps : (spot + 1) * steps, lane : lane + LANES] = gated[
                lane // LANES, rows, :
            ].astype(BF16)


def outward_kernel(gated_ref, proj_hbm, send_ref, keep_ref, proj, arrived):
    parts, _, width = proj_hbm.shape
    middle = send_ref.shape[0]
    group = 4

    def fetch(part):
        columns = pl.ds(pl.multiple_of(part * width, width), width)
        return pltpu.make_async_copy(proj_hbm.at[part], proj.at[:, columns], arrived.at[part])

    for part in range(2 * group):
        fetch(part).start()

    def product(step, carry):
        for part in range(group):
            fetch(step * group + part).wait()

        @pl.when(step < parts // group - 2)
        def _():
            for part in range(group):
                fetch((step + 2) * group + part).start()

        wide = group * width
        columns = pl.ds(pl.multiple_of(step * wide, wide), wide)
        terms = jnp.dot(gated_ref[...], proj[:, columns], preferred_element_type=F32)
        send_ref[:, columns] = terms[:middle].astype(BF16)
        keep_ref[:, columns] = terms[middle:]
        return carry

    lax.fori_loop(0, parts // group, product, 0)


def expert_kernel(rows_ref, gate_ref, up_ref, down_ref, first_ref, second_ref, inner):
    tile = 1024
    middle = first_ref.shape[0]
    gate = jnp.dot(rows_ref[...], gate_ref[...], preferred_element_type=F32)
    upper = jnp.dot(rows_ref[...], up_ref[...], preferred_element_type=F32)
    inner[...] = (gate * jax.nn.sigmoid(gate) * upper).astype(BF16)

    def narrow(part, carry):
        columns = pl.ds(pl.multiple_of(part * tile, tile), tile)
        piece = jnp.dot(inner[...], down_ref[:, columns], preferred_element_type=F32)
        first_ref[:, columns] = piece[:middle].astype(BF16)
        second_ref[:, columns] = piece[middle:].astype(BF16)
        return carry

    lax.fori_loop(0, first_ref.shape[1] // tile, narrow, 0)


def expert(rows, gate, up, down):
    count, features = rows.shape
    hidden = gate.shape[1]
    return pl.pallas_call(
        expert_kernel,
        out_shape=(jax.ShapeDtypeStruct((count // 2, features), BF16),) * 2,
        in_specs=[whole()] * 4,
        out_specs=[whole()] * 2,
        scratch_shapes=[pltpu.VMEM((count, hidden), BF16)],
        compiler_params=params(12),
        cost_estimate=pl.CostEstimate(
            flops=count * features, bytes_accessed=count * features, transcendentals=count
        ),
        name="expert",
    )(rows, gate, up, down)


def halves(block):
    middle = block.shape[0] // 2
    return block[:middle], block[middle:]


def added(*blocks):
    total = blocks[0].astype(F32)
    for block in blocks[1:]:
        total = total + block.astype(F32)
    return total.astype(BF16)


def experts_on_grid(rows, gate, up, down):
    run = functools.partial(expert, gate=gate, up=up, down=down)
    behind = along(rows, 0, 1)
    ahead = along(rows, 0, -1)
    across = jnp.concatenate(
        [along(halves(behind)[0], 0, 1), along(halves(ahead)[1], 0, -1)], axis=0
    )
    own_first = jnp.concatenate([rows, behind], axis=0)
    behind_first = along(own_first, 1, 1)
    across, own_first_later = lax.optimization_barrier((across, own_first))
    own_second = jnp.concatenate([ahead, across], axis=0)
    ahead_second = jnp.concatenate([along(ahead, 1, -1), along(across, 1, -1)], axis=0)
    behind_second = along(own_second, 1, 1)
    ahead_first = along(own_first_later, 1, -1)
    far_first = along(behind_first, 1, 1)
    far_second = along(ahead_second, 1, -1)
    behind_out, ahead_out = run(jnp.concatenate([behind_first, ahead_second], axis=0))
    early_first = along(behind_out, 1, -1)
    early_second = along(ahead_out, 1, 1)
    behind_second, ahead_first, behind_out = lax.optimization_barrier(
        (behind_second, ahead_first, behind_out)
    )
    behind_rest, ahead_rest = run(jnp.concatenate([behind_second, ahead_first], axis=0))
    far_first, far_second, behind_rest = lax.optimization_barrier(
        (far_first, far_second, behind_rest)
    )
    across_first, across_second = run(jnp.concatenate([far_first, far_second], axis=0))
    from_behind = along(across_first, 1, 1)
    from_ahead = along(across_second, 1, -1)
    own_out = run(jnp.concatenate([own_first, own_second], axis=0))
    from_behind, from_ahead, early_first, early_second, own_out = lax.optimization_barrier(
        (from_behind, from_ahead, early_first, early_second, own_out)
    )
    late_first = along(added(ahead_rest, from_behind), 1, 1)
    late_second = along(added(behind_rest, from_ahead), 1, -1)
    kept, behind = halves(added(own_out[0], early_first, late_first))
    ahead, across = halves(added(own_out[1], early_second, late_second))
    across_first, across_second = halves(across)
    ahead_first, ahead_second = halves(ahead)
    behind_first, behind_second = halves(behind)
    ahead_first = added(ahead_first, along(across_first, 0, 1))
    behind_second = added(behind_second, along(across_second, 0, -1))
    from_behind = along(jnp.concatenate([ahead_first, ahead_second], axis=0), 0, 1)
    from_ahead = along(jnp.concatenate([behind_first, behind_second], axis=0), 0, -1)
    return added(kept, from_behind, from_ahead)


def device_places():
    owners, seqs = lax.axis_size("exp"), lax.axis_size("seq")
    side, grid_side = owners // 2, math.isqrt(seqs)
    owner = lax.axis_index("exp").astype(jnp.int32)
    place = lax.axis_index("seq").astype(jnp.int32)
    chip, core = owner // 2, owner % 2
    hops = jnp.arange(side, dtype=jnp.int32)
    onward, back = (chip + hops) % side, (chip - hops) % side
    blocks = [onward * 2 + 1 - core, onward * 2 + core, back * 2 + core, back * 2 + 1 - core]
    return jnp.concatenate(blocks + [(place % grid_side)[None], (place // grid_side)[None]])


def mixer(
    places,
    tail,
    x_in,
    z_in,
    conv_weight,
    conv_bias,
    x_proj,
    dt_proj,
    dt_bias,
    a_log,
    d_skip,
    out_proj,
):
    length, channels = x_in.shape
    steps = length // SEG
    owners = lax.axis_size("exp")
    seqs = lax.axis_size("seq")
    side = owners // 2
    swap = [(e, e + 1 - 2 * (e % 2)) for e in range(owners)]

    def along_z(block, hop):
        return lax.ppermute(block, "exp", [(e, (e + 2 * hop) % owners) for e in range(owners)])

    columns = lax.all_gather(out_proj, "seq", axis=0)
    rates = (-jnp.exp(a_log) * LOG2E).T
    rim = passed_along(tail, "seq", 1)
    mixed, send, keep = pl.pallas_call(
        conv_kernel,
        out_shape=(
            jax.ShapeDtypeStruct((length, channels), F32),
            jax.ShapeDtypeStruct((length // 2, RANK + 2 * STATE), F32),
            jax.ShapeDtypeStruct((length // 2, RANK + 2 * STATE), F32),
        ),
        in_specs=[pl.BlockSpec(memory_space=pltpu.SMEM)] + [far()] * 2 + [whole()] * 2,
        out_specs=[whole()] * 3,
        scratch_shapes=[
            pltpu.VMEM(x_in.shape, BF16),
            pltpu.VMEM(x_proj.shape[::-1], BF16),
            pltpu.VMEM((channels // LANES, length + 8, LANES), F32),
            pltpu.VMEM((length, RANK + 2 * STATE), F32),
            pltpu.SemaphoreType.DMA((2,)),
        ],
        compiler_params=params(12),
        name="conv",
    )(places, x_in, x_proj.T, jnp.concatenate([conv_weight, conv_bias[None, :]], axis=0), rim)
    sums = (keep + lax.ppermute(send, "exp", swap)).reshape(side, length // owners, -1)
    summed = sums[0]
    for hop in range(1, side):
        summed = summed + along_z(sums[hop], hop)
    coef = summed[:, RANK:]
    coef_high = coef.astype(BF16)
    coef_low = (coef - coef_high.astype(F32)).astype(BF16)
    near = jnp.concatenate([summed[:, :RANK].astype(BF16), coef_high, coef_low], axis=1)
    near = jnp.concatenate([near] + [along_z(near, hop) for hop in range(1, side)], axis=0)
    other = lax.ppermute(near, "exp", swap)
    packed, message, y_local, delta, before, enter = pl.pallas_call(
        scan_kernel,
        out_shape=(
            jax.ShapeDtypeStruct((length, RANK + 4 * STATE), BF16),
            jax.ShapeDtypeStruct((STATE, channels + LANES), BF16),
            jax.ShapeDtypeStruct((length, channels), F32),
            jax.ShapeDtypeStruct((length, channels), F32),
            jax.ShapeDtypeStruct((SEG, channels), F32),
            jax.ShapeDtypeStruct((STATE, SEG, channels), F32),
        ),
        in_specs=[pl.BlockSpec(memory_space=pltpu.SMEM)] + [whole()] * 4 + [far()] * 2,
        out_specs=[whole()] * 4 + [far()] * 2,
        scratch_shapes=[
            pltpu.VMEM((STATE, length, LANES), F32),
            pltpu.VMEM((STATE, length, LANES), F32),
            pltpu.VMEM(dt_proj.shape, BF16),
            pltpu.VMEM((1, channels), F32),
            pltpu.VMEM((STATE, channels), F32),
            pltpu.VMEM((STATE, LANES), F32),
            pltpu.VMEM((SEG, channels), F32),
            pltpu.VMEM((STATE, SEG, channels), F32),
            pltpu.SemaphoreType.DMA((2,)),
            pltpu.SemaphoreType.DMA((2, channels // LANES)),
        ],
        compiler_params=params(14),
        name="scan",
    )(places, near, other, mixed, rates, dt_proj, dt_bias[None, :])
    totals, prefix = pl.pallas_call(
        meet_kernel,
        out_shape=(
            jax.ShapeDtypeStruct((STATE, channels + LANES), F32),
            jax.ShapeDtypeStruct((STATE + 1, channels), F32),
        ),
        in_specs=[pl.BlockSpec(memory_space=pltpu.SMEM)] + [whole()] * 5,
        out_specs=[whole()] * 2,
        compiler_params=params(4),
        name="meet",
    )(places, message, *ringed(message, "y"), rates)
    lines_before = ringed(totals.astype(BF16), "x")
    gated = pl.pallas_call(
        finish_kernel,
        out_shape=jax.ShapeDtypeStruct((length, channels), BF16),
        in_specs=[pl.BlockSpec(memory_space=pltpu.SMEM)] + [whole()] * 9 + [far()] * 4,
        out_specs=whole(),
        scratch_shapes=[
            pltpu.VMEM((SEG, channels), F32),
            pltpu.VMEM((STATE, SEG, channels), F32),
            pltpu.VMEM((1, channels), F32),
            pltpu.VMEM((length, channels), BF16),
            pltpu.VMEM((STATE, length, LANES), F32),
            pltpu.VMEM((channels // LANES, length, LANES), F32),
            pltpu.VMEM((channels // LANES, length, LANES), F32),
            pltpu.VMEM((STATE, channels), F32),
            pltpu.SemaphoreType.DMA((4,)),
        ],
        compiler_params=params(16),
        name="finish",
    )(
        places,
        prefix,
        *lines_before,
        rates,
        delta,
        packed,
        y_local,
        mixed,
        before,
        enter,
        d_skip[None, :],
        z_in,
    )
    width = out_proj.shape[1]
    features = seqs * width
    send, keep = pl.pallas_call(
        outward_kernel,
        out_shape=(
            jax.ShapeDtypeStruct((length // 2, features), BF16),
            jax.ShapeDtypeStruct((length // 2, features), F32),
        ),
        in_specs=[whole(), far()],
        out_specs=[whole()] * 2,
        scratch_shapes=[
            pltpu.VMEM((channels, features), BF16),
            pltpu.SemaphoreType.DMA((seqs,)),
        ],
        compiler_params=params(50),
        name="outward",
    )(gated, columns)
    sums = keep + lax.ppermute(send, "exp", swap).astype(F32)
    sums = sums.reshape(side, length // owners, features)
    total = sums[0]
    for hop in range(1, side):
        total = total + along_z(sums[hop].astype(BF16), hop).astype(F32)
    return total


def shards(
    x_in,
    z_in,
    conv_weight,
    conv_bias,
    x_proj,
    dt_proj,
    dt_bias,
    a_log,
    d_skip,
    out_proj,
    residual,
    expert_ids,
    gate_weights,
    w_gate,
    w_up,
    w_down,
):
    owners = lax.axis_size("exp")
    tok_rows = residual.shape[0]
    capacity = max(2, tok_rows // 4)
    slots = owners * capacity
    chosen_count = expert_ids.shape[1]
    flat_ids = expert_ids.reshape(-1)
    hits = (flat_ids[:, None] == jnp.arange(owners, dtype=jnp.int32)[None, :]).astype(jnp.int32)
    before = jnp.cumsum(hits, axis=0) - hits
    ranked = jnp.sum(before * hits, axis=1)
    valid = jnp.sum(hits, axis=1)
    target = flat_ids * capacity + ranked
    placed = (
        (target[:, None] == jnp.arange(slots, dtype=jnp.int32)[None, :]) & (valid[:, None] > 0)
    ).astype(jnp.float32)
    dispatch_table = jnp.sum(placed.reshape(tok_rows, chosen_count, slots), axis=1)
    combine_table = jnp.sum(
        (placed * gate_weights.reshape(-1)[:, None]).reshape(tok_rows, chosen_count, slots), axis=1
    )
    tail, places, dispatch_table, combine_table = lax.optimization_barrier(
        (x_in[-(CONV - 1) :], device_places(), dispatch_table.astype(BF16), combine_table)
    )
    mixed = mixer(
        places,
        tail,
        x_in,
        z_in,
        conv_weight,
        conv_bias,
        x_proj,
        dt_proj,
        dt_bias,
        a_log,
        d_skip,
        out_proj,
    )
    hidden = residual.astype(jnp.float32) + mixed
    normed = (hidden * lax.rsqrt(jnp.mean(hidden * hidden, axis=-1, keepdims=True) + 1e-06)).astype(
        jnp.bfloat16
    )
    outgoing = jnp.einsum(
        "ts,td->sd", dispatch_table, normed, preferred_element_type=jnp.float32
    )
    outgoing = outgoing.astype(jnp.bfloat16).reshape(owners, capacity, -1)
    arrived = lax.all_to_all(outgoing, "exp", split_axis=0, concat_axis=0, tiled=True)
    summed = experts_on_grid(arrived.reshape(slots, -1), w_gate[0], w_up[0], w_down[0])
    expert_out = summed.reshape(owners, capacity, -1)
    returned_rows = lax.all_to_all(
        expert_out, "exp", split_axis=0, concat_axis=0, tiled=True
    ).reshape(slots, -1)
    combined = jnp.dot(
        combine_table, returned_rows.astype(jnp.float32), precision=lax.Precision.HIGHEST
    )
    return hidden + combined


def solution(mesh):
    placed = (
        P("seq", "exp"),
        P("seq", "exp"),
        P(None, "exp"),
        P("exp"),
        P("exp", None),
        P(None, "exp"),
        P("exp"),
        P("exp", None),
        P("exp"),
        P("exp", "seq"),
        P(("seq", "exp"), None),
        P(("seq", "exp"), None),
        P(("seq", "exp"), None),
        P("exp", None, "seq"),
        P("exp", None, "seq"),
        P("exp", "seq", None),
    )
    return jax.shard_map(
        shards, mesh=mesh, in_specs=placed, out_specs=P(("seq", "exp"), None), check_vma=False
    )
```
